32 devices in a mesh: rep: 16 (over z, y, x), shard: 2 (over core).
Axes of the slice: x: 2, y: 2, z: 4, core: 2. Of those that a mesh axis runs over, the one named last changes fastest.
Arguments:
- tokens: bfloat16 [16384, 1024], P(('rep', 'shard')), may hold values from -6 to 6
- cotangent: bfloat16 [16384, 1024], P(('rep', 'shard')), may hold values from -6 to 6
- doc_blocks: int32 [16, 8], P('rep'), may hold values from 0 to 1, as said below
- gain_in: bfloat16 [1024], P('shard'), may hold values from 0.5 to 1.5
- w_query: bfloat16 [1024, 512], P('shard'), may hold values from -0.1875 to 0.1875
- w_kv: bfloat16 [1024, 256], P('shard'), may hold values from -0.1875 to 0.1875
- w_attn_out: bfloat16 [512, 1024], P('shard'), may hold values from -0.25 to 0.25
- gain_attn: bfloat16 [1024], P('shard'), may hold values from 0.5 to 1.5
- w_ssm_in: bfloat16 [1024, 3072], P('shard'), may hold values from -0.1875 to 0.1875
- w_ssm_aux: bfloat16 [1024, 280], P('shard'), may hold values from -0.1875 to 0.1875
- dt_bias: float32 [24], replicated, may hold values from -9 to -2.3
- decay_log: float32 [24], replicated, may hold values from 0 to 2.77
- w_ssm_out: bfloat16 [1536, 1024], P('shard'), may hold values from -0.15625 to 0.15625
- gain_ssm: bfloat16 [1024], P('shard'), may hold values from 0.5 to 1.5
- gain_ff: bfloat16 [1024], P('shard'), may hold values from 0.5 to 1.5
- w_gate: bfloat16 [1024, 2048], P('shard'), may hold values from -0.1875 to 0.1875
- w_up: bfloat16 [1024, 2048], P('shard'), may hold values from -0.1875 to 0.1875
- w_down: bfloat16 [2048, 1024], P('shard'), may hold values from -0.125 to 0.125
Outputs:
- output: bfloat16 [16384, 1024], P(('rep', 'shard'))
- grad_tokens: float32 [16384, 1024], P(('rep', 'shard'))
- grad_gain_in: float32 [1024], P('shard')
- grad_w_query: float32 [1024, 512], P('shard')
- grad_w_kv: float32 [1024, 256], P('shard')
- grad_w_attn_out: float32 [512, 1024], P('shard')
- grad_gain_attn: float32 [1024], P('shard')
- grad_w_ssm_in: float32 [1024, 3072], P('shard')
- grad_w_ssm_aux: float32 [1024, 280], P('shard')
- grad_dt_bias: float32 [24], replicated
- grad_decay_log: float32 [24], replicated
- grad_w_ssm_out: float32 [1536, 1024], P('shard')
- grad_gain_ssm: float32 [1024], P('shard')
- grad_gain_ff: float32 [1024], P('shard')
- grad_w_gate: float32 [1024, 2048], P('shard')
- grad_w_up: float32 [1024, 2048], P('shard')
- grad_w_down: float32 [2048, 1024], P('shard')
The draws below stay inside these ranges and needn't reach their ends.
Inputs may be any that keep to these rules, and one draw needn't show every extreme that they name: `doc_blocks`: each group holds two documents: a row is 0 on the blocks before one cut block and 1 from the cut block on. The cut block lies at 1 to 2 or at 6 to 7, so that one document runs across the middle of the group.
All inputs are finite; a program needn't handle non-finite values.
Results may differ from the reference program's by a relative error of at most 0.015.
The reference program's roundings to bfloat16 on the way count: a program that leaves them out, or rounds other values in their place, can miss the bound.
Values may be sent and summed in bfloat16 or wider, within the bound.
No kernel may reach another device: no remote copies, remote signals or barrier semaphores. Data moves between devices by JAX's collectives and lax.ppermute only.
A program may use at most 256 MiB of HBM per device.

```python
import jax
import jax.numpy as jnp
from jax import lax

D = 1024
HD = 64
QH = 8
KVH = 2
SH = 24
SP = 64
STATE = 128
FF = 2048
WIN = 1024
BLOCK = 128
INNER = 1536
GB = 8
TOKENS = 16384
N_REP = 16


def draw_doc_blocks(key, part):
    key = jax.random.fold_in(key, 7)
    quarter = GB // 4
    places = jnp.arange(GB, dtype=jnp.int32)
    picks = jax.random.randint(key, (N_REP,), 0, 2 * quarter, dtype=jnp.int32)
    cuts = jnp.where(picks < quarter, picks + 1, GB - 2 * quarter + picks).astype(jnp.int32)
    return (places[None, :] >= cuts[:, None]).astype(jnp.int32)


def steps_of(rng, shape, split, least, high):
    level = 1.0
    for position, blocks in split:
        heights = jax.random.uniform(jax.random.fold_in(jax.random.fold_in(rng, 6), position), (blocks,), jnp.float32, least / len(split), high / len(split))
        level = level * jnp.repeat(jnp.exp(heights), shape[position] // blocks).reshape((-1,) + (1,) * (len(shape) - 1 - position))
    return level


def bell_draw(own_key, extent, width, most, split=(), held_as=jnp.bfloat16):
    array = width * jax.random.normal(own_key, extent, jnp.float32)
    if split:
        array = array * steps_of(own_key, extent, split, -0.22, 0.18)
    return jnp.clip(array, -most, most).astype(held_as)


def setup_inputs(seed: int = 0) -> dict:
    key_list = jax.random.split(jax.random.key(seed), 19)
    return {
        "tokens": bell_draw(key_list[0], (TOKENS, D), 1.0, 6.0, ((0, 32),)),
        "cotangent": bell_draw(key_list[1], (TOKENS, D), 1.0, 6.0, ((0, 32),)),
        "doc_blocks": draw_doc_blocks(jax.random.fold_in(key_list[18], 71), 0),
        "gain_in": jnp.clip(1.0 + 0.1 * jax.random.normal(key_list[3], (D,), jnp.float32), 0.5, 1.5).astype(jnp.bfloat16),
        "w_query": bell_draw(key_list[4], (D, QH * HD), D ** -0.5, 0.1875, ((0, 2),)),
        "w_kv": bell_draw(key_list[5], (D, 2 * KVH * HD), D ** -0.5, 0.1875, ((0, 2),)),
        "w_attn_out": bell_draw(key_list[6], (QH * HD, D), (QH * HD) ** -0.5, 0.25, ((0, 2),)),
        "gain_attn": jnp.clip(1.0 + 0.1 * jax.random.normal(key_list[7], (D,), jnp.float32), 0.5, 1.5).astype(jnp.bfloat16),
        "w_ssm_in": bell_draw(key_list[8], (D, 2 * INNER), D ** -0.5, 0.1875, ((0, 2),)),
        "w_ssm_aux": bell_draw(key_list[9], (D, 2 * STATE + SH), D ** -0.5, 0.1875, ((0, 2),)),
        "dt_bias": jnp.clip(jax.random.uniform(key_list[10], (SH,), jnp.float32, -9.0, -2.3), -9.0, -2.3),
        "decay_log": jnp.clip(jax.random.uniform(key_list[11], (SH,), jnp.float32, 0.0, 2.77), 0.0, 2.77),
        "w_ssm_out": bell_draw(key_list[12], (INNER, D), INNER ** -0.5, 0.15625, ((0, 2),)),
        "gain_ssm": jnp.clip(1.0 + 0.1 * jax.random.normal(key_list[13], (D,), jnp.float32), 0.5, 1.5).astype(jnp.bfloat16),
        "gain_ff": jnp.clip(1.0 + 0.1 * jax.random.normal(key_list[14], (D,), jnp.float32), 0.5, 1.5).astype(jnp.bfloat16),
        "w_gate": bell_draw(key_list[15], (D, FF), D ** -0.5, 0.1875, ((0, 2),)),
        "w_up": bell_draw(key_list[16], (D, FF), D ** -0.5, 0.1875, ((0, 2),)),
        "w_down": bell_draw(key_list[17], (FF, D), FF ** -0.5, 0.125, ((0, 2),)),
    }


HIGHEST = lax.Precision.HIGHEST
EPSILON = 1e-05
NEGATIVE = -1e+30

@jax.custom_vjp
def low(v):
    return lax.optimization_barrier(v.astype(jnp.bfloat16)).astype(jnp.float32)

@jax.custom_vjp
def low_back(v):
    return v

def low_keep(v):
    return (low(v), None)

def low_pass(kept, grad):
    return (grad,)

def back_keep(v):
    return (v, None)

def back_low(kept, grad):
    return (low(grad),)
low.defvjp(low_keep, low_pass)
low_back.defvjp(back_keep, back_low)

def product(left, right):
    return jnp.dot(left, right, precision=HIGHEST, preferred_element_type=jnp.float32)

def rms_norm(values, gain):
    return values * lax.rsqrt(lax.optimization_barrier(jnp.mean(values * values, axis=-1, keepdims=True)) + EPSILON) * gain

def ssm_inputs(mixed_in, aux_out, dt_bias, decay_log):
    row_count = mixed_in.shape[0]
    step_size = jax.nn.softplus(aux_out[:, 2 * STATE:] + dt_bias)
    log_decay = -step_size * jnp.exp(decay_log)
    scaled = mixed_in[:, :INNER].reshape(row_count, SH, SP) * step_size[:, :, None]
    return (scaled, aux_out[:, :STATE], aux_out[:, STATE:2 * STATE], log_decay)

def block_step(state_now, pieces):
    scaled, b_in, c_out, log_decay, reset_flag = pieces
    state_now = jnp.where(reset_flag, 0.0, state_now)
    cumulated = jnp.cumsum(log_decay, axis=0)
    places = jnp.arange(BLOCK, dtype=jnp.int32)
    lower_mask = (places[:, None] >= places[None, :])[:, :, None]
    spread = jnp.where(lower_mask, cumulated[:, None, :] - cumulated[None, :, :], 0.0)
    weight = jnp.where(lower_mask, jnp.exp(spread), 0.0) * product(c_out, b_in.T)[:, :, None]
    inner_part = jnp.einsum('tsh,shp->thp', weight, scaled, precision=HIGHEST)
    outer_part = jnp.exp(cumulated)[:, :, None] * jnp.einsum('tn,hpn->thp', c_out, state_now, precision=HIGHEST)
    tail_decay = jnp.exp(cumulated[-1:] - cumulated)
    fresh_state = jnp.einsum('sh,shp,sn->hpn', tail_decay, scaled, b_in, precision=HIGHEST)
    return (jnp.exp(cumulated[-1])[:, None, None] * state_now + fresh_state, inner_part + outer_part)

def scan_blocks(scaled, b_in, c_out, log_decay, state_in, block_docs, prior_doc):
    count = block_docs.shape[0]
    earlier = jnp.concatenate([prior_doc, block_docs[:-1]])
    resets = block_docs != earlier
    state_out, outputs = lax.scan(jax.checkpoint(block_step), state_in, (scaled.reshape(count, BLOCK, SH, SP), b_in.reshape(count, BLOCK, STATE), c_out.reshape(count, BLOCK, STATE), log_decay.reshape(count, BLOCK, SH), resets))
    return (outputs.reshape(count * BLOCK, SH, SP), state_out)

def attend(queries, keys, values, token_docs):
    count = queries.shape[0]
    block_rows = min(512, count)
    grouped = queries.reshape(count, KVH, QH // KVH, HD)
    pad_keys = jnp.concatenate([jnp.zeros((WIN, KVH * HD), jnp.float32), keys]).reshape(WIN + count, KVH, HD)
    pad_values = jnp.concatenate([jnp.zeros((WIN, KVH * HD), jnp.float32), values]).reshape(WIN + count, KVH, HD)
    pad_docs = jnp.concatenate([jnp.full((WIN,), -1, jnp.int32), token_docs.astype(jnp.int32)])

    def one_block(row_start):
        q_rows = lax.dynamic_slice_in_dim(grouped, row_start, block_rows, 0)
        k_rows = lax.dynamic_slice_in_dim(pad_keys, row_start, WIN + block_rows, 0)
        v_rows = lax.dynamic_slice_in_dim(pad_values, row_start, WIN + block_rows, 0)
        q_docs = lax.dynamic_slice_in_dim(token_docs.astype(jnp.int32), row_start, block_rows, 0)
        k_docs = lax.dynamic_slice_in_dim(pad_docs, row_start, WIN + block_rows, 0)
        q_place = row_start + jnp.arange(block_rows, dtype=jnp.int32)
        k_place = row_start - WIN + jnp.arange(WIN + block_rows, dtype=jnp.int32)
        allowed = (q_docs[:, None] == k_docs[None, :]) & (k_place[None, :] <= q_place[:, None]) & (k_place[None, :] > q_place[:, None] - WIN)
        raw = jnp.einsum('ikgd,jkd->kgij', q_rows, k_rows, precision=HIGHEST)
        scores = jnp.where(allowed, low_back(raw * HD ** (-0.5)), NEGATIVE)
        weights = low(jax.nn.softmax(scores, axis=-1))
        return jnp.einsum('kgij,jkd->ikgd', weights, v_rows, precision=HIGHEST).reshape(block_rows, QH * HD)
    starts = jnp.arange(count // block_rows, dtype=jnp.int32) * block_rows
    return lax.map(jax.checkpoint(one_block), starts).reshape(count, QH * HD)

def layer(hidden, token_docs, params):
    gain_in, w_query, w_kv, w_attn_out, gain_attn, w_ssm_in, w_ssm_aux, dt_bias, decay_log, w_ssm_out, gain_ssm, gain_ff, w_gate, w_up, w_down = params
    row_count = hidden.shape[0]
    normed = low(rms_norm(hidden, gain_in))
    queries = low(low_back(product(normed, w_query)))
    key_vals = low(low_back(product(normed, w_kv)))
    attended = low(low_back(attend(queries, key_vals[:, :KVH * HD], key_vals[:, KVH * HD:], token_docs)))
    attn_branch = low_back(product(attended, w_attn_out))
    mixed_in = low_back(product(normed, w_ssm_in))
    aux_out = low_back(product(normed, w_ssm_aux))
    scaled, b_in, c_out, log_decay = ssm_inputs(mixed_in, aux_out, dt_bias, decay_log)
    block_docs = token_docs[::BLOCK]
    ssm_out, state_last = scan_blocks(scaled, b_in, c_out, log_decay, jnp.zeros((SH, SP, STATE), jnp.float32), block_docs, block_docs[:1])
    gated = low(ssm_out.reshape(row_count, INNER) * jax.nn.silu(mixed_in[:, INNER:]))
    ssm_branch = low_back(product(gated, w_ssm_out))
    middle = hidden + 0.5 * (rms_norm(attn_branch, gain_attn) + rms_norm(ssm_branch, gain_ssm))
    normed_ff = low(rms_norm(middle, gain_ff))
    gate_val = low_back(product(normed_ff, w_gate))
    up_val = low_back(product(normed_ff, w_up))
    activated = low(jax.nn.silu(gate_val) * up_val)
    return middle + low_back(product(activated, w_down))

def reference(tokens, cotangent, doc_blocks, gain_in, w_query, w_kv, w_attn_out, gain_attn, w_ssm_in, w_ssm_aux, dt_bias, decay_log, w_ssm_out, gain_ssm, gain_ff, w_gate, w_up, w_down):
    params = tuple((item.astype(jnp.float32) for item in (gain_in, w_query, w_kv, w_attn_out, gain_attn, w_ssm_in, w_ssm_aux, dt_bias, decay_log, w_ssm_out, gain_ssm, gain_ff, w_gate, w_up, w_down)))
    groups = doc_blocks.shape[0]
    span = tokens.shape[0] // groups
    inputs = tokens.astype(jnp.float32).reshape(groups, span, D)
    cotangents = cotangent.astype(jnp.float32).reshape(groups, span, D)
    token_docs = jnp.repeat(doc_blocks.astype(jnp.int32), BLOCK, axis=1)

    def one_group(totals, pieces):
        hidden, group_cot, group_docs = pieces
        result, back_fn = jax.vjp(lambda inner_hidden, inner_params: layer(inner_hidden, group_docs, inner_params), hidden, params)
        grad_hidden, grad_params = back_fn(group_cot)
        totals = jax.tree.map(jnp.add, totals, grad_params)
        return (totals, (result.astype(jnp.bfloat16), grad_hidden))
    zeros = jax.tree.map(jnp.zeros_like, params)
    totals, (results, grads) = lax.scan(one_group, zeros, (inputs, cotangents, token_docs))
    return (results.reshape(tokens.shape), grads.reshape(tokens.shape), totals[0], totals[1], totals[2], totals[3], totals[4], totals[5], totals[6], totals[7], totals[8], totals[9], totals[10], totals[11], totals[12], totals[13], totals[14])
```

```python
import functools

import jax
import jax.numpy as jnp
from jax import lax
from jax.experimental import pallas as pl
from jax.experimental.pallas import tpu as pltpu
from jax.sharding import PartitionSpec as P

HD = 64
QH = 8
KVH = 2
SH = 24
SP = 64
STATE = 128
BLOCK = 128
INNER = 1536
LANES = 128
KV_AT = QH * HD
AUX_AT = KV_AT + 2 * KVH * HD
EPSILON = 1e-05
NEGATIVE = -1e30
BF = jnp.bfloat16
F32 = jnp.float32
SWAP = [(0, 1), (1, 0)]
VMEM_LIMIT = 56 * 1024 * 1024


def dot(left, right, over=((1,), (0,))):
    return lax.dot_general(left, right, (over, ((), ())), preferred_element_type=F32)


def split2(value):
    high = value.astype(BF)
    return high, (value - high.astype(F32)).astype(BF)


def split3(value):
    high = value.astype(BF)
    rest = value - high.astype(F32)
    middle = rest.astype(BF)
    return high, middle, (rest - middle.astype(F32)).astype(BF)


def dot3(left, right, over=((1,), (0,))):
    left_high, left_low = split2(left)
    right_high, right_low = split2(right)
    return dot(left_high, right_high, over) + (
        dot(left_high, right_low, over) + dot(left_low, right_high, over)
    )


def spread(value, ones):
    high, middle, low = split3(value)
    return dot(high, ones) + (dot(middle, ones) + dot(low, ones))


def gather_heads(value, ones):
    high, low = split2(value)
    return dot(high, ones, ((1,), (1,))) + dot(low, ones, ((1,), (1,)))


def head_ones():
    head = lax.broadcasted_iota(jnp.int32, (LANES, INNER), 0)
    column = lax.broadcasted_iota(jnp.int32, (LANES, INNER), 1)
    return ((column >= head * SP) & (column < (head + 1) * SP)).astype(BF)


def lower_ones():
    rows = lax.broadcasted_iota(jnp.int32, (BLOCK, BLOCK), 0)
    columns = lax.broadcasted_iota(jnp.int32, (BLOCK, BLOCK), 1)
    return rows >= columns


def cumulate(value, lower, over):
    high, middle, low = split3(value)
    return dot(lower, high, over) + (dot(lower, middle, over) + dot(lower, low, over))


def decays(aux, dt_bias, rate):
    raw = aux[:, 2 * STATE :] + dt_bias
    step = jnp.maximum(raw, 0.0) + jnp.log1p(jnp.exp(-jnp.abs(raw)))
    log_decay = -step * rate
    cumulated = cumulate(log_decay, lower_ones().astype(BF), ((1,), (0,)))
    return raw, step, log_decay, cumulated


def state_kernel(resets, mixed, aux, dt_bias, decay_log, state_out, state):
    number = pl.program_id(0)

    @pl.when((number == 0) | (resets[number] != 0))
    def _():
        state[...] = jnp.zeros_like(state)

    ones = head_ones()
    aux_now = aux[...]
    _, step, _, cumulated = decays(aux_now, dt_bias[...], jnp.exp(decay_log[...]))
    last = cumulated[BLOCK - 1 :, :]
    tail = spread(step * jnp.exp(last - cumulated), ones)
    carried = spread(jnp.exp(jnp.broadcast_to(last, (8, LANES))), ones)[:1]
    fresh = dot3(aux_now[:, :STATE], mixed[...] * tail, ((0,), (0,)))
    state[...] = carried * state[...] + fresh
    state_out[...] = state[...]


def forward_kernel(
    resets, mixed, gate, aux, dt_bias, decay_log, state_in, ssm_out, gated, states, state
):
    number = pl.program_id(0)

    @pl.when(number == 0)
    def _():
        state[...] = state_in[...]

    @pl.when(resets[number] != 0)
    def _():
        state[...] = jnp.zeros_like(state)

    ones = head_ones()
    aux_now = aux[...]
    b_in = aux_now[:, :STATE]
    c_out = aux_now[:, STATE : 2 * STATE]
    _, step, _, cumulated = decays(aux_now, dt_bias[...], jnp.exp(decay_log[...]))
    last = cumulated[BLOCK - 1 :, :]
    scaled = mixed[...] * spread(step, ones)
    tail = spread(jnp.exp(last - cumulated), ones)
    grown = spread(jnp.exp(cumulated), ones)
    before = state[...]
    states[...] = before[None]
    state[...] = grown[BLOCK - 1 :, :] * before + dot3(b_in, scaled * tail, ((0,), (0,)))
    outer = grown * dot3(c_out, before)
    both = dot3(c_out, b_in, ((1,), (1,)))
    lower = lower_ones()
    flipped = cumulated.T
    first_half = lax.broadcasted_iota(jnp.int32, (BLOCK, LANES), 1) < SP
    scaled_high, scaled_low = split2(scaled)
    zero = jnp.zeros((BLOCK, LANES), BF)
    for pair in range(SH // 2):
        weights = []
        for head in (2 * pair, 2 * pair + 1):
            spread_now = cumulated[:, head : head + 1] - flipped[head : head + 1, :]
            weights.append(jnp.exp(jnp.where(lower, spread_now, NEGATIVE)) * both)
        weight_high, weight_low = split2(jnp.concatenate(weights, axis=1))
        columns = slice(pair * LANES, (pair + 1) * LANES)
        high = scaled_high[:, columns]
        low = scaled_low[:, columns]
        high = jnp.concatenate([jnp.where(first_half, high, zero), jnp.where(first_half, zero, high)])
        low = jnp.concatenate([jnp.where(first_half, low, zero), jnp.where(first_half, zero, low)])
        inner = dot(weight_high, high) + (dot(weight_high, low) + dot(weight_low, high))
        total = inner + outer[:, columns]
        ssm_out[:, columns] = total
        gate_now = gate[:, columns]
        gated[:, columns] = (total * (gate_now / (1.0 + jnp.exp(-gate_now)))).astype(BF)


def silu_of(gate):
    chance = 1.0 / (1.0 + jnp.exp(-gate))
    return gate * chance, chance


def state_back_kernel(
    resets, d_gated, gate, aux, ssm_out, dt_bias, decay_log, d_state_out, d_gate, d_state
):
    number = pl.num_programs(0) - 1 - pl.program_id(0)

    @pl.when(pl.program_id(0) == 0)
    def _():
        d_state[...] = jnp.zeros_like(d_state)

    ones = head_ones()
    aux_now = aux[...]
    _, _, _, cumulated = decays(aux_now, dt_bias[...], jnp.exp(decay_log[...]))
    grown = spread(jnp.exp(cumulated), ones)
    gate_silu, chance = silu_of(gate[...])
    d_gated_now = d_gated[...]
    d_gate[...] = (d_gated_now * ssm_out[...] * (chance + gate_silu * (1.0 - chance))).astype(BF)
    d_grown = d_gated_now * gate_silu * grown
    c_out = aux_now[:, STATE : 2 * STATE]
    d_state[...] = grown[BLOCK - 1 :, :] * d_state[...] + dot3(c_out, d_grown, ((0,), (0,)))

    @pl.when(resets[number] != 0)
    def _():
        d_state[...] = jnp.zeros_like(d_state)

    d_state_out[...] = d_state[...].astype(BF)


def backward_kernel(
    resets,
    d_gated,
    mixed,
    gate,
    aux,
    ssm_out,
    states,
    dt_bias,
    decay_log,
    d_state_in,
    d_mixed,
    d_aux,
    d_heads,
    d_state,
):
    number = pl.num_programs(0) - 1 - pl.program_id(0)

    @pl.when(pl.program_id(0) == 0)
    def _():
        d_state[...] = d_state_in[...].astype(F32)
        d_heads[...] = jnp.zeros_like(d_heads)

    ones = head_ones()
    lower = lower_ones()
    aux_now = aux[...]
    b_in = aux_now[:, :STATE]
    c_out = aux_now[:, STATE : 2 * STATE]
    rate = jnp.exp(decay_log[...])
    raw, step, log_decay, cumulated = decays(aux_now, dt_bias[...], rate)
    last = cumulated[BLOCK - 1 :, :]
    step_wide = spread(step, ones)
    mixed_now = mixed[...]
    scaled = mixed_now * step_wide
    tail = spread(jnp.exp(last - cumulated), ones)
    grown = spread(jnp.exp(cumulated), ones)
    gate_now = gate[...]
    gate_silu, _ = silu_of(gate_now)
    d_gated_now = d_gated[...]
    ssm_now = ssm_out[...]
    d_out = d_gated_now * gate_silu
    before = states[0]
    d_after = d_state[...]
    d_grown = d_out * grown
    d_c = dot3(d_grown, before, ((1,), (1,)))
    d_before = grown[BLOCK - 1 :, :] * d_after + dot3(c_out, d_grown, ((0,), (0,)))
    tailed = scaled * tail
    d_b = dot3(tailed, d_after, ((1,), (1,)))
    d_tailed = dot3(b_in, d_after)
    ends = jnp.sum(tailed * d_tailed, axis=0, keepdims=True) + grown[BLOCK - 1 :, :] * jnp.sum(
        d_after * before, axis=0, keepdims=True
    )
    d_last = gather_heads(jnp.broadcast_to(ends, (8, INNER)), ones)[:1]
    both = dot3(c_out, b_in, ((1,), (1,)))
    flipped = cumulated.T
    first_half = lax.broadcasted_iota(jnp.int32, (BLOCK, LANES), 1) < SP
    scaled_high, scaled_low = split2(scaled)
    d_high, d_low = split2(d_out)
    zero = jnp.zeros((BLOCK, LANES), BF)
    d_both = jnp.zeros((BLOCK, BLOCK), F32)
    parts = []
    for pair in range(SH // 2):
        columns = slice(pair * LANES, (pair + 1) * LANES)
        falls = []
        for head in (2 * pair, 2 * pair + 1):
            spread_now = cumulated[:, head : head + 1] - flipped[head : head + 1, :]
            falls.append(jnp.exp(jnp.where(lower, spread_now, NEGATIVE)))
        weight_high, weight_low = split2(jnp.concatenate([falls[0] * both, falls[1] * both]))
        high = d_high[:, columns]
        low = d_low[:, columns]
        high = jnp.concatenate([jnp.where(first_half, high, zero), jnp.where(first_half, zero, high)])
        low = jnp.concatenate([jnp.where(first_half, low, zero), jnp.where(first_half, zero, low)])
        flat = ((1,), (1,))
        d_weight = dot(high, scaled_high[:, columns], flat) + (
            dot(high, scaled_low[:, columns], flat) + dot(low, scaled_high[:, columns], flat)
        )
        d_both = d_both + falls[0] * d_weight[:BLOCK] + falls[1] * d_weight[BLOCK:]
        down = ((0,), (0,))
        parts.append(
            dot(weight_high, high, down) + (dot(weight_high, low, down) + dot(weight_low, high, down))
        )
    d_scaled = jnp.concatenate(parts, axis=1) + tail * d_tailed
    d_mixed[...] = (d_scaled * step_wide).astype(BF)
    d_step = gather_heads(d_scaled * mixed_now, ones)
    d_cumulated = gather_heads(d_out * ssm_now, ones) - step * d_step
    d_decay = cumulate(d_cumulated, lower.astype(BF), ((0,), (0,))) + d_last
    d_raw = (d_step - d_decay * rate) * (1.0 / (1.0 + jnp.exp(-raw)))
    real = lax.broadcasted_iota(jnp.int32, (BLOCK, LANES), 1) < SH
    d_raw = jnp.where(real, d_raw, 0.0)
    d_c = d_c + dot3(d_both, b_in)
    d_b = d_b + dot3(d_both, c_out, ((0,), (0,)))
    d_aux[...] = jnp.concatenate([d_b, d_c, d_raw], axis=1).astype(BF)
    d_heads[...] += jnp.concatenate(
        [
            jnp.sum(d_raw, axis=0, keepdims=True),
            jnp.sum(jnp.where(real, d_decay * log_decay, 0.0), axis=0, keepdims=True),
            jnp.zeros((6, LANES), F32),
        ]
    )
    d_state[...] = d_before

    @pl.when(resets[number] != 0)
    def _():
        d_state[...] = jnp.zeros_like(d_state)


def scalars():
    return pl.BlockSpec(memory_space=pltpu.SMEM)


def whole(shape):
    return pl.BlockSpec(shape, lambda number: (0,) * len(shape))


def params_of():
    return pltpu.CompilerParams(
        dimension_semantics=("arbitrary",), vmem_limit_bytes=VMEM_LIMIT
    )


def run_state(resets, mixed, aux, dt_bias, decay_log):
    count = mixed.shape[0] // BLOCK
    return pl.pallas_call(
        state_kernel,
        grid=(count,),
        in_specs=[
            scalars(),
            pl.BlockSpec((BLOCK, INNER), lambda number: (number, 0)),
            pl.BlockSpec((BLOCK, 3 * LANES), lambda number: (number, 0)),
            whole((1, LANES)),
            whole((1, LANES)),
        ],
        out_specs=whole((STATE, INNER)),
        out_shape=jax.ShapeDtypeStruct((STATE, INNER), F32),
        scratch_shapes=[pltpu.VMEM((STATE, INNER), F32)],
        compiler_params=params_of(),
        cost_estimate=pl.CostEstimate(flops=count * 400_000_000, bytes_accessed=6_000_000, transcendentals=0),
        name="ssm_state",
    )(resets, mixed, aux, dt_bias, decay_log)


def run_forward(resets, mixed, aux, dt_bias, decay_log, state_in):
    rows = mixed.shape[0]
    count = rows // BLOCK
    return pl.pallas_call(
        forward_kernel,
        grid=(count,),
        in_specs=[
            scalars(),
            pl.BlockSpec((BLOCK, INNER), lambda number: (number, 0)),
            pl.BlockSpec((BLOCK, INNER), lambda number: (number, 1)),
            pl.BlockSpec((BLOCK, 3 * LANES), lambda number: (number, 0)),
            whole((1, LANES)),
            whole((1, LANES)),
            whole((STATE, INNER)),
        ],
        out_specs=[
            pl.BlockSpec((BLOCK, INNER), lambda number: (number, 0)),
            pl.BlockSpec((BLOCK, INNER), lambda number: (number, 0)),
            pl.BlockSpec((1, STATE, INNER), lambda number: (number, 0, 0)),
        ],
        out_shape=[
            jax.ShapeDtypeStruct((rows, INNER), F32),
            jax.ShapeDtypeStruct((rows, INNER), BF),
            jax.ShapeDtypeStruct((count, STATE, INNER), F32),
        ],
        scratch_shapes=[pltpu.VMEM((STATE, INNER), F32)],
        compiler_params=params_of(),
        cost_estimate=pl.CostEstimate(flops=count * 3_000_000_000, bytes_accessed=20_000_000, transcendentals=0),
        name="ssm_forward",
    )(resets, mixed, mixed, aux, dt_bias, decay_log, state_in)


def run_state_back(resets, d_gated, mixed, aux, ssm_out, dt_bias, decay_log):
    count = mixed.shape[0] // BLOCK
    turned = lambda number: (count - 1 - number, 0)
    return pl.pallas_call(
        state_back_kernel,
        grid=(count,),
        in_specs=[
            scalars(),
            pl.BlockSpec((BLOCK, INNER), turned),
            pl.BlockSpec((BLOCK, INNER), lambda number: (count - 1 - number, 1)),
            pl.BlockSpec((BLOCK, 3 * LANES), turned),
            pl.BlockSpec((BLOCK, INNER), turned),
            whole((1, LANES)),
            whole((1, LANES)),
        ],
        out_specs=[whole((STATE, INNER)), pl.BlockSpec((BLOCK, INNER), turned)],
        out_shape=[
            jax.ShapeDtypeStruct((STATE, INNER), BF),
            jax.ShapeDtypeStruct((mixed.shape[0], INNER), BF),
        ],
        scratch_shapes=[pltpu.VMEM((STATE, INNER), F32)],
        compiler_params=params_of(),
        cost_estimate=pl.CostEstimate(flops=count * 400_000_000, bytes_accessed=8_000_000, transcendentals=0),
        name="ssm_state_back",
    )(resets, d_gated, mixed, aux, ssm_out, dt_bias, decay_log)


def run_backward(resets, d_gated, mixed, aux, ssm_out, states, dt_bias, decay_log, d_state_in):
    rows = mixed.shape[0]
    count = rows // BLOCK
    turned = lambda number: (count - 1 - number, 0)
    return pl.pallas_call(
        backward_kernel,
        grid=(count,),
        in_specs=[
            scalars(),
            pl.BlockSpec((BLOCK, INNER), turned),
            pl.BlockSpec((BLOCK, INNER), turned),
            pl.BlockSpec((BLOCK, INNER), lambda number: (count - 1 - number, 1)),
            pl.BlockSpec((BLOCK, 3 * LANES), turned),
            pl.BlockSpec((BLOCK, INNER), turned),
            pl.BlockSpec((1, STATE, INNER), lambda number: (count - 1 - number, 0, 0)),
            whole((1, LANES)),
            whole((1, LANES)),
            whole((STATE, INNER)),
        ],
        out_specs=[
            pl.BlockSpec((BLOCK, INNER), turned),
            pl.BlockSpec((BLOCK, 3 * LANES), turned),
            whole((8, LANES)),
        ],
        out_shape=[
            jax.ShapeDtypeStruct((rows, INNER), BF),
            jax.ShapeDtypeStruct((rows, 3 * LANES), BF),
            jax.ShapeDtypeStruct((8, LANES), F32),
        ],
        scratch_shapes=[pltpu.VMEM((STATE, INNER), F32)],
        compiler_params=params_of(),
        cost_estimate=pl.CostEstimate(flops=count * 6_000_000_000, bytes_accessed=24_000_000, transcendentals=0),
        name="ssm_backward",
    )(resets, d_gated, mixed, mixed, aux, ssm_out, states, dt_bias, decay_log, d_state_in)


def head_rows(ref, start, group, width):
    return jnp.concatenate(
        [
            ref[start : start + BLOCK, (group * width + head) * HD : (group * width + head + 1) * HD]
            for head in range(width)
        ]
    )


def masked_scores(q_rows, k_rows, bias_row, lower, width):
    raw = dot(q_rows, k_rows, ((1,), (1,))) + bias_row
    edge = raw.shape[1] - BLOCK
    corner = jnp.where(jnp.concatenate([lower] * width), raw[:, edge:], NEGATIVE)
    return jnp.concatenate([raw[:, :edge], corner], axis=1)


def attend_kernel(q_ref, prior_ref, here_ref, bias_ref, out_ref, total_ref):
    width = QH // KVH
    rows = q_ref.shape[0]
    halo = prior_ref.shape[0]
    lower = lower_ones()
    for group in range(KVH):
        key_columns = slice(group * HD, (group + 1) * HD)
        value_columns = slice((KVH + group) * HD, (KVH + group + 1) * HD)
        keys = jnp.concatenate([prior_ref[:, key_columns], here_ref[:, key_columns]])
        values = jnp.concatenate([prior_ref[:, value_columns], here_ref[:, value_columns]])
        for block in range(rows // BLOCK):
            start = block * BLOCK
            reach = halo + start + BLOCK
            q_rows = head_rows(q_ref, start, group, width)
            scores = masked_scores(
                q_rows, keys[:reach], bias_ref[block : block + 1, :reach], lower, width
            )
            top = jnp.max(scores, axis=1, keepdims=True)
            powers = jnp.exp(scores - top)
            total = jnp.sum(powers, axis=1, keepdims=True)
            probs = (powers * (1.0 / total)).astype(BF)
            out = dot(probs, values[:reach])
            log_total = top + jnp.log(total)
            for head in range(width):
                place = group * width + head
                some = slice(head * BLOCK, (head + 1) * BLOCK)
                out_ref[start : start + BLOCK, place * HD : (place + 1) * HD] = out[some].astype(BF)
                total_ref[start : start + BLOCK, place : place + 1] = log_total[some]


def attend_back_kernel(
    q_ref, prior_ref, here_ref, bias_ref, total_ref, d_ref, dq_ref, d_prior_ref, d_here_ref, sums
):
    width = QH // KVH
    rows = q_ref.shape[0]
    halo = prior_ref.shape[0]
    lower = lower_ones()
    sums[...] = jnp.zeros_like(sums)
    for group in range(KVH):
        key_columns = slice(group * HD, (group + 1) * HD)
        value_columns = slice((KVH + group) * HD, (KVH + group + 1) * HD)
        keys = jnp.concatenate([prior_ref[:, key_columns], here_ref[:, key_columns]])
        values = jnp.concatenate([prior_ref[:, value_columns], here_ref[:, value_columns]])
        for block in range(rows // BLOCK):
            start = block * BLOCK
            reach = halo + start + BLOCK
            q_rows = head_rows(q_ref, start, group, width)
            d_rows = head_rows(d_ref, start, group, width)
            scores = masked_scores(
                q_rows, keys[:reach], bias_ref[block : block + 1, :reach], lower, width
            )
            log_total = jnp.concatenate(
                [
                    total_ref[start : start + BLOCK, group * width + head : group * width + head + 1]
                    for head in range(width)
                ]
            )
            probs = jnp.exp(scores - log_total)
            probs_low = probs.astype(BF)
            d_probs = dot(d_rows, values[:reach], ((1,), (1,)))
            weighed = probs * d_probs
            d_scores = (weighed - probs * jnp.sum(weighed, axis=1, keepdims=True)).astype(BF)
            d_queries = dot(d_scores, keys[:reach]) * HD**-0.5
            for head in range(width):
                place = group * width + head
                some = slice(head * BLOCK, (head + 1) * BLOCK)
                dq_ref[start : start + BLOCK, place * HD : (place + 1) * HD] = d_queries[some].astype(BF)
            sums[:reach, key_columns] += dot(d_scores, q_rows, ((0,), (0,)))
            sums[:reach, value_columns] += dot(probs_low, d_rows, ((0,), (0,)))
    d_prior_ref[...] = sums[:halo].astype(BF)
    d_here_ref[...] = sums[halo:]


def run_attend(queries, prior, here, bias):
    rows = queries.shape[0]
    return pl.pallas_call(
        attend_kernel,
        out_shape=[
            jax.ShapeDtypeStruct((rows, QH * HD), BF),
            jax.ShapeDtypeStruct((rows, QH), F32),
        ],
        compiler_params=pltpu.CompilerParams(vmem_limit_bytes=VMEM_LIMIT),
        cost_estimate=pl.CostEstimate(flops=6_000_000_000, bytes_accessed=2_000_000, transcendentals=4_000_000),
        name="attend",
    )(queries, prior, here, bias)


def run_attend_back(queries, prior, here, bias, log_total, d_attended):
    rows = queries.shape[0]
    halo = prior.shape[0]
    return pl.pallas_call(
        attend_back_kernel,
        out_shape=[
            jax.ShapeDtypeStruct((rows, QH * HD), BF),
            jax.ShapeDtypeStruct((halo, 2 * KVH * HD), BF),
            jax.ShapeDtypeStruct((rows, 2 * KVH * HD), F32),
        ],
        scratch_shapes=[pltpu.VMEM((halo + rows, 2 * KVH * HD), F32)],
        compiler_params=pltpu.CompilerParams(vmem_limit_bytes=VMEM_LIMIT),
        cost_estimate=pl.CostEstimate(flops=12_000_000_000, bytes_accessed=4_000_000, transcendentals=4_000_000),
        name="attend_back",
    )(queries, prior, here, bias, log_total, d_attended)


def swap(value):
    return lax.ppermute(value, "shard", SWAP)


def natural(mine, theirs, position, axis):
    return jnp.where(
        position == 0,
        jnp.concatenate([mine, theirs], axis=axis),
        jnp.concatenate([theirs, mine], axis=axis),
    )


def half_of(value, which, axis):
    size = value.shape[axis] // 2
    return lax.dynamic_slice_in_dim(value, which * size, size, axis)


class Stream:
    def __init__(self, terms):
        self.terms = terms
        self.count = lax.axis_size("rep")
        self.pairs = self.count % 4 == 0
        self.far = self.count // 4 if self.pairs else self.count
        rep = lax.axis_index("rep")
        core = lax.axis_index("shard")
        near = rep % 4 if self.pairs else 0
        self.far_at = rep // 4 if self.pairs else rep
        fast, slow = near % 2, near // 2
        self.bits = (jnp.where(core == 0, fast, slow), jnp.where(core == 0, slow, fast))
        around = [0, 1] if self.pairs else []
        self.steps = [("scatter", phase) for phase in around]
        if self.far > 1:
            self.steps += [("scatter", 2), ("gather", 2)]
        self.steps += [("gather", phase) for phase in reversed(around)]
        self.stack = None
        self.got = None
        self.operands = []

    def pair_list(self, phase):
        flips = (1, 2) if phase == 0 else (2, 1)
        return [
            (rep * 2 + core, (rep ^ flips[core]) * 2 + core)
            for rep in range(self.count)
            for core in range(2)
        ]

    def far_list(self, shift):
        near = 4 if self.pairs else 1
        return [
            (rep * 2 + core, ((rep + shift * near) % self.count) * 2 + core)
            for rep in range(self.count)
            for core in range(2)
        ]

    def part(self, start, size):
        total = lax.dynamic_slice_in_dim(self.terms[0], start, size, 0).astype(F32)
        for term in self.terms[1:]:
            total = total + lax.dynamic_slice_in_dim(term, start, size, 0).astype(F32)
        return total.astype(BF)

    def prepare(self):
        if not self.steps:
            self.operands = []
            return
        kind, phase = self.steps[0]
        if kind == "gather":
            if self.stack is None:
                self.stack = self.part(0, self.terms[0].shape[0])
            elif self.got is not None:
                self.stack = jnp.concatenate([self.stack, *self.got])
            self.operands = [self.stack]
        elif phase < 2:
            size = self.terms[0].shape[0] // 2
            self.operands = [self.part((1 - self.bits[phase]) * size, size)]
        else:
            size = self.terms[0].shape[0] // self.far
            self.operands = [
                self.part((self.far_at + shift) % self.far * size, size) for shift in range(1, self.far)
            ]

    def go(self):
        if not self.steps:
            return
        kind, phase = self.steps.pop(0)
        if phase < 2:
            lists = [self.pair_list(phase)]
        else:
            lists = [self.far_list(shift) for shift in range(1, self.far)]
        operands = self.operands * len(lists) if kind == "gather" else self.operands
        self.got = [
            lax.ppermute(operand, ("rep", "shard"), pairs) for operand, pairs in zip(operands, lists)
        ]
        if kind == "scatter":
            parts, at = (2, self.bits[phase]) if phase < 2 else (self.far, self.far_at)
            size = self.terms[0].shape[0] // parts
            self.terms = [
                lax.dynamic_slice_in_dim(term, at * size, size, 0) for term in self.terms
            ] + self.got
            self.got = None

    def places(self):
        at = (self.far_at - jnp.arange(self.far, dtype=jnp.int32)) % self.far
        for phase in (1, 0) if self.pairs else ():
            span = self.far * (1 if phase == 1 else 2)
            own = self.bits[phase]
            at = jnp.concatenate([own * span + at, (1 - own) * span + at])
        return at.astype(jnp.int32)

    def finish(self, outputs, started=None):
        if self.stack is None:
            self.stack = self.part(0, self.terms[0].shape[0])
        stacks = [self.stack, *(self.got or [])]
        places = self.places()
        blocks = places.shape[0]
        each = blocks // len(stacks)
        size = stacks[0].shape[0] // each
        width = stacks[0].shape[1]
        if size % 16:
            flat = jnp.concatenate(stacks).reshape(blocks, size, width)
            flat = jnp.zeros_like(flat).at[places].set(flat).reshape(blocks * size, width)
            made = []
            for shape, _, pieces in outputs:
                cuts = [flat[:, begin:end].astype(F32) for _, begin, end in pieces]
                whole_width = shape.shape[-1]
                if len(shape.shape) == 3:
                    value = jnp.stack(cuts)
                    value = jnp.pad(value, ((0, 0), (0, 0), (whole_width - value.shape[-1], 0)))
                else:
                    value = jnp.concatenate(cuts, axis=1)
                made.append(value)
            if started is not None:
                made[-1] = jnp.concatenate([made[-1], started[:, made[-1].shape[1] :]], axis=1)
            return made
        in_specs = [
            pl.BlockSpec((size, width), lambda step, places: (jnp.minimum(step, each - 1), 0))
        ]
        if len(stacks) == 2:
            in_specs.append(
                pl.BlockSpec((size, width), lambda step, places: (jnp.maximum(step - each, 0), 0))
            )
        out_specs = []
        for shape, block, _ in outputs:
            if len(shape.shape) == 3:
                last = shape.shape[2] // block[0] - 1
                out_specs.append(
                    pl.BlockSpec(
                        (shape.shape[0], size, block[0]),
                        lambda step, places, last=last: (0, places[step], last),
                    )
                )
            else:
                out_specs.append(
                    pl.BlockSpec((size, block[0]), lambda step, places: (places[step], 0))
                )
        aliases = {}
        inputs = list(stacks)
        if started is not None:
            aliases = {1 + len(inputs): len(outputs) - 1}
            inputs.append(started)
            in_specs.append(pl.BlockSpec(memory_space=pl.ANY))
        return pl.pallas_call(
            functools.partial(finish_kernel, len(stacks), [pieces for _, _, pieces in outputs]),
            grid_spec=pltpu.PrefetchScalarGridSpec(
                num_scalar_prefetch=1, grid=(blocks,), in_specs=in_specs, out_specs=out_specs
            ),
            out_shape=[shape for shape, _, _ in outputs],
            input_output_aliases=aliases,
            compiler_params=params_of(),
            name="unpack",
        )(places, *inputs)


def finish_kernel(count, layout, places, *refs):
    del places
    outputs = refs[-len(layout) :]
    steps = pl.num_programs(0)

    def write(ref):
        for out, pieces in zip(outputs, layout):
            for target, begin, end in pieces:
                value = ref[:, begin:end].astype(F32)
                if len(out.shape) == 3:
                    out[target] = value
                else:
                    out[:, target : target + end - begin] = value

    if count == 1:
        write(refs[0])
        return

    @pl.when(pl.program_id(0) < steps // 2)
    def _():
        write(refs[0])

    @pl.when(pl.program_id(0) >= steps // 2)
    def _():
        write(refs[1])


def after(value, *others):
    return lax.optimization_barrier((value, *others))[0]


def columns_of(ref, which, size):
    return ref[:, pl.ds(pl.multiple_of(which * size, size), size)]


def inverse_rms(values):
    return lax.rsqrt(jnp.mean(values * values, axis=-1, keepdims=True) + EPSILON)


def norm_back(values, inverse, gain, grad):
    scaled = grad * gain
    shared = jnp.mean(scaled * values, axis=-1, keepdims=True) * (inverse * inverse)
    return (
        inverse * (scaled - values * shared),
        jnp.sum(grad * (values * inverse), axis=0, keepdims=True),
    )


def project_kernel(
    position,
    tokens,
    gains,
    small_mine,
    small_theirs,
    ssm_mine,
    ssm_theirs,
    normed,
    queries,
    key_vals,
    aux,
    mixed,
):
    here = position[0]
    half = tokens.shape[1] // 2

    def product(mine, theirs, begin=0, end=None):
        return dot(columns_of(normed, here, half), mine[:, begin:end]) + dot(
            columns_of(normed, 1 - here, half), theirs[:, begin:end]
        )

    @pl.when(pl.program_id(0) == 0)
    def _():
        hidden = tokens[...].astype(F32)
        normed[...] = (hidden * inverse_rms(hidden) * gains[0:1]).astype(BF)
        low = product(small_mine, small_theirs, 0, AUX_AT)
        queries[...] = low[:, :KV_AT].astype(BF) * jnp.asarray(HD**-0.5, BF)
        key_vals[...] = low[:, KV_AT:].astype(BF)
        aux[...] = product(small_mine, small_theirs, AUX_AT)

    mixed[...] = product(ssm_mine, ssm_theirs)


CHUNK = 512


def run_project(position, tokens, gains, small, ssm):
    rows, width = tokens.shape
    half = width // 2
    inner = ssm[0].shape[1]
    aux_width = small[0].shape[1] - AUX_AT
    fixed = lambda shape: pl.BlockSpec(shape, lambda step, place: (0,) * len(shape))
    sliding = pl.BlockSpec((half, CHUNK), lambda step, place: (0, step))
    weights = [fixed(small[0].shape)] * 2
    return pl.pallas_call(
        project_kernel,
        grid_spec=pltpu.PrefetchScalarGridSpec(
            num_scalar_prefetch=1,
            grid=(inner // CHUNK,),
            in_specs=[fixed(tokens.shape), fixed(gains.shape), *weights, sliding, sliding],
            out_specs=[
                fixed((rows, width)),
                fixed((rows, KV_AT)),
                fixed((rows, AUX_AT - KV_AT)),
                fixed((rows, aux_width)),
                pl.BlockSpec((rows, CHUNK), lambda step, place: (0, step)),
            ],
        ),
        out_shape=[
            jax.ShapeDtypeStruct((rows, width), BF),
            jax.ShapeDtypeStruct((rows, KV_AT), BF),
            jax.ShapeDtypeStruct((rows, AUX_AT - KV_AT), BF),
            jax.ShapeDtypeStruct((rows, aux_width), F32),
            jax.ShapeDtypeStruct((rows, inner), F32),
        ],
        compiler_params=params_of(),
        cost_estimate=pl.CostEstimate(flops=6_000_000_000, bytes_accessed=20_000_000, transcendentals=0),
        name="project",
    )(position, tokens, gains, *small, *ssm)


def project_back_kernel(
    position,
    tokens,
    gains,
    d_middle,
    d_query,
    d_kv,
    d_aux,
    d_mixed,
    d_gate,
    small_mine,
    small_theirs,
    ssm_mine,
    ssm_theirs,
    grad_tokens,
    grad_gain,
    d_normed,
):
    here = position[0]
    step = pl.program_id(0)
    count = pl.num_programs(0)
    half = tokens.shape[1] // 2
    flat = ((1,), (1,))

    def place(which):
        return pl.ds(pl.multiple_of(which * half, half), half)

    @pl.when(step == 0)
    def _():
        for which, small in ((here, small_mine), (1 - here, small_theirs)):
            d_normed[:, place(which)] = (
                dot(d_query[...], small[:, :KV_AT], flat)
                + dot(d_kv[...], small[:, KV_AT:AUX_AT], flat)
                + dot(d_aux[...], small[:, AUX_AT:], flat)
            )

    d_now = jnp.where(step < count // 2, d_mixed[...], d_gate[...])
    d_normed[:, place(here)] += dot(d_now, ssm_mine[...], flat)
    d_normed[:, place(1 - here)] += dot(d_now, ssm_theirs[...], flat)

    @pl.when(step == count - 1)
    def _():
        hidden = tokens[...].astype(F32)
        d_hidden, d_gain = norm_back(hidden, inverse_rms(hidden), gains[0:1], d_normed[...])
        grad_tokens[...] = d_middle[...] + d_hidden
        grad_gain[...] = jnp.broadcast_to(d_gain, grad_gain.shape)


def run_project_back(
    position, tokens, gains, d_middle, d_query, d_kv, d_aux, d_mixed, d_gate, small, ssm
):
    rows, width = tokens.shape
    half = width // 2
    count = ssm[0].shape[1] // CHUNK
    fixed = lambda array: pl.BlockSpec(array.shape, lambda step, place: (0,) * len(array.shape))
    sliding = pl.BlockSpec((half, CHUNK), lambda step, place: (0, step))
    weights = small
    return pl.pallas_call(
        project_back_kernel,
        grid_spec=pltpu.PrefetchScalarGridSpec(
            num_scalar_prefetch=1,
            grid=(count,),
            in_specs=[
                *[fixed(item) for item in (tokens, gains, d_middle, d_query, d_kv, d_aux)],
                pl.BlockSpec(
                    (rows, CHUNK), lambda step, place: (0, jnp.minimum(step, count // 2 - 1))
                ),
                pl.BlockSpec(
                    (rows, CHUNK), lambda step, place: (0, jnp.maximum(step - count // 2, 0))
                ),
                *[fixed(item) for item in weights],
                sliding,
                sliding,
            ],
            out_specs=[
                pl.BlockSpec((rows, width), lambda step, place: (0, 0)),
                pl.BlockSpec((8, width), lambda step, place: (0, 0)),
            ],
            scratch_shapes=[pltpu.VMEM((rows, width), F32)],
        ),
        out_shape=[
            jax.ShapeDtypeStruct((rows, width), F32),
            jax.ShapeDtypeStruct((8, width), F32),
        ],
        compiler_params=params_of(),
        cost_estimate=pl.CostEstimate(flops=6_000_000_000, bytes_accessed=20_000_000, transcendentals=0),
        name="project_back",
    )(position, tokens, gains, d_middle, d_query, d_kv, d_aux, d_mixed, d_gate, *weights, *ssm)


def middle_kernel(
    position,
    tokens,
    attended,
    gated,
    cotangent,
    gains,
    attn_mine,
    attn_theirs,
    ssm_mine,
    ssm_theirs,
    gate,
    up,
    down,
    output,
    d_middle,
    d_attn_branch,
    d_ssm_branch,
    d_attended,
    d_gated,
    gain_grads,
    grad_down_theirs,
    grad_down_mine,
    grad_wide_theirs,
    grad_wide_mine,
    attn_branch,
    ssm_branch,
    middle,
    normed,
    flipped,
    out_sum,
    d_normed,
):
    here = position[0]
    step = pl.program_id(0)
    count = pl.num_programs(0)
    width = tokens.shape[1]
    half = width // 2
    attn_half = attended.shape[1] // 2
    ssm_half = gated.shape[1] // 2
    flat = ((1,), (1,))

    def place(which, size):
        return pl.ds(pl.multiple_of(which * size, size), size)

    @pl.when(step == 0)
    def _():
        attn = dot(columns_of(attended, here, attn_half), attn_mine[...]) + dot(
            columns_of(attended, 1 - here, attn_half), attn_theirs[...]
        )
        attn_branch[...] = attn
        ssm = dot(columns_of(gated, here, ssm_half), ssm_mine[...]) + dot(
            columns_of(gated, 1 - here, ssm_half), ssm_theirs[...]
        )
        ssm_branch[...] = ssm
        joined = tokens[...].astype(F32) + 0.5 * (
            attn * inverse_rms(attn) * gains[1:2] + ssm * inverse_rms(ssm) * gains[2:3]
        )
        middle[...] = joined
        out_sum[...] = joined
        scaled = joined * inverse_rms(joined) * gains[3:4]
        normed[...] = scaled.astype(BF)
        flipped[...] = scaled.T.astype(BF)
        d_normed[...] = jnp.zeros_like(d_normed)

    gate_val = dot(normed[...], gate[...])
    up_val = dot(normed[...], up[...])
    gate_silu, chance = silu_of(gate_val)
    activated = (gate_silu * up_val).astype(BF)
    d_activated = dot(cotangent[...], down[...], flat)
    out_sum[...] += dot(activated, down[...])
    d_up = (d_activated * gate_silu).astype(BF)
    d_gate = (d_activated * up_val * (chance + gate_silu * (1.0 - chance))).astype(BF)
    d_normed[...] += dot(d_gate, gate[...], flat) + dot(d_up, up[...], flat)
    grad_down = dot(activated, cotangent[...], ((0,), (0,))).astype(BF)
    first = step < count // 2

    @pl.when(first)
    def _():
        grad_down_theirs[...] = grad_down

    @pl.when(jnp.logical_not(first))
    def _():
        grad_down_mine[...] = grad_down

    for which, ref in ((here, grad_wide_mine), (1 - here, grad_wide_theirs)):
        turned = flipped[place(which, half), :]
        ref[:, :CHUNK] = dot(turned, d_gate).astype(BF)
        ref[:, CHUNK:] = dot(turned, d_up).astype(BF)

    @pl.when(step == count - 1)
    def _():
        output[...] = out_sum[...].astype(BF)
        joined = middle[...]
        d_joined, d_gain_ff = norm_back(joined, inverse_rms(joined), gains[3:4], d_normed[...])
        d_joined = cotangent[...].astype(F32) + d_joined
        d_middle[...] = d_joined
        attn = attn_branch[...]
        d_attn, d_gain_attn = norm_back(attn, inverse_rms(attn), gains[1:2], 0.5 * d_joined)
        d_attn_low = d_attn.astype(BF)
        d_attn_branch[...] = d_attn_low
        ssm = ssm_branch[...]
        d_ssm, d_gain_ssm = norm_back(ssm, inverse_rms(ssm), gains[2:3], 0.5 * d_joined)
        d_ssm_low = d_ssm.astype(BF)
        d_ssm_branch[...] = d_ssm_low
        gain_grads[...] = jnp.concatenate(
            [d_gain_attn, d_gain_ssm, d_gain_ff, jnp.zeros((5, width), F32)]
        )
        for which, attn_weight, ssm_weight in (
            (here, attn_mine, ssm_mine),
            (1 - here, attn_theirs, ssm_theirs),
        ):
            d_attended[:, place(which, attn_half)] = dot(d_attn_low, attn_weight[...], flat).astype(BF)
            d_gated[:, place(which, ssm_half)] = dot(d_ssm_low, ssm_weight[...], flat)


def run_middle(position, tokens, attended, gated, cotangent, gains, attn, ssm, gate, up, down):
    rows, width = tokens.shape
    half = width // 2
    hidden = gate.shape[1]
    count = hidden // CHUNK
    fixed = lambda shape: pl.BlockSpec(shape, lambda step, place: (0,) * len(shape))

    def chunk(step, place):
        first = step < count // 2
        return jnp.where(first, 1 - place[0], place[0]) * (count // 2) + step % (count // 2)

    sliding = pl.BlockSpec((width, CHUNK), lambda step, place: (0, chunk(step, place)))
    early = lambda step, place: (jnp.minimum(step, count // 2 - 1), 0)
    late = lambda step, place: (jnp.maximum(step - count // 2, 0), 0)
    wide = pl.BlockSpec((half, 2 * CHUNK), lambda step, place: (0, chunk(step, place)))
    low = lambda shape: jax.ShapeDtypeStruct(shape, BF)
    full = lambda shape: jax.ShapeDtypeStruct(shape, F32)
    return pl.pallas_call(
        middle_kernel,
        grid_spec=pltpu.PrefetchScalarGridSpec(
            num_scalar_prefetch=1,
            grid=(count,),
            in_specs=[
                *[fixed(item.shape) for item in (tokens, attended, gated, cotangent, gains)],
                *[fixed(item.shape) for item in (*attn, *ssm)],
                *[sliding] * 2,
                pl.BlockSpec((CHUNK, width), lambda step, place: (chunk(step, place), 0)),
            ],
            out_specs=[
                *[fixed((rows, width))] * 4,
                fixed(attended.shape),
                fixed(gated.shape),
                fixed((8, width)),
                pl.BlockSpec((CHUNK, width), early),
                pl.BlockSpec((CHUNK, width), late),
                wide,
                wide,
            ],
            scratch_shapes=[
                *[pltpu.VMEM((rows, width), F32)] * 3,
                pltpu.VMEM((rows, width), BF),
                pltpu.VMEM((width, rows), BF),
                *[pltpu.VMEM((rows, width), F32)] * 2,
            ],
        ),
        out_shape=[
            low((rows, width)),
            full((rows, width)),
            low((rows, width)),
            low((rows, width)),
            low(attended.shape),
            full(gated.shape),
            full((8, width)),
            low((hidden // 2, width)),
            low((hidden // 2, width)),
            low((half, 2 * hidden)),
            low((half, 2 * hidden)),
        ],
        compiler_params=params_of(),
        cost_estimate=pl.CostEstimate(flops=30_000_000_000, bytes_accessed=40_000_000, transcendentals=0),
        name="middle",
    )(position, tokens, attended, gated, cotangent, gains, *attn, *ssm, gate, up, down)


def local(
    tokens,
    cotangent,
    doc_blocks,
    gain_in,
    w_query,
    w_kv,
    w_attn_out,
    gain_attn,
    w_ssm_in,
    w_ssm_aux,
    dt_bias,
    decay_log,
    w_ssm_out,
    gain_ssm,
    gain_ff,
    w_gate,
    w_up,
    w_down,
):
    rows, width = tokens.shape
    half = width // 2
    position = lax.axis_index("shard")
    here = position.astype(jnp.int32).reshape(1)
    blocks_here = rows // BLOCK
    docs = doc_blocks[0]
    here_docs = lax.dynamic_slice_in_dim(docs, position * blocks_here, blocks_here, 0)
    prior_docs = jnp.where(position > 0, docs[:blocks_here], -1)
    earlier = jnp.concatenate([prior_docs[-1:], here_docs[:-1]])
    resets = (here_docs != earlier).astype(jnp.int32)
    key_docs = jnp.repeat(jnp.concatenate([prior_docs, here_docs]), BLOCK)
    bias = jnp.where(here_docs[:, None] == key_docs[None, :], 0.0, NEGATIVE)
    lane_pad = LANES - SH
    dt_row = jnp.pad(dt_bias, (0, lane_pad))[None]
    decay_row = jnp.pad(decay_log, (0, lane_pad))[None]

    gains = jnp.stack([gain_in, gain_attn, gain_ssm, gain_ff])
    gains_theirs = swap(gains)
    small = jnp.concatenate([w_query, w_kv, jnp.pad(w_ssm_aux, ((0, 0), (0, lane_pad)))], axis=1)
    ssm_in = (w_ssm_in, swap(w_ssm_in))
    small = (small, swap(small))
    attn_out = (w_attn_out, swap(w_attn_out))
    ssm_back = (w_ssm_out, swap(w_ssm_out))
    gate = lax.all_gather(w_gate, "shard", axis=0, tiled=True)
    up = lax.all_gather(w_up, "shard", axis=0, tiled=True)
    down = lax.all_gather(w_down, "shard", axis=0, tiled=True)
    gains_all = jnp.pad(natural(gains, gains_theirs, position, 1).astype(F32), ((0, 4), (0, 0)))

    normed, scaled_queries, key_vals, aux, mixed = run_project(
        here, tokens, gains_all, small, ssm_in
    )
    key_prior = lax.ppermute(key_vals, "shard", [(0, 1)])
    state_end = run_state(resets, mixed, aux, dt_row, decay_row)
    state_prior = lax.ppermute(state_end, "shard", [(0, 1)])
    attended, log_total = run_attend(scaled_queries, key_prior, key_vals, bias)
    ssm_out, gated, states = run_forward(resets, mixed, aux, dt_row, decay_row, state_prior)

    (
        output,
        d_middle,
        d_attn_low,
        d_ssm_low,
        d_attended,
        d_gated,
        gain_grads,
        down_theirs,
        down_mine,
        wide_theirs,
        wide_mine,
    ) = run_middle(
        here, tokens, attended, gated, cotangent, gains_all, attn_out, ssm_back, gate, up, down
    )
    down_got = swap(down_theirs)
    wide_got = swap(wide_theirs)

    wide = Stream([wide_mine, wide_got])
    d_state_start, d_mixed_gate = run_state_back(
        resets, d_gated, mixed, aux, ssm_out, dt_row, decay_row
    )
    d_state_end = lax.ppermute(d_state_start, "shard", [(1, 0)])
    outs_rows = w_attn_out.shape[0]

    def grads_of(left, right):
        return (
            dot(half_of(left, 1 - position, 1), right, ((0,), (0,))).astype(BF),
            dot(half_of(left, position, 1), right, ((0,), (0,))).astype(BF),
        )

    def beside(*arrays):
        return jnp.concatenate(
            [
                array[start : start + outs_rows]
                for array in arrays
                for start in range(0, array.shape[0], outs_rows)
            ],
            axis=1,
        )

    outs_theirs, outs_mine = zip(
        grads_of(attended, d_attn_low), grads_of(gated, d_ssm_low), grads_of(normed, d_mixed_gate)
    )
    outs_mine = beside(*outs_mine)
    outs_got = swap(beside(*outs_theirs))
    down_sum = (down_mine.astype(F32) + down_got.astype(F32)).astype(BF)
    grad_down = lax.psum(down_sum, "rep")
    wide.prepare()
    d_mixed, d_aux, d_heads = run_backward(
        resets,
        after(d_gated, down_sum, *wide.operands),
        mixed,
        aux,
        ssm_out,
        states,
        dt_row,
        decay_row,
        d_state_end,
    )
    wide.go()
    outs = Stream([outs_mine, outs_got])
    outs.prepare()
    wide.prepare()
    d_query, d_prior, d_here = run_attend_back(
        scaled_queries,
        key_prior,
        key_vals,
        bias,
        log_total,
        after(d_attended, d_aux, *outs.operands, *wide.operands),
    )
    wide.go()
    outs.go()
    d_kv = (d_here + lax.ppermute(d_prior, "shard", [(1, 0)]).astype(F32)).astype(BF)

    d_rest = jnp.concatenate([d_query, d_kv, d_mixed, d_aux], axis=1)
    rest_theirs, rest_mine = grads_of(normed, d_rest)
    wide.prepare()
    outs.prepare()
    grad_tokens, gain_in_grads = run_project_back(
        here,
        tokens,
        gains_all,
        d_middle,
        d_query,
        d_kv,
        d_aux,
        d_mixed,
        after(d_mixed_gate, rest_theirs, *wide.operands, *outs.operands),
        small,
        ssm_in,
    )
    wide.go()
    outs.go()
    head_column = jnp.pad(d_heads[:2, :SH].reshape(2 * SH), (0, half - 2 * SH))[:, None]
    spare = AUX_AT + INNER + 2 * STATE + SH

    def with_extra(array, which):
        extra = half_of(jnp.concatenate([gain_in_grads[:1], gain_grads[:3]]), which, 1).T
        extra = jnp.concatenate([extra, head_column], axis=1).astype(BF)
        extra = jnp.pad(extra, ((0, 0), (0, lane_pad - extra.shape[1])))
        return jnp.concatenate([array[:, :spare], extra], axis=1)

    rest = Stream([with_extra(rest_mine, position), swap(with_extra(rest_theirs, 1 - position))])
    rest.prepare()
    rest.go()
    for stream in (wide, outs):
        stream.prepare()
        stream.go()
    rest.prepare()
    rest.go()
    for stream in (wide, outs):
        stream.prepare()
        stream.go()
    rest.prepare()
    rest.go()
    for stream in (wide, outs):
        stream.prepare()
        stream.go()
    for stream in (wide, outs, rest):
        while stream.steps:
            stream.prepare()
            stream.go()

    full = lambda *shape: jax.ShapeDtypeStruct(shape, F32)
    pieces = [
        [
            (column, 2 * column + offset, 2 * column + offset + CHUNK)
            for column in range(0, w_gate.shape[1], CHUNK)
        ]
        for offset in (0, CHUNK)
    ]
    grad_gate, grad_up = wide.finish(
        [
            (full(half, w_gate.shape[1]), (w_gate.shape[1],), pieces[0]),
            (full(half, w_gate.shape[1]), (w_gate.shape[1],), pieces[1]),
        ]
    )
    ssm_pieces = w_ssm_out.shape[0] // outs_rows
    gate_at = width * (1 + ssm_pieces)
    grad_attn_out, grad_ssm_out, grad_ssm_in = outs.finish(
        [
            (full(outs_rows, width), (width,), [(0, 0, width)]),
            (
                full(ssm_pieces, outs_rows, width),
                (width,),
                [(piece, width * (1 + piece), width * (2 + piece)) for piece in range(ssm_pieces)],
            ),
            (
                full(half // outs_rows, outs_rows, 2 * INNER),
                (INNER,),
                [
                    (piece, gate_at + INNER * piece, gate_at + INNER * (piece + 1))
                    for piece in range(half // outs_rows)
                ],
            ),
        ]
    )
    aux_at = AUX_AT + INNER
    grad_query, grad_kv, grad_aux, extras, grad_ssm_in = rest.finish(
        [
            (full(half, KV_AT), (KV_AT,), [(0, 0, KV_AT)]),
            (full(half, AUX_AT - KV_AT), (AUX_AT - KV_AT,), [(0, KV_AT, AUX_AT)]),
            (full(half, spare - aux_at), (spare - aux_at,), [(0, aux_at, spare)]),
            (full(half, LANES), (LANES,), [(0, aux_at + 2 * STATE, aux_at + 3 * LANES)]),
            (full(half, 2 * INNER), (INNER,), [(0, AUX_AT, aux_at)]),
        ],
        grad_ssm_in.reshape(half, 2 * INNER),
    )
    return (
        output,
        grad_tokens,
        extras[:, SH],
        grad_query,
        grad_kv,
        grad_attn_out,
        extras[:, SH + 1],
        grad_ssm_in,
        grad_aux,
        extras[:SH, SH + 4],
        extras[SH : 2 * SH, SH + 4],
        grad_ssm_out.reshape(w_ssm_out.shape),
        extras[:, SH + 2],
        extras[:, SH + 3],
        grad_gate,
        grad_up,
        grad_down.astype(F32),
    )


def solution(mesh):
    halves = P("shard", None)
    half = P("shard")
    tokens = P(("rep", "shard"), None)
    return jax.shard_map(
        local,
        mesh=mesh,
        in_specs=(
            tokens,
            tokens,
            P("rep", None),
            half,
            halves,
            halves,
            halves,
            half,
            halves,
            halves,
            P(),
            P(),
            halves,
            half,
            half,
            halves,
            halves,
            halves,
        ),
        out_specs=(
            tokens,
            tokens,
            half,
            halves,
            halves,
            halves,
            half,
            halves,
            halves,
            P(),
            P(),
            halves,
            half,
            half,
            halves,
            halves,
            halves,
        ),
        check_vma=False,
    )
```

```python
import functools

import jax
import jax.numpy as jnp
from jax import lax
from jax.experimental import pallas as pl
from jax.experimental.pallas import tpu as pltpu
from jax.sharding import PartitionSpec as P

HD = 64
QH = 8
KVH = 2
SH = 24
SP = 64
STATE = 128
BLOCK = 128
INNER = 1536
LANES = 128
KV_AT = QH * HD
X, Y, Z, ZZ = 0, 1, 2, 3
TURNED = -1
WHOLE = {"down": 2, "wide": 1, "outs": 1, "rest": 2}
LINKS = {
    "down": ((X, Z, ZZ, Y), (Y, Z, X, ZZ)),
    "wide": ((X, Y, Z, ZZ), (Y, Z, X, ZZ)),
    "outs": ((Z, Y, X, ZZ), (X, Z, Y, ZZ)),
    "rest": ((X, Y, ZZ, Z), (Y, Z, X, ZZ)),
}
PLAN = (
    "state",
    "down",
    "grads",
    "wide",
    "down",
    "outs",
    "scan",
    "wide",
    "down",
    "attend",
    "sums",
    "outs",
    "wide",
    "down",
    "rest",
    "early",
    "outs",
    "wide",
    "down",
    "rest",
    "outs",
    "wide",
    "late",
    "down",
    "rest",
    "outs",
    "wide",
    "down",
    "rest",
    "outs",
    "wide",
    "rest",
    "outs",
    "wide",
    "rest",
    "outs",
    "rest",
)
AUX_AT = KV_AT + 2 * KVH * HD
EPSILON = 1e-05
NEGATIVE = -1e30
BF = jnp.bfloat16
F32 = jnp.float32
SWAP = [(0, 1), (1, 0)]
VMEM_LIMIT = 30 * 1024 * 1024
LARGE_LIMIT = 50 * 1024 * 1024
LONG = pl.CostEstimate(flops=15_000_000_000, bytes_accessed=1_000_000, transcendentals=0)
COST = pl.CostEstimate(flops=1_000_000, bytes_accessed=1_000_000, transcendentals=0)


def dot(left, right, over=((1,), (0,))):
    return lax.dot_general(left, right, (over, ((), ())), preferred_element_type=F32)


def split2(value):
    high = value.astype(BF)
    return high, (value - high.astype(F32)).astype(BF)


def split3(value):
    high = value.astype(BF)
    rest = value - high.astype(F32)
    middle = rest.astype(BF)
    return high, middle, (rest - middle.astype(F32)).astype(BF)


def dot3(left, right, over=((1,), (0,))):
    left_high, left_low = split2(left)
    right_high, right_low = split2(right)
    return dot(left_high, right_high, over) + (
        dot(left_high, right_low, over) + dot(left_low, right_high, over)
    )


def dot1(left, right, over=((1,), (0,))):
    return dot(left.astype(BF), right.astype(BF), over)


def spread(value, begin=0, end=SH):
    first_half = lax.broadcasted_iota(jnp.int32, (value.shape[0], LANES), 1) < SP
    return jnp.concatenate(
        [
            jnp.where(first_half, value[:, head : head + 1], value[:, head + 1 : head + 2])
            for head in range(begin, end, 2)
        ],
        axis=1,
    )


def gather_heads(*values):
    parts = [part for value in values for part in split2(value)]
    sums = dot(jnp.concatenate(parts), head_ones(), ((1,), (1,)))
    found, row = [], 0
    for value in values:
        rows = value.shape[0]
        found.append(sums[row : row + rows] + sums[row + rows : row + 2 * rows])
        row += 2 * rows
    return found


def head_ones():
    head = lax.broadcasted_iota(jnp.int32, (LANES, INNER), 0)
    column = lax.broadcasted_iota(jnp.int32, (LANES, INNER), 1)
    return ((column >= head * SP) & (column < (head + 1) * SP)).astype(BF)


def lower_ones():
    rows = lax.broadcasted_iota(jnp.int32, (BLOCK, BLOCK), 0)
    columns = lax.broadcasted_iota(jnp.int32, (BLOCK, BLOCK), 1)
    return rows >= columns


def cumulate(value, lower, over):
    high, middle, low = split3(value)
    return dot(lower, high, over) + (dot(lower, middle, over) + dot(lower, low, over))


def decays(aux, dt_bias, rate):
    raw = aux[:, 2 * STATE :] + dt_bias
    step = jnp.maximum(raw, 0.0) + jnp.log1p(jnp.exp(-jnp.abs(raw)))
    log_decay = -step * rate
    cumulated = cumulate(log_decay, lower_ones().astype(BF), ((1,), (0,)))
    return raw, step, log_decay, cumulated


def forward_kernel(
    resets, mixed, gate, aux, dt_bias, decay_log, state_in, ssm_out, gated, states, state
):
    number = pl.program_id(0)

    @pl.when(number == 0)
    def _():
        state[...] = state_in[...]

    @pl.when(resets[number] != 0)
    def _():
        state[...] = jnp.zeros_like(state)

    aux_now = aux[...]
    b_in = aux_now[:, :STATE]
    c_out = aux_now[:, STATE : 2 * STATE]
    _, step, _, cumulated = decays(aux_now, dt_bias[...], jnp.exp(decay_log[...]))
    scaled = mixed[...].astype(F32) * spread(step)
    wide = spread(cumulated)
    tail = jnp.exp(wide[BLOCK - 1 :, :] - wide)
    grown = jnp.exp(wide)
    before = state[...]
    states[...] = before[None].astype(BF)
    state[...] = grown[BLOCK - 1 :, :] * before + dot1(b_in, scaled * tail, ((0,), (0,)))
    outer = grown * dot1(c_out, before)
    both = dot3(c_out, b_in, ((1,), (1,)))
    lower = lower_ones()
    flipped = cumulated.T
    first_half = lax.broadcasted_iota(jnp.int32, (BLOCK, LANES), 1) < SP
    scaled_low = scaled.astype(BF)
    zero = jnp.zeros((BLOCK, LANES), BF)
    for pair in range(SH // 2):
        weights = []
        for head in (2 * pair, 2 * pair + 1):
            spread_now = cumulated[:, head : head + 1] - flipped[head : head + 1, :]
            weights.append((jnp.exp(jnp.where(lower, spread_now, NEGATIVE)) * both).astype(BF))
        columns = slice(pair * LANES, (pair + 1) * LANES)
        low = scaled_low[:, columns]
        low = jnp.concatenate([jnp.where(first_half, low, zero), jnp.where(first_half, zero, low)])
        inner = dot(jnp.concatenate(weights, axis=1), low)
        total = inner + outer[:, columns]
        ssm_out[:, columns] = total
        gate_now = gate[:, columns].astype(F32)
        gated[:, columns] = (total * (gate_now / (1.0 + jnp.exp(-gate_now)))).astype(BF)


def silu_of(gate):
    chance = 1.0 / (1.0 + jnp.exp(-gate))
    return gate * chance, chance


def state_back_kernel(
    resets, d_gated, gate, aux, ssm_out, dt_bias, decay_log, d_state_out, d_gate, d_state
):
    number = pl.num_programs(0) - 1 - pl.program_id(0)

    @pl.when(pl.program_id(0) == 0)
    def _():
        d_state[...] = jnp.zeros_like(d_state)

    aux_now = aux[...]
    _, _, _, cumulated = decays(aux_now, dt_bias[...], jnp.exp(decay_log[...]))
    grown = spread(jnp.exp(cumulated))
    gate_silu, chance = silu_of(gate[...].astype(F32))
    d_gated_now = d_gated[...].astype(F32)
    d_gate[...] = (d_gated_now * ssm_out[...] * (chance + gate_silu * (1.0 - chance))).astype(BF)
    d_grown = d_gated_now * gate_silu * grown
    c_out = aux_now[:, STATE : 2 * STATE]
    d_state[...] = grown[BLOCK - 1 :, :] * d_state[...] + dot1(c_out, d_grown, ((0,), (0,)))

    @pl.when(resets[number] != 0)
    def _():
        d_state[...] = jnp.zeros_like(d_state)

    d_state_out[...] = d_state[...].astype(BF)


def backward_kernel(
    resets,
    d_gated,
    mixed,
    gate,
    aux,
    ssm_out,
    states,
    dt_bias,
    decay_log,
    d_state_in,
    d_mixed,
    d_aux,
    d_heads,
    d_state,
):
    number = pl.num_programs(0) - 1 - pl.program_id(0)

    @pl.when(pl.program_id(0) == 0)
    def _():
        d_state[...] = d_state_in[...].astype(F32)
        d_heads[...] = jnp.zeros_like(d_heads)

    lower = lower_ones()
    aux_now = aux[...]
    b_in = aux_now[:, :STATE]
    c_out = aux_now[:, STATE : 2 * STATE]
    rate = jnp.exp(decay_log[...])
    raw, step, log_decay, cumulated = decays(aux_now, dt_bias[...], rate)
    step_wide = spread(step)
    mixed_now = mixed[...].astype(F32)
    scaled = mixed_now * step_wide
    wide = spread(cumulated)
    tail = jnp.exp(wide[BLOCK - 1 :, :] - wide)
    grown = jnp.exp(wide)
    gate_now = gate[...].astype(F32)
    gate_silu, _ = silu_of(gate_now)
    d_gated_now = d_gated[...].astype(F32)
    ssm_now = ssm_out[...]
    d_out = d_gated_now * gate_silu
    before = states[0].astype(F32)
    d_after = d_state[...]
    d_grown = d_out * grown
    d_c = dot1(d_grown, before, ((1,), (1,)))
    d_before = grown[BLOCK - 1 :, :] * d_after + dot1(c_out, d_grown, ((0,), (0,)))
    tailed = scaled * tail
    d_b = dot1(tailed, d_after, ((1,), (1,)))
    d_tailed = dot1(b_in, d_after)
    ends = jnp.sum(tailed * d_tailed, axis=0, keepdims=True) + grown[BLOCK - 1 :, :] * jnp.sum(
        d_after * before, axis=0, keepdims=True
    )
    both = dot3(c_out, b_in, ((1,), (1,)))
    flipped = cumulated.T
    first_half = lax.broadcasted_iota(jnp.int32, (BLOCK, LANES), 1) < SP
    scaled_low = scaled.astype(BF)
    d_low = d_out.astype(BF)
    zero = jnp.zeros((BLOCK, LANES), BF)
    d_both = jnp.zeros((BLOCK, BLOCK), F32)
    parts = []
    for pair in range(SH // 2):
        columns = slice(pair * LANES, (pair + 1) * LANES)
        falls = []
        for head in (2 * pair, 2 * pair + 1):
            spread_now = cumulated[:, head : head + 1] - flipped[head : head + 1, :]
            falls.append(jnp.exp(jnp.where(lower, spread_now, NEGATIVE)))
        weight = jnp.concatenate([(falls[0] * both).astype(BF), (falls[1] * both).astype(BF)])
        low = d_low[:, columns]
        low = jnp.concatenate([jnp.where(first_half, low, zero), jnp.where(first_half, zero, low)])
        d_weight = dot(low, scaled_low[:, columns], ((1,), (1,)))
        d_both = d_both + falls[0] * d_weight[:BLOCK] + falls[1] * d_weight[BLOCK:]
        parts.append(dot(weight, low, ((0,), (0,))))
    d_inner = jnp.concatenate(parts, axis=1)
    carried = tail * d_tailed
    d_scaled = d_inner + carried
    d_mixed[...] = (d_scaled * step_wide).astype(BF)
    d_step, d_cumulated, d_last = gather_heads(
        d_scaled * mixed_now,
        d_low.astype(F32) * ssm_now - scaled_low.astype(F32) * d_inner - scaled * carried,
        jnp.broadcast_to(ends, (8, INNER)),
    )
    d_decay = cumulate(d_cumulated, lower.astype(BF), ((0,), (0,))) + d_last[:1]
    d_raw = (d_step - d_decay * rate) * (1.0 / (1.0 + jnp.exp(-raw)))
    real = lax.broadcasted_iota(jnp.int32, (BLOCK, LANES), 1) < SH
    d_raw = jnp.where(real, d_raw, 0.0)
    d_c = d_c + dot1(d_both, b_in)
    d_b = d_b + dot1(d_both, c_out, ((0,), (0,)))
    d_aux[...] = jnp.concatenate([d_b, d_c, d_raw], axis=1).astype(BF)
    d_heads[...] += jnp.concatenate(
        [
            jnp.sum(d_raw, axis=0, keepdims=True),
            jnp.sum(jnp.where(real, d_decay * log_decay, 0.0), axis=0, keepdims=True),
            jnp.zeros((6, LANES), F32),
        ]
    )
    d_state[...] = d_before

    @pl.when(resets[number] != 0)
    def _():
        d_state[...] = jnp.zeros_like(d_state)


def scalars():
    return pl.BlockSpec(memory_space=pltpu.SMEM)


def whole(shape):
    return pl.BlockSpec(shape, lambda number: (0,) * len(shape))


def params_of(limit=VMEM_LIMIT):
    return pltpu.CompilerParams(dimension_semantics=("arbitrary",), vmem_limit_bytes=limit)


def run_forward(resets, mixed, aux, dt_bias, decay_log, state_in):
    rows = mixed.shape[0]
    count = rows // BLOCK
    return pl.pallas_call(
        forward_kernel,
        grid=(count,),
        in_specs=[
            scalars(),
            pl.BlockSpec((BLOCK, INNER), lambda number: (number, 0)),
            pl.BlockSpec((BLOCK, INNER), lambda number: (number, 1)),
            pl.BlockSpec((BLOCK, 3 * LANES), lambda number: (number, 0)),
            whole((1, LANES)),
            whole((1, LANES)),
            whole((STATE, INNER)),
        ],
        out_specs=[
            pl.BlockSpec((BLOCK, INNER), lambda number: (number, 0)),
            pl.BlockSpec((BLOCK, INNER), lambda number: (number, 0)),
            pl.BlockSpec((1, STATE, INNER), lambda number: (number, 0, 0)),
        ],
        out_shape=[
            jax.ShapeDtypeStruct((rows, INNER), F32),
            jax.ShapeDtypeStruct((rows, INNER), BF),
            jax.ShapeDtypeStruct((count, STATE, INNER), BF),
        ],
        scratch_shapes=[pltpu.VMEM((STATE, INNER), F32)],
        compiler_params=params_of(),
        cost_estimate=LONG,
        name="ssm_forward",
    )(resets, mixed, mixed, aux, dt_bias, decay_log, state_in)


def run_state_back(resets, d_gated, mixed, aux, ssm_out, dt_bias, decay_log):
    count = mixed.shape[0] // BLOCK
    turned = lambda number: (count - 1 - number, 0)
    return pl.pallas_call(
        state_back_kernel,
        grid=(count,),
        in_specs=[
            scalars(),
            pl.BlockSpec((BLOCK, INNER), turned),
            pl.BlockSpec((BLOCK, INNER), lambda number: (count - 1 - number, 1)),
            pl.BlockSpec((BLOCK, 3 * LANES), turned),
            pl.BlockSpec((BLOCK, INNER), turned),
            whole((1, LANES)),
            whole((1, LANES)),
        ],
        out_specs=[whole((STATE, INNER)), pl.BlockSpec((BLOCK, INNER), turned)],
        out_shape=[
            jax.ShapeDtypeStruct((STATE, INNER), BF),
            jax.ShapeDtypeStruct((mixed.shape[0], INNER), BF),
        ],
        scratch_shapes=[pltpu.VMEM((STATE, INNER), F32)],
        compiler_params=params_of(),
        cost_estimate=COST,
        name="ssm_state_back",
    )(resets, d_gated, mixed, aux, ssm_out, dt_bias, decay_log)


def run_backward(resets, d_gated, mixed, aux, ssm_out, states, dt_bias, decay_log, d_state_in):
    rows = mixed.shape[0]
    count = rows // BLOCK
    turned = lambda number: (count - 1 - number, 0)
    return pl.pallas_call(
        backward_kernel,
        grid=(count,),
        in_specs=[
            scalars(),
            pl.BlockSpec((BLOCK, INNER), turned),
            pl.BlockSpec((BLOCK, INNER), turned),
            pl.BlockSpec((BLOCK, INNER), lambda number: (count - 1 - number, 1)),
            pl.BlockSpec((BLOCK, 3 * LANES), turned),
            pl.BlockSpec((BLOCK, INNER), turned),
            pl.BlockSpec((1, STATE, INNER), lambda number: (count - 1 - number, 0, 0)),
            whole((1, LANES)),
            whole((1, LANES)),
            whole((STATE, INNER)),
        ],
        out_specs=[
            pl.BlockSpec((BLOCK, INNER), turned),
            pl.BlockSpec((BLOCK, 3 * LANES), turned),
            whole((8, LANES)),
        ],
        out_shape=[
            jax.ShapeDtypeStruct((rows, INNER), BF),
            jax.ShapeDtypeStruct((rows, 3 * LANES), BF),
            jax.ShapeDtypeStruct((8, LANES), F32),
        ],
        scratch_shapes=[pltpu.VMEM((STATE, INNER), F32)],
        compiler_params=params_of(),
        cost_estimate=COST,
        name="ssm_backward",
    )(resets, d_gated, mixed, mixed, aux, ssm_out, states, dt_bias, decay_log, d_state_in)


def head_rows(ref, start, group, width):
    return jnp.concatenate(
        [
            ref[start : start + BLOCK, (group * width + head) * HD : (group * width + head + 1) * HD]
            for head in range(width)
        ]
    )


def masked_scores(q_rows, k_rows, bias_row, lower, width):
    raw = dot(q_rows, k_rows, ((1,), (1,))) + bias_row
    edge = raw.shape[1] - BLOCK
    corner = jnp.where(jnp.concatenate([lower] * width), raw[:, edge:], NEGATIVE)
    return jnp.concatenate([raw[:, :edge], corner], axis=1)


def attend_kernel(q_ref, prior_ref, here_ref, bias_ref, out_ref, total_ref):
    width = QH // KVH
    rows = q_ref.shape[0]
    halo = prior_ref.shape[0]
    lower = lower_ones()
    for group in range(KVH):
        key_columns = slice(group * HD, (group + 1) * HD)
        value_columns = slice((KVH + group) * HD, (KVH + group + 1) * HD)
        keys = jnp.concatenate([prior_ref[:, key_columns], here_ref[:, key_columns]])
        values = jnp.concatenate([prior_ref[:, value_columns], here_ref[:, value_columns]])
        for block in range(rows // BLOCK):
            start = block * BLOCK
            reach = halo + start + BLOCK
            q_rows = head_rows(q_ref, start, group, width)
            scores = masked_scores(
                q_rows, keys[:reach], bias_ref[block : block + 1, :reach], lower, width
            )
            top = jnp.max(scores, axis=1, keepdims=True)
            powers = jnp.exp(scores - top)
            total = jnp.sum(powers, axis=1, keepdims=True)
            probs = (powers * (1.0 / total)).astype(BF)
            out = dot(probs, values[:reach])
            log_total = top + jnp.log(total)
            for head in range(width):
                place = group * width + head
                some = slice(head * BLOCK, (head + 1) * BLOCK)
                out_ref[start : start + BLOCK, place * HD : (place + 1) * HD] = out[some].astype(BF)
                total_ref[start : start + BLOCK, place : place + 1] = log_total[some]


def attend_back_kernel(
    q_ref, prior_ref, here_ref, bias_ref, total_ref, d_ref, dq_ref, d_prior_ref, d_here_ref, sums
):
    width = QH // KVH
    rows = q_ref.shape[0]
    halo = prior_ref.shape[0]
    lower = lower_ones()
    sums[...] = jnp.zeros_like(sums)
    for group in range(KVH):
        key_columns = slice(group * HD, (group + 1) * HD)
        value_columns = slice((KVH + group) * HD, (KVH + group + 1) * HD)
        keys = jnp.concatenate([prior_ref[:, key_columns], here_ref[:, key_columns]])
        values = jnp.concatenate([prior_ref[:, value_columns], here_ref[:, value_columns]])
        for block in range(rows // BLOCK):
            start = block * BLOCK
            reach = halo + start + BLOCK
            q_rows = head_rows(q_ref, start, group, width)
            d_rows = head_rows(d_ref, start, group, width)
            scores = masked_scores(
                q_rows, keys[:reach], bias_ref[block : block + 1, :reach], lower, width
            )
            log_total = jnp.concatenate(
                [
                    total_ref[start : start + BLOCK, group * width + head : group * width + head + 1]
                    for head in range(width)
                ]
            )
            probs = jnp.exp(scores - log_total)
            probs_low = probs.astype(BF)
            d_probs = dot(d_rows, values[:reach], ((1,), (1,)))
            weighed = probs * d_probs
            d_scores = (weighed - probs * jnp.sum(weighed, axis=1, keepdims=True)).astype(BF)
            d_queries = dot(d_scores, keys[:reach]) * HD**-0.5
            for head in range(width):
                place = group * width + head
                some = slice(head * BLOCK, (head + 1) * BLOCK)
                dq_ref[start : start + BLOCK, place * HD : (place + 1) * HD] = d_queries[some].astype(BF)
            sums[:reach, key_columns] += dot(d_scores, q_rows, ((0,), (0,)))
            sums[:reach, value_columns] += dot(probs_low, d_rows, ((0,), (0,)))
    d_prior_ref[...] = sums[:halo].astype(BF)
    d_here_ref[...] = sums[halo:]


def run_attend(queries, prior, here, bias):
    rows = queries.shape[0]
    return pl.pallas_call(
        attend_kernel,
        out_shape=[
            jax.ShapeDtypeStruct((rows, QH * HD), BF),
            jax.ShapeDtypeStruct((rows, QH), F32),
        ],
        compiler_params=pltpu.CompilerParams(vmem_limit_bytes=VMEM_LIMIT),
        cost_estimate=LONG,
        name="attend",
    )(queries, prior, here, bias)


def run_attend_back(queries, prior, here, bias, log_total, d_attended):
    rows = queries.shape[0]
    halo = prior.shape[0]
    return pl.pallas_call(
        attend_back_kernel,
        out_shape=[
            jax.ShapeDtypeStruct((rows, QH * HD), BF),
            jax.ShapeDtypeStruct((halo, 2 * KVH * HD), BF),
            jax.ShapeDtypeStruct((rows, 2 * KVH * HD), F32),
        ],
        scratch_shapes=[pltpu.VMEM((halo + rows, 2 * KVH * HD), F32)],
        compiler_params=pltpu.CompilerParams(vmem_limit_bytes=VMEM_LIMIT),
        cost_estimate=COST,
        name="attend_back",
    )(queries, prior, here, bias, log_total, d_attended)


def swap(value):
    return lax.ppermute(value, "shard", SWAP)


def natural(mine, theirs, position, axis):
    return jnp.where(
        position == 0,
        jnp.concatenate([mine, theirs], axis=axis),
        jnp.concatenate([theirs, mine], axis=axis),
    )


def half_of(value, which, axis):
    size = value.shape[axis] // 2
    return lax.dynamic_slice_in_dim(value, which * size, size, axis)


class Stream:
    def __init__(self, terms, whole, *orders):
        self.terms = terms
        self.count = lax.axis_size("rep")
        self.bits = self.count.bit_length() - 1
        self.stack = None
        self.got = None
        self.gone = 0
        if self.count != 1 << self.bits:
            self.stack = lax.psum(self.part(0, terms[0].shape[0]), "rep")
            self.bits = 0
        places = range(self.bits)
        self.orders = [
            [bit for bit in order if bit < self.bits] + [bit for bit in places if bit not in order]
            for order in orders
        ]
        rep, core = lax.axis_index("rep"), lax.axis_index("shard")
        self.cuts = max(0, self.bits - whole)
        self.sides = [
            jnp.where(core == 0, (rep >> first) & 1, (rep >> second) & 1)
            for first, second in zip(*self.orders)
        ][: self.cuts]
        self.steps = [("scatter", step) for step in places[: self.cuts]]
        self.steps += [("exchange", step) for step in places[self.cuts :]]
        self.steps += [("gather", step) for step in reversed(places[: self.cuts])]

    def pairs(self, step):
        return [
            (rep * 2 + core, (rep ^ (1 << self.orders[core][step])) * 2 + core)
            for rep in range(self.count)
            for core in range(2)
        ]

    def part(self, start, size):
        total = lax.dynamic_slice_in_dim(self.terms[0], start, size, 0).astype(F32)
        for term in self.terms[1:]:
            total = total + lax.dynamic_slice_in_dim(term, start, size, 0).astype(F32)
        return total.astype(BF)

    def latest(self):
        if self.got is not None:
            return self.got
        return self.terms[-1] if self.stack is None else self.stack

    def hold(self, token):
        if self.got is not None:
            self.got = after(self.got, token)
        elif self.stack is None:
            self.terms[-1] = after(self.terms[-1], token)

    def prepare(self):
        kind, step = self.steps[0]
        if kind == "gather":
            if self.stack is None:
                self.stack = self.part(0, self.terms[0].shape[0])
            else:
                self.stack = jnp.concatenate([self.stack, self.got])
            self.operand = self.stack
        elif kind == "exchange":
            self.operand = self.part(0, self.terms[0].shape[0])
        else:
            size = self.terms[0].shape[0] // 2
            self.operand = self.part((1 - self.sides[step]) * size, size)

    def go(self):
        kind, step = self.steps.pop(0)
        self.gone += 1
        got = lax.ppermute(self.operand, ("rep", "shard"), self.pairs(step))
        if kind == "gather":
            self.got = got
        elif kind == "exchange":
            self.terms = [self.operand, got]
        else:
            size = self.terms[0].shape[0] // 2
            self.terms = [
                lax.dynamic_slice_in_dim(term, self.sides[step] * size, size, 0)
                for term in self.terms
            ] + [got]

    def own(self):
        block = jnp.zeros((), jnp.int32)
        for side in self.sides:
            block = 2 * block + side
        return block.astype(jnp.int32)

    def finish(self, outputs, started=None, weights=()):
        if self.stack is None:
            self.stack = self.part(0, self.terms[0].shape[0])
        stacks = [self.stack] if self.got is None else [self.stack, self.got]
        blocks = 1 << self.cuts
        far = max(1, blocks // 4)
        quarters = blocks // far
        each = quarters // len(stacks)
        size = stacks[0].shape[0] // each // far
        width = stacks[0].shape[1]
        own = self.own()
        if size % 16:
            flat = jnp.concatenate(stacks).reshape(blocks, size, width)
            flat = jnp.zeros_like(flat).at[jnp.arange(blocks) ^ own].set(flat).reshape(-1, width)
            made = []
            for shape, _, pieces in outputs:
                cuts = [flat[:, begin:end].astype(F32) for _, begin, end in pieces]
                if pieces[0][0] == TURNED:
                    made.append(cuts[0].T)
                    continue
                whole_width = shape.shape[-1]
                if len(shape.shape) == 3:
                    value = jnp.stack(cuts)
                    value = jnp.pad(value, ((0, 0), (0, 0), (whole_width - value.shape[-1], 0)))
                else:
                    value = jnp.concatenate(cuts, axis=1)
                made.append(value)
            products = [
                jnp.sum(
                    value * weight[:, : value.shape[1]].astype(F32),
                    axis=0 if pieces[0][0] == TURNED else 1,
                )
                for value, weight, (_, _, pieces) in zip(made, weights, outputs)
                if weight is not None
            ]
            if started is not None:
                made[-1] = jnp.concatenate([made[-1], started[:, made[-1].shape[1] :]], axis=1)
            if products:
                made.append(jnp.broadcast_to(sum(products), (8, products[0].shape[0])))
            return made
        rows = far * size
        in_specs = [
            pl.BlockSpec((rows, width), lambda step, places: (jnp.minimum(step, each - 1), 0))
        ]
        if len(stacks) == 2:
            in_specs.append(
                pl.BlockSpec((rows, width), lambda step, places: (jnp.maximum(step - each, 0), 0))
            )
        out_specs = []
        scratch = []
        for shape, block, pieces in outputs:
            if pieces[0][0] == TURNED:
                out_specs.append(
                    pl.BlockSpec((shape.shape[0], rows), lambda step, places: (0, places[step]))
                )
                scratch = [pltpu.VMEM((rows, block), F32)]
            elif len(shape.shape) == 3:
                last = shape.shape[2] // block - 1
                out_specs.append(
                    pl.BlockSpec(
                        (shape.shape[0], rows, block),
                        lambda step, places, last=last: (0, places[step], last),
                    )
                )
            else:
                out_specs.append(pl.BlockSpec((rows, block), lambda step, places: (places[step], 0)))
        inputs = list(stacks)
        shapes = [shape for shape, _, _ in outputs]
        for weight, (_, block, pieces) in zip(weights, outputs):
            if weight is None:
                continue
            inputs.append(weight)
            if pieces[0][0] == TURNED:
                in_specs.append(
                    pl.BlockSpec((weight.shape[0], rows), lambda step, places: (0, places[step]))
                )
            else:
                in_specs.append(pl.BlockSpec((rows, block), lambda step, places: (places[step], 0)))
        if weights:
            out_specs.append(pl.BlockSpec((8, rows), lambda step, places: (0, places[step])))
            shapes.append(jax.ShapeDtypeStruct((8, rows * quarters), F32))
        aliases = {}
        if started is not None:
            aliases = {1 + len(inputs): len(outputs) - 1}
            inputs.append(started)
            in_specs.append(pl.BlockSpec(memory_space=pl.ANY))
        places = jnp.concatenate(
            [jnp.arange(quarters, dtype=jnp.int32) ^ (own // far), (own % far).reshape(1)]
        )
        return pl.pallas_call(
            functools.partial(
                finish_kernel,
                len(stacks),
                far,
                [cut for _, _, cut in outputs],
                [weight is not None for weight in weights],
            ),
            grid_spec=pltpu.PrefetchScalarGridSpec(
                num_scalar_prefetch=1,
                grid=(quarters,),
                in_specs=in_specs,
                out_specs=out_specs,
                scratch_shapes=scratch,
            ),
            out_shape=shapes,
            input_output_aliases=aliases,
            compiler_params=params_of(),
            cost_estimate=COST,
            name="unpack",
        )(places, *inputs)


def finish_kernel(count, far, layout, weighed, places, *refs):
    turned = any(pieces[0][0] == TURNED for pieces in layout)
    if turned:
        held, refs = refs[-1], refs[:-1]
    if any(weighed):
        products, refs = refs[-1], refs[:-1]
    outputs = refs[-len(layout) :]
    weights = list(refs[count : count + sum(weighed)])
    steps = pl.num_programs(0)
    within = places[steps]
    size = refs[0].shape[0] // far

    def write(ref):
        width = ref.shape[1]
        for number in range(far):
            row = pl.multiple_of((within ^ number) * size, size)
            piece_rows = slice(number * size, (number + 1) * size)
            for out, pieces in zip(outputs, layout):
                for target, begin, end in pieces:
                    if target == TURNED:
                        continue
                    value = ref[piece_rows, begin:end].astype(F32)
                    if len(out.shape) == 3:
                        out[target, pl.ds(row, size), :] = value
                    else:
                        out[pl.ds(row, size), target : target + end - begin] = value
            if turned:
                held[pl.ds(row, size), :] = ref[piece_rows, width - held.shape[1] :].astype(F32)
        if turned:
            flipped = held[...].T
            for out, pieces in zip(outputs, layout):
                target, begin, end = pieces[0]
                if target == TURNED:
                    first = width - held.shape[1]
                    out[...] = flipped[begin - first : end - first, :]

    if count == 1:
        write(refs[0])
    else:

        @pl.when(pl.program_id(0) < steps // 2)
        def _():
            write(refs[0])

        @pl.when(pl.program_id(0) >= steps // 2)
        def _():
            write(refs[1])

    if any(weighed):
        ones = jnp.ones((8, LANES), BF)
        total = jnp.zeros(products.shape, F32)
        for out, pieces, used in zip(outputs, layout, weighed):
            if not used:
                continue
            product = out[...] * weights.pop(0)[...].astype(F32)
            if pieces[0][0] == TURNED:
                total = total + jnp.sum(product, axis=0, keepdims=True)
                continue
            narrow = product[:, :LANES]
            for column in range(LANES, product.shape[1], LANES):
                narrow = narrow + product[:, column : column + LANES]
            for part in split3(narrow):
                total = total + dot(ones, part, ((1,), (1,)))
        products[...] = total


def after(value, *others):
    return lax.optimization_barrier((value, *others))[0]


def fence(value, *others):
    anywhere = pl.BlockSpec(memory_space=pl.ANY)
    return pl.pallas_call(
        lambda *refs: None,
        in_specs=[anywhere] * (1 + len(others)),
        out_specs=anywhere,
        out_shape=jax.ShapeDtypeStruct(value.shape, value.dtype),
        input_output_aliases={0: 0},
        cost_estimate=COST,
        name="fence",
    )(value, *others)


def columns_of(ref, which, size):
    return ref[:, pl.ds(pl.multiple_of(which * size, size), size)]


def inverse_rms(values):
    return lax.rsqrt(jnp.mean(values * values, axis=-1, keepdims=True) + EPSILON)


def norm_back(values, inverse, gain, grad):
    scaled = grad * gain
    shared = jnp.mean(scaled * values, axis=-1, keepdims=True) * (inverse * inverse)
    return (
        inverse * (scaled - values * shared),
        jnp.sum(grad * (values * inverse), axis=0, keepdims=True),
    )


def project_kernel(
    position,
    resets,
    tokens,
    gains,
    dt_bias,
    decay_log,
    query_mine,
    query_theirs,
    kv_mine,
    kv_theirs,
    aux_mine,
    aux_theirs,
    ssm_mine,
    ssm_theirs,
    normed,
    queries,
    key_vals,
    aux,
    mixed,
    state_out,
    tails,
    carries,
):
    here = position[0]
    half = tokens.shape[1] // 2
    step = pl.program_id(0)
    blocks = tokens.shape[0] // BLOCK

    def product(mine, theirs, over=((1,), (0,))):
        return dot(columns_of(normed, here, half), mine[...], over) + dot(
            columns_of(normed, 1 - here, half), theirs[...], over
        )

    @pl.when(pl.program_id(0) == 0)
    def _():
        hidden = tokens[...].astype(F32)
        normed[...] = (hidden * inverse_rms(hidden) * gains[0:1]).astype(BF)
        queries[...] = product(query_mine, query_theirs).astype(BF) * jnp.asarray(HD**-0.5, BF)
        key_vals[...] = product(kv_mine, kv_theirs).astype(BF)
        found = product(aux_mine, aux_theirs, ((1,), (1,)))
        aux[:, : found.shape[1]] = found
        aux[:, found.shape[1] :] = jnp.zeros_like(aux[:, found.shape[1] :])
        rate = jnp.exp(decay_log[...])
        for block in range(blocks):
            rows = slice(block * BLOCK, (block + 1) * BLOCK)
            _, step_size, _, cumulated = decays(aux[rows, :], dt_bias[...], rate)
            last = cumulated[BLOCK - 1 :, :]
            tails[rows, :] = step_size * jnp.exp(last - cumulated)
            carries[block : block + 1, :] = jnp.exp(last)

    found = product(ssm_mine, ssm_theirs)
    mixed[...] = found.astype(BF)

    for number in range(INNER // CHUNK):

        @pl.when(step == number)
        def _():
            heads = (number * CHUNK // SP, (number + 1) * CHUNK // SP)
            scaled = (found * spread(tails[...], *heads)).astype(BF)
            carried = spread(carries[...], *heads)
            state = jnp.zeros((STATE, CHUNK), F32)
            for block in range(blocks):
                rows = slice(block * BLOCK, (block + 1) * BLOCK)
                b_in = aux[rows, :STATE].astype(BF)
                state = jnp.where(resets[block] != 0, 0.0, carried[block : block + 1, :] * state)
                state = state + dot(b_in, scaled[rows, :], ((0,), (0,)))
            state_out[...] = state


CHUNK = 512


def run_project(position, resets, tokens, gains, dt_bias, decay_log, query, kv, aux, ssm):
    rows, width = tokens.shape
    half = width // 2
    inner = ssm[0].shape[1]
    aux_width = 3 * LANES
    fixed = lambda shape: pl.BlockSpec(shape, lambda step, place, resets: (0,) * len(shape))
    sliding = pl.BlockSpec((half, CHUNK), lambda step, place, resets: (0, step))
    weights = [fixed(item.shape) for item in (*query, *kv, *aux)]
    return pl.pallas_call(
        project_kernel,
        grid_spec=pltpu.PrefetchScalarGridSpec(
            num_scalar_prefetch=2,
            grid=(inner // CHUNK,),
            in_specs=[
                *[fixed(item.shape) for item in (tokens, gains, dt_bias, decay_log)],
                *weights,
                sliding,
                sliding,
            ],
            out_specs=[
                fixed((rows, width)),
                fixed((rows, KV_AT)),
                fixed((rows, AUX_AT - KV_AT)),
                fixed((rows, aux_width)),
                pl.BlockSpec((rows, CHUNK), lambda step, place, resets: (0, step)),
                pl.BlockSpec(
                    (STATE, CHUNK),
                    lambda step, place, resets: (0, jnp.minimum(step, INNER // CHUNK - 1)),
                ),
            ],
            scratch_shapes=[pltpu.VMEM((rows, LANES), F32), pltpu.VMEM((8, LANES), F32)],
        ),
        out_shape=[
            jax.ShapeDtypeStruct((rows, width), BF),
            jax.ShapeDtypeStruct((rows, KV_AT), BF),
            jax.ShapeDtypeStruct((rows, AUX_AT - KV_AT), BF),
            jax.ShapeDtypeStruct((rows, aux_width), F32),
            jax.ShapeDtypeStruct((rows, inner), BF),
            jax.ShapeDtypeStruct((STATE, INNER), F32),
        ],
        compiler_params=params_of(LARGE_LIMIT),
        cost_estimate=LONG,
        name="project",
    )(position, resets, tokens, gains, dt_bias, decay_log, *query, *kv, *aux, *ssm)


def middle_kernel(
    position,
    tokens,
    attended,
    gated,
    cotangent,
    gains,
    attn_mine,
    attn_theirs,
    ssm_mine,
    ssm_theirs,
    gate_mine,
    gate_theirs,
    up_mine,
    up_theirs,
    down_mine,
    down_theirs,
    output,
    d_middle,
    d_attn_branch,
    d_ssm_branch,
    d_attended,
    d_gated,
    gain_grads,
    grad_down_theirs,
    grad_down_mine,
    grad_wide_theirs,
    grad_wide_mine,
    attn_branch,
    ssm_branch,
    middle,
    normed,
    flipped,
    out_sum,
    d_normed,
):
    here = position[0]
    step = pl.program_id(0)
    count = pl.num_programs(0)
    width = tokens.shape[1]
    half = width // 2
    attn_half = attended.shape[1] // 2
    ssm_half = gated.shape[1] // 2
    flat = ((1,), (1,))

    def place(which, size):
        return pl.ds(pl.multiple_of(which * size, size), size)

    @pl.when(step == 0)
    def _():
        attn = dot(columns_of(attended, here, attn_half), attn_mine[...]) + dot(
            columns_of(attended, 1 - here, attn_half), attn_theirs[...]
        )
        attn_branch[...] = attn
        ssm = dot(columns_of(gated, here, ssm_half), ssm_mine[...]) + dot(
            columns_of(gated, 1 - here, ssm_half), ssm_theirs[...]
        )
        ssm_branch[...] = ssm
        joined = tokens[...].astype(F32) + 0.5 * (
            attn * inverse_rms(attn) * gains[1:2] + ssm * inverse_rms(ssm) * gains[2:3]
        )
        middle[...] = joined
        out_sum[...] = joined
        scaled = joined * inverse_rms(joined) * gains[3:4]
        normed[...] = scaled.astype(BF)
        flipped[...] = scaled.T.astype(BF)
        d_normed[...] = jnp.zeros_like(d_normed)

    first = step < count // 2
    mine = columns_of(normed, here, half)
    theirs = columns_of(normed, 1 - here, half)
    gate_val = dot(mine, gate_mine[...]) + dot(theirs, gate_theirs[...])
    up_val = dot(mine, up_mine[...]) + dot(theirs, up_theirs[...])
    gate_silu, chance = silu_of(gate_val)
    activated = (gate_silu * up_val).astype(BF)
    down = jnp.where(first, down_theirs[...], down_mine[...])
    d_activated = dot(cotangent[...], down, flat)
    out_sum[...] += dot(activated, down)
    d_up = (d_activated * gate_silu).astype(BF)
    d_gate = (d_activated * up_val * (chance + gate_silu * (1.0 - chance))).astype(BF)
    d_normed[:, place(here, half)] += dot(d_gate, gate_mine[...], flat) + dot(d_up, up_mine[...], flat)
    d_normed[:, place(1 - here, half)] += dot(d_gate, gate_theirs[...], flat) + dot(
        d_up, up_theirs[...], flat
    )
    grad_down = dot(activated, cotangent[...], ((0,), (0,))).astype(BF)

    @pl.when(first)
    def _():
        grad_down_theirs[...] = grad_down

    @pl.when(jnp.logical_not(first))
    def _():
        grad_down_mine[...] = grad_down

    for which, ref in ((here, grad_wide_mine), (1 - here, grad_wide_theirs)):
        turned = flipped[place(which, half), :]
        ref[:, :CHUNK] = dot(turned, d_gate).astype(BF)
        ref[:, CHUNK:] = dot(turned, d_up).astype(BF)

    @pl.when(step == count - 1)
    def _():
        output[...] = out_sum[...].astype(BF)
        joined = middle[...]
        d_joined, d_gain_ff = norm_back(joined, inverse_rms(joined), gains[3:4], d_normed[...])
        d_joined = cotangent[...].astype(F32) + d_joined
        d_middle[...] = d_joined
        attn = attn_branch[...]
        d_attn, d_gain_attn = norm_back(attn, inverse_rms(attn), gains[1:2], 0.5 * d_joined)
        d_attn_low = d_attn.astype(BF)
        d_attn_branch[...] = d_attn_low
        ssm = ssm_branch[...]
        d_ssm, d_gain_ssm = norm_back(ssm, inverse_rms(ssm), gains[2:3], 0.5 * d_joined)
        d_ssm_low = d_ssm.astype(BF)
        d_ssm_branch[...] = d_ssm_low
        gain_grads[...] = jnp.concatenate(
            [d_gain_attn, d_gain_ssm, d_gain_ff, jnp.zeros((5, width), F32)]
        )
        for which, attn_weight, ssm_weight in (
            (here, attn_mine, ssm_mine),
            (1 - here, attn_theirs, ssm_theirs),
        ):
            d_attended[:, place(which, attn_half)] = dot(d_attn_low, attn_weight[...], flat).astype(BF)
            d_gated[:, place(which, ssm_half)] = dot(d_ssm_low, ssm_weight[...], flat).astype(BF)


def run_middle(position, tokens, attended, gated, cotangent, gains, attn, ssm, gate, up, down):
    rows, width = tokens.shape
    half = width // 2
    hidden = gate[0].shape[1]
    count = hidden // CHUNK
    fixed = lambda shape: pl.BlockSpec(shape, lambda step, place: (0,) * len(shape))

    def chunk(step, place):
        first = step < count // 2
        return jnp.where(first, 1 - place[0], place[0]) * (count // 2) + step % (count // 2)

    sliding = pl.BlockSpec((half, CHUNK), lambda step, place: (0, chunk(step, place)))
    early = lambda step, place: (jnp.minimum(step, count // 2 - 1), 0)
    late = lambda step, place: (jnp.maximum(step - count // 2, 0), 0)
    wide = pl.BlockSpec((half, 2 * CHUNK), lambda step, place: (0, chunk(step, place)))
    low = lambda shape: jax.ShapeDtypeStruct(shape, BF)
    full = lambda shape: jax.ShapeDtypeStruct(shape, F32)
    return pl.pallas_call(
        middle_kernel,
        grid_spec=pltpu.PrefetchScalarGridSpec(
            num_scalar_prefetch=1,
            grid=(count,),
            in_specs=[
                *[fixed(item.shape) for item in (tokens, attended, gated, cotangent, gains)],
                *[fixed(item.shape) for item in (*attn, *ssm)],
                *[sliding] * 4,
                pl.BlockSpec((CHUNK, width), late),
                pl.BlockSpec((CHUNK, width), early),
            ],
            out_specs=[
                *[fixed((rows, width))] * 4,
                fixed(attended.shape),
                fixed(gated.shape),
                fixed((8, width)),
                pl.BlockSpec((CHUNK, width), early),
                pl.BlockSpec((CHUNK, width), late),
                wide,
                wide,
            ],
            scratch_shapes=[
                *[pltpu.VMEM((rows, width), F32)] * 3,
                pltpu.VMEM((rows, width), BF),
                pltpu.VMEM((width, rows), BF),
                *[pltpu.VMEM((rows, width), F32)] * 2,
            ],
        ),
        out_shape=[
            low((rows, width)),
            full((rows, width)),
            low((rows, width)),
            low((rows, width)),
            low(attended.shape),
            low(gated.shape),
            full((8, width)),
            low((hidden // 2, width)),
            low((hidden // 2, width)),
            low((half, 2 * hidden)),
            low((half, 2 * hidden)),
        ],
        compiler_params=params_of(LARGE_LIMIT),
        cost_estimate=LONG,
        name="middle",
    )(position, tokens, attended, gated, cotangent, gains, *attn, *ssm, *gate, *up, *down)


def outs_grads_kernel(
    position, attended, gated, normed, d_attn, d_ssm, d_gate, theirs, mine
):
    here = position[0]
    step = pl.program_id(0)
    which = jnp.where(step == 0, 1 - here, here)
    rows = theirs.shape[0]
    down = ((0,), (0,))

    def write(ref):
        at = 0
        for left, right in ((attended, d_attn), (gated, d_ssm), (normed, d_gate)):
            half = left.shape[1] // 2
            for begin in range(0, half, rows):
                turned = left[:, pl.ds(pl.multiple_of(which * half + begin, rows), rows)]
                ref[:, at : at + right.shape[1]] = dot(turned, right[...], down).astype(BF)
                at += right.shape[1]

    @pl.when(step == 0)
    def _():
        write(theirs)

    @pl.when(step == 1)
    def _():
        write(mine)


def run_outs_grads(position, attended, gated, normed, d_attn, d_ssm, d_gate):
    inputs = (attended, gated, normed, d_attn, d_ssm, d_gate)
    rows = attended.shape[1] // 2
    width = sum(
        left.shape[1] // 2 // rows * right.shape[1] for left, right in zip(inputs[:3], inputs[3:])
    )
    fixed = lambda shape: pl.BlockSpec(shape, lambda step, place: (0, 0))
    return pl.pallas_call(
        outs_grads_kernel,
        grid_spec=pltpu.PrefetchScalarGridSpec(
            num_scalar_prefetch=1,
            grid=(2,),
            in_specs=[fixed(item.shape) for item in inputs],
            out_specs=[fixed((rows, width))] * 2,
        ),
        out_shape=[jax.ShapeDtypeStruct((rows, width), BF)] * 2,
        compiler_params=params_of(),
        cost_estimate=COST,
        name="outs_grads",
    )(position, *inputs)


def early_back_kernel(
    position,
    d_query,
    d_kv,
    d_gate,
    query_mine,
    query_theirs,
    kv_mine,
    kv_theirs,
    ssm_mine,
    ssm_theirs,
    d_normed,
):
    here = position[0]
    half = d_normed.shape[1] // 2
    flat = ((1,), (1,))
    for which, query, kv, ssm in (
        (here, query_mine, kv_mine, ssm_mine),
        (1 - here, query_theirs, kv_theirs, ssm_theirs),
    ):
        d_normed[:, pl.ds(pl.multiple_of(which * half, half), half)] = (
            dot(d_query[...], query[...], flat)
            + dot(d_kv[...], kv[...], flat)
            + dot(d_gate[...], ssm[...], flat)
        )


def run_early_back(position, d_query, d_kv, d_gate, query, kv, ssm):
    rows = d_query.shape[0]
    half = query[0].shape[0]
    fixed = lambda shape: pl.BlockSpec(shape, lambda step, place: (0, 0))
    return pl.pallas_call(
        early_back_kernel,
        grid_spec=pltpu.PrefetchScalarGridSpec(
            num_scalar_prefetch=1,
            grid=(1,),
            in_specs=[
                *[fixed(item.shape) for item in (d_query, d_kv, d_gate, *query, *kv)],
                *[pl.BlockSpec((half, INNER), lambda step, place: (0, 1))] * 2,
            ],
            out_specs=fixed((rows, 2 * half)),
        ),
        out_shape=jax.ShapeDtypeStruct((rows, 2 * half), F32),
        compiler_params=params_of(),
        cost_estimate=COST,
        name="early_back",
    )(position, d_query, d_kv, d_gate, *query, *kv, *ssm)


def rest_grads_kernel(
    position, normed, d_query, d_kv, d_mixed, d_aux, gain_grads, d_heads, theirs, mine
):
    here = position[0]
    step = pl.program_id(0)
    half = normed.shape[1] // 2
    which = jnp.where(step == 0, 1 - here, here)
    turned = normed[:, pl.ds(pl.multiple_of(which * half, half), half)]

    def write(ref):
        at = 0
        for right in (d_query, d_kv, d_mixed):
            ref[:, at : at + right.shape[1]] = dot(turned, right[...], ((0,), (0,))).astype(BF)
            at += right.shape[1]
        gains = gain_grads[0:3, pl.ds(pl.multiple_of(which * half, half), half)]
        heads = jnp.concatenate([d_heads[0:1, :], d_heads[1:2, :]], axis=1)
        heads = jnp.concatenate([heads, jnp.zeros((1, half - heads.shape[1]), F32)], axis=1)
        before = 2 * STATE + SH
        columns = jnp.concatenate(
            [
                jnp.zeros((before, half), F32),
                gains,
                heads,
                jnp.zeros((d_aux.shape[1] - before - 4, half), F32),
            ]
        ).T
        ref[:, at:] = (dot(turned, d_aux[...], ((0,), (0,))) + columns).astype(BF)

    @pl.when(step == 0)
    def _():
        write(theirs)

    @pl.when(step == 1)
    def _():
        write(mine)


def run_rest_grads(position, *inputs):
    half = inputs[0].shape[1] // 2
    total = sum(item.shape[1] for item in inputs[1:5])
    fixed = lambda shape: pl.BlockSpec(shape, lambda step, place: (0, 0))
    return pl.pallas_call(
        rest_grads_kernel,
        grid_spec=pltpu.PrefetchScalarGridSpec(
            num_scalar_prefetch=1,
            grid=(2,),
            in_specs=[fixed(item.shape) for item in inputs],
            out_specs=[fixed((half, total))] * 2,
        ),
        out_shape=[jax.ShapeDtypeStruct((half, total), BF)] * 2,
        compiler_params=params_of(),
        cost_estimate=COST,
        name="rest_grads",
    )(position, *inputs)


def late_back_kernel(
    position,
    tokens,
    gains,
    d_middle,
    d_normed,
    d_mixed,
    d_aux,
    aux_mine,
    aux_theirs,
    ssm_mine,
    ssm_theirs,
    grad_tokens,
    total,
):
    here = position[0]
    half = tokens.shape[1] // 2
    for which, aux, ssm in ((here, aux_mine, ssm_mine), (1 - here, aux_theirs, ssm_theirs)):
        columns = pl.ds(pl.multiple_of(which * half, half), half)
        total[:, columns] = (
            d_normed[:, columns]
            + dot(d_mixed[...], ssm[...], ((1,), (1,)))
            + dot(d_aux[:, : aux.shape[0]], aux[...])
        )
    hidden = tokens[...].astype(F32)
    d_hidden, _ = norm_back(hidden, inverse_rms(hidden), gains[0:1], total[...])
    grad_tokens[...] = d_middle[...] + d_hidden


def run_late_back(position, tokens, gains, d_middle, d_normed, d_mixed, d_aux, aux, ssm):
    rows, width = tokens.shape
    half = width // 2
    fixed = lambda shape: pl.BlockSpec(shape, lambda step, place: (0, 0))
    inputs = (tokens, gains, d_middle, d_normed, d_mixed, d_aux, *aux)
    return pl.pallas_call(
        late_back_kernel,
        grid_spec=pltpu.PrefetchScalarGridSpec(
            num_scalar_prefetch=1,
            grid=(1,),
            in_specs=[
                *[fixed(item.shape) for item in inputs],
                *[pl.BlockSpec((half, INNER), lambda step, place: (0, 0))] * 2,
            ],
            out_specs=fixed((rows, width)),
            scratch_shapes=[pltpu.VMEM((rows, width), F32)],
        ),
        out_shape=jax.ShapeDtypeStruct((rows, width), F32),
        compiler_params=params_of(),
        cost_estimate=COST,
        name="late_back",
    )(position, *inputs, *ssm)


def local(
    tokens,
    cotangent,
    doc_blocks,
    gain_in,
    w_query,
    w_kv,
    w_attn_out,
    gain_attn,
    w_ssm_in,
    w_ssm_aux,
    dt_bias,
    decay_log,
    w_ssm_out,
    gain_ssm,
    gain_ff,
    w_gate,
    w_up,
    w_down,
):
    rows, width = tokens.shape
    half = width // 2
    position = lax.axis_index("shard")
    here = position.astype(jnp.int32).reshape(1)
    blocks_here = rows // BLOCK
    docs = doc_blocks[0]
    here_docs = lax.dynamic_slice_in_dim(docs, position * blocks_here, blocks_here, 0)
    prior_docs = jnp.where(position > 0, docs[:blocks_here], -1)
    earlier = jnp.concatenate([prior_docs[-1:], here_docs[:-1]])
    resets = (here_docs != earlier).astype(jnp.int32)
    key_docs = jnp.repeat(jnp.concatenate([prior_docs, here_docs]), BLOCK)
    bias = jnp.where(here_docs[:, None] == key_docs[None, :], 0.0, NEGATIVE)
    lane_pad = LANES - SH
    dt_row = jnp.pad(dt_bias, (0, lane_pad))[None]
    decay_row = jnp.pad(decay_log, (0, lane_pad))[None]

    gains = jnp.stack([gain_in, gain_attn, gain_ssm, gain_ff])
    gains_theirs = swap(gains)
    ssm_in = (w_ssm_in, swap(w_ssm_in))
    query = (w_query, swap(w_query))
    kv = (w_kv, swap(w_kv))
    aux_in = (w_ssm_aux.T, swap(w_ssm_aux.T))
    attn_out = (w_attn_out, swap(w_attn_out))
    ssm_back = (w_ssm_out, swap(w_ssm_out))
    gate = (w_gate, swap(w_gate))
    up = (w_up, swap(w_up))
    down = (w_down, swap(w_down))
    gains_all = jnp.pad(natural(gains, gains_theirs, position, 1).astype(F32), ((0, 4), (0, 0)))

    normed, scaled_queries, key_vals, aux, mixed, state_end = run_project(
        here, resets, tokens, gains_all, dt_row, decay_row, query, kv, aux_in, ssm_in
    )
    key_prior = lax.ppermute(key_vals, "shard", [(0, 1)])
    state_prior = lax.ppermute(state_end, "shard", [(0, 1)])
    attended, log_total = run_attend(scaled_queries, key_prior, key_vals, bias)
    ssm_out, gated, states = run_forward(resets, mixed, aux, dt_row, decay_row, state_prior)

    (
        output,
        d_middle,
        d_attn_low,
        d_ssm_low,
        d_attended,
        d_gated,
        gain_grads,
        down_theirs,
        down_mine,
        wide_theirs,
        wide_mine,
    ) = run_middle(
        here, tokens, attended, gated, cotangent, gains_all, attn_out, ssm_back, gate, up, down
    )
    sums = {
        "down": Stream([down_mine, swap(down_theirs)], WHOLE["down"], *LINKS["down"]),
        "wide": Stream([wide_mine, swap(wide_theirs)], WHOLE["wide"], *LINKS["wide"]),
    }
    token = wide_theirs
    made = {}
    outs_rows = w_attn_out.shape[0]
    full = lambda *shape: jax.ShapeDtypeStruct(shape, F32)
    ssm_pieces = w_ssm_out.shape[0] // outs_rows
    gate_at = width * (1 + ssm_pieces)
    aux_at = AUX_AT + INNER
    spare = aux_at + 2 * STATE + SH
    wide_pieces = [
        [
            (column, 2 * column + offset, 2 * column + offset + CHUNK)
            for column in range(0, w_gate.shape[1], CHUNK)
        ]
        for offset in (0, CHUNK)
    ]
    layouts = {
        "down": [(full(*w_down.shape), width, [(0, 0, width)])],
        "wide": [(full(half, w_gate.shape[1]), w_gate.shape[1], pieces) for pieces in wide_pieces],
        "outs": [
            (full(outs_rows, width), width, [(0, 0, width)]),
            (
                full(ssm_pieces, outs_rows, width),
                width,
                [(piece, width * (1 + piece), width * (2 + piece)) for piece in range(ssm_pieces)],
            ),
            (
                full(half // outs_rows, outs_rows, 2 * INNER),
                INNER,
                [
                    (piece, gate_at + INNER * piece, gate_at + INNER * (piece + 1))
                    for piece in range(half // outs_rows)
                ],
            ),
        ],
        "rest": [
            (full(half, KV_AT), KV_AT, [(0, 0, KV_AT)]),
            (full(half, AUX_AT - KV_AT), AUX_AT - KV_AT, [(0, KV_AT, AUX_AT)]),
            (full(spare - aux_at, half), 3 * LANES, [(TURNED, aux_at, spare)]),
            (full(8, half), 3 * LANES, [(TURNED, spare, spare + 8)]),
            (full(half, 2 * INNER), INNER, [(0, AUX_AT, aux_at)]),
        ],
    }
    def closed(value, number):
        if number + 1 == len(PLAN) or PLAN[number + 1] not in layouts:
            return value
        names = []
        for name in PLAN[number + 1 :]:
            if name not in layouts:
                break
            names.append(name)
        waits = [
            stream.latest()
            for name, stream in sums.items()
            if stream.steps
            and (name in names or stream.gone > 1 or (stream.gone == 1 and name == "down"))
        ]
        return fence(value, *waits)

    d_kv = None

    def key_grads(made_before):
        if made_before is not None:
            return made_before
        return (d_here + after(d_prior_got, token).astype(F32)).astype(BF)

    def go_on(name):
        nonlocal token
        stream = sums[name]
        stream.hold(token)
        if stream.steps:
            stream.prepare()
            token = stream.operand
            stream.go()
        elif name not in made:
            started = made["outs"][2].reshape(half, 2 * INNER) if name == "rest" else None
            weights = (w_query, w_kv, w_ssm_aux.T, None, w_ssm_in) if name == "rest" else ()
            made[name] = stream.finish(layouts[name], started, weights)
            token = made[name][0]

    for number, name in enumerate(PLAN):
        if name in layouts:
            go_on(name)
        elif name == "state":
            d_state_start, d_mixed_gate = run_state_back(
                resets, after(d_gated, token), mixed, aux, ssm_out, dt_row, decay_row
            )
            token = closed(d_state_start, number)
            d_state_end = lax.ppermute(token, "shard", [(1, 0)])
        elif name == "grads":
            outs_theirs, outs_mine = run_outs_grads(
                here, after(attended, token), gated, normed, d_attn_low, d_ssm_low, d_mixed_gate
            )
            token = closed(outs_theirs, number)
            sums["outs"] = Stream([outs_mine, swap(token)], WHOLE["outs"], *LINKS["outs"])
        elif name == "attend":
            d_query, d_prior, d_here = run_attend_back(
                scaled_queries, key_prior, key_vals, bias, log_total, after(d_attended, token)
            )
            token = closed(d_prior, number)
            d_prior_got = lax.ppermute(token, "shard", [(1, 0)])
        elif name == "scan":
            d_mixed, d_aux, d_heads = run_backward(
                resets,
                after(d_gated, token),
                mixed,
                aux,
                ssm_out,
                states,
                dt_row,
                decay_row,
                d_state_end,
            )
            token = d_heads = closed(d_heads, number)
        elif name == "sums":
            d_kv = key_grads(d_kv)
            rest_theirs, rest_mine = run_rest_grads(
                here, normed, d_query, d_kv, d_mixed, d_aux, gain_grads, d_heads
            )
            token = closed(rest_theirs, number)
            sums["rest"] = Stream([rest_mine, swap(token)], WHOLE["rest"], *LINKS["rest"])
        elif name == "early":
            d_kv = key_grads(d_kv)
            d_normed = run_early_back(
                here, after(d_query, token), d_kv, d_mixed_gate, query, kv, ssm_in
            )
            token = d_normed
        elif name == "late":
            grad_tokens = run_late_back(
                here,
                tokens,
                gains_all,
                d_middle,
                d_normed,
                d_mixed,
                after(d_aux, token),
                aux_in,
                ssm_in,
            )
            token = grad_tokens

    for name in layouts:
        while name not in made:
            go_on(name)
    (grad_down,) = made["down"]
    grad_gate, grad_up = made["wide"]
    grad_attn_out, grad_ssm_out, _ = made["outs"]
    grad_query, grad_kv, grad_aux, extras, grad_ssm_in, products = made["rest"]
    gate_products = jnp.sum(
        w_ssm_in[:, INNER:].astype(F32) * made["outs"][2].reshape(half, 2 * INNER)[:, INNER:], axis=1
    )
    grad_gain_in = (products[0] + gate_products) / gain_in.astype(F32)
    return (
        output,
        grad_tokens,
        grad_gain_in,
        grad_query,
        grad_kv,
        grad_attn_out,
        extras[0],
        grad_ssm_in,
        grad_aux.T,
        extras[3, :SH],
        extras[3, LANES : LANES + SH],
        grad_ssm_out.reshape(w_ssm_out.shape),
        extras[1],
        extras[2],
        grad_gate,
        grad_up,
        grad_down,
    )


def solution(mesh):
    halves = P("shard", None)
    half = P("shard")
    tokens = P(("rep", "shard"), None)
    return jax.shard_map(
        local,
        mesh=mesh,
        in_specs=(
            tokens,
            tokens,
            P("rep", None),
            half,
            halves,
            halves,
            halves,
            half,
            halves,
            halves,
            P(),
            P(),
            halves,
            half,
            half,
            halves,
            halves,
            halves,
        ),
        out_specs=(
            tokens,
            tokens,
            half,
            halves,
            halves,
            halves,
            half,
            halves,
            halves,
            P(),
            P(),
            halves,
            half,
            half,
            halves,
            halves,
            halves,
        ),
        check_vma=False,
    )
```

```python
import functools

import jax
import jax.numpy as jnp
from jax import lax
from jax.experimental import pallas as pl
from jax.experimental.pallas import tpu as pltpu
from jax.sharding import PartitionSpec as P

HD = 64
QH = 8
KVH = 2
SH = 24
SP = 64
STATE = 128
BLOCK = 128
INNER = 1536
LANES = 128
KV_AT = QH * HD
X, Y, Z, ZZ = 0, 1, 2, 3
TURNED = -1
WHOLE = {"down": 2, "wide": 1, "outs": 1, "rest": 2}
LINKS = {
    "down": ((Z, Y, ZZ, X), (Z, X, Y, ZZ)),
    "wide": ((X, Y, ZZ, Z), (Y, X, Z, ZZ)),
    "outs": ((Z, Y, X, ZZ), (Y, X, Z, ZZ)),
    "rest": ((X, Z, Y, ZZ), (Y, X, Z, ZZ)),
}
PLAN = (
    "state",
    "wide",
    "down",
    "grads",
    "scan",
    "wide",
    "down",
    "outs",
    "attend",
    "wide",
    "sums",
    "early",
    "down",
    "outs",
    "wide",
    "rest",
    "down",
    "outs",
    "wide",
    "rest",
    "down",
    "outs",
    "wide",
    "rest",
    "down",
    "outs",
    "wide",
    "rest",
    "down",
    "outs",
    "late",
    "wide",
    "rest",
    "outs",
    "rest",
    "outs",
    "rest",
)
AUX_AT = KV_AT + 2 * KVH * HD
EPSILON = 1e-05
NEGATIVE = -1e30
BF = jnp.bfloat16
F32 = jnp.float32
SWAP = [(0, 1), (1, 0)]
VMEM_LIMIT = 30 * 1024 * 1024
LARGE_LIMIT = 50 * 1024 * 1024
WHOLE_LIMIT = 60 * 1024 * 1024
LONG = pl.CostEstimate(flops=15_000_000_000, bytes_accessed=1_000_000, transcendentals=0)
COST = pl.CostEstimate(flops=1_000_000, bytes_accessed=1_000_000, transcendentals=0)


def dot(left, right, over=((1,), (0,))):
    return lax.dot_general(left, right, (over, ((), ())), preferred_element_type=F32)


def split2(value):
    high = value.astype(BF)
    return high, (value - high.astype(F32)).astype(BF)


def split3(value):
    high = value.astype(BF)
    rest = value - high.astype(F32)
    middle = rest.astype(BF)
    return high, middle, (rest - middle.astype(F32)).astype(BF)


def dot3(left, right, over=((1,), (0,))):
    left_high, left_low = split2(left)
    right_high, right_low = split2(right)
    return dot(left_high, right_high, over) + (
        dot(left_high, right_low, over) + dot(left_low, right_high, over)
    )


def dot1(left, right, over=((1,), (0,))):
    return dot(left.astype(BF), right.astype(BF), over)


def spread(value, begin=0, end=SH):
    first_half = lax.broadcasted_iota(jnp.int32, (value.shape[0], LANES), 1) < SP
    return jnp.concatenate(
        [
            jnp.where(first_half, value[:, head : head + 1], value[:, head + 1 : head + 2])
            for head in range(begin, end, 2)
        ],
        axis=1,
    )


def gather_heads(*values):
    parts = [part for value in values for part in split2(value)]
    sums = dot(jnp.concatenate(parts), head_ones(), ((1,), (1,)))
    found, row = [], 0
    for value in values:
        rows = value.shape[0]
        found.append(sums[row : row + rows] + sums[row + rows : row + 2 * rows])
        row += 2 * rows
    return found


def head_ones():
    head = lax.broadcasted_iota(jnp.int32, (LANES, INNER), 0)
    column = lax.broadcasted_iota(jnp.int32, (LANES, INNER), 1)
    return ((column >= head * SP) & (column < (head + 1) * SP)).astype(BF)


def lower_ones():
    rows = lax.broadcasted_iota(jnp.int32, (BLOCK, BLOCK), 0)
    columns = lax.broadcasted_iota(jnp.int32, (BLOCK, BLOCK), 1)
    return rows >= columns


def cumulate(value, lower, over):
    high, middle, low = split3(value)
    return dot(lower, high, over) + (dot(lower, middle, over) + dot(lower, low, over))


def decays(aux, dt_bias, rate):
    raw = aux[:, 2 * STATE :] + dt_bias
    step = jnp.maximum(raw, 0.0) + jnp.log1p(jnp.exp(-jnp.abs(raw)))
    log_decay = -step * rate
    cumulated = cumulate(log_decay, lower_ones().astype(BF), ((1,), (0,)))
    return raw, step, log_decay, cumulated


def forward_kernel(
    resets, mixed, gate, aux, dt_bias, decay_log, state_in, ssm_out, gated, states, state
):
    number = pl.program_id(0)

    @pl.when(number == 0)
    def _():
        state[...] = state_in[...]

    @pl.when(resets[number] != 0)
    def _():
        state[...] = jnp.zeros_like(state)

    aux_now = aux[...]
    b_in = aux_now[:, :STATE]
    c_out = aux_now[:, STATE : 2 * STATE]
    _, step, _, cumulated = decays(aux_now, dt_bias[...], jnp.exp(decay_log[...]))
    scaled = mixed[...].astype(F32) * spread(step)
    wide = spread(cumulated)
    tail = jnp.exp(wide[BLOCK - 1 :, :] - wide)
    grown = jnp.exp(wide)
    before = state[...]
    states[...] = before[None].astype(BF)
    state[...] = grown[BLOCK - 1 :, :] * before + dot1(b_in, scaled * tail, ((0,), (0,)))
    outer = grown * dot1(c_out, before)
    both = dot3(c_out, b_in, ((1,), (1,)))
    lower = lower_ones()
    flipped = cumulated.T
    first_half = lax.broadcasted_iota(jnp.int32, (BLOCK, LANES), 1) < SP
    scaled_low = scaled.astype(BF)
    zero = jnp.zeros((BLOCK, LANES), BF)
    for pair in range(SH // 2):
        weights = []
        for head in (2 * pair, 2 * pair + 1):
            spread_now = cumulated[:, head : head + 1] - flipped[head : head + 1, :]
            weights.append((jnp.exp(jnp.where(lower, spread_now, NEGATIVE)) * both).astype(BF))
        columns = slice(pair * LANES, (pair + 1) * LANES)
        low = scaled_low[:, columns]
        low = jnp.concatenate([jnp.where(first_half, low, zero), jnp.where(first_half, zero, low)])
        inner = dot(jnp.concatenate(weights, axis=1), low)
        total = inner + outer[:, columns]
        ssm_out[:, columns] = total
        gate_now = gate[:, columns].astype(F32)
        gated[:, columns] = (total * (gate_now / (1.0 + jnp.exp(-gate_now)))).astype(BF)


def silu_of(gate):
    chance = 1.0 / (1.0 + jnp.exp(-gate))
    return gate * chance, chance


def state_back_kernel(
    resets, d_gated, gate, aux, ssm_out, dt_bias, decay_log, d_state_out, d_gate, d_state
):
    number = pl.num_programs(0) - 1 - pl.program_id(0)

    @pl.when(pl.program_id(0) == 0)
    def _():
        d_state[...] = jnp.zeros_like(d_state)

    aux_now = aux[...]
    _, _, _, cumulated = decays(aux_now, dt_bias[...], jnp.exp(decay_log[...]))
    grown = spread(jnp.exp(cumulated))
    gate_silu, chance = silu_of(gate[...].astype(F32))
    d_gated_now = d_gated[...].astype(F32)
    d_gate[...] = (d_gated_now * ssm_out[...] * (chance + gate_silu * (1.0 - chance))).astype(BF)
    d_grown = d_gated_now * gate_silu * grown
    c_out = aux_now[:, STATE : 2 * STATE]
    d_state[...] = grown[BLOCK - 1 :, :] * d_state[...] + dot1(c_out, d_grown, ((0,), (0,)))

    @pl.when(resets[number] != 0)
    def _():
        d_state[...] = jnp.zeros_like(d_state)

    d_state_out[...] = d_state[...].astype(BF)


def backward_kernel(
    resets,
    d_gated,
    mixed,
    gate,
    aux,
    ssm_out,
    states,
    dt_bias,
    decay_log,
    d_state_in,
    d_mixed,
    d_aux,
    d_heads,
    d_state,
):
    number = pl.num_programs(0) - 1 - pl.program_id(0)

    @pl.when(pl.program_id(0) == 0)
    def _():
        d_state[...] = d_state_in[...].astype(F32)
        d_heads[...] = jnp.zeros_like(d_heads)

    lower = lower_ones()
    aux_now = aux[...]
    b_in = aux_now[:, :STATE]
    c_out = aux_now[:, STATE : 2 * STATE]
    rate = jnp.exp(decay_log[...])
    raw, step, log_decay, cumulated = decays(aux_now, dt_bias[...], rate)
    step_wide = spread(step)
    mixed_now = mixed[...].astype(F32)
    scaled = mixed_now * step_wide
    wide = spread(cumulated)
    tail = jnp.exp(wide[BLOCK - 1 :, :] - wide)
    grown = jnp.exp(wide)
    gate_now = gate[...].astype(F32)
    gate_silu, _ = silu_of(gate_now)
    d_gated_now = d_gated[...].astype(F32)
    ssm_now = ssm_out[...]
    d_out = d_gated_now * gate_silu
    before = states[0].astype(F32)
    d_after = d_state[...]
    d_grown = d_out * grown
    d_c = dot1(d_grown, before, ((1,), (1,)))
    d_before = grown[BLOCK - 1 :, :] * d_after + dot1(c_out, d_grown, ((0,), (0,)))
    tailed = scaled * tail
    d_b = dot1(tailed, d_after, ((1,), (1,)))
    d_tailed = dot1(b_in, d_after)
    ends = jnp.sum(tailed * d_tailed, axis=0, keepdims=True) + grown[BLOCK - 1 :, :] * jnp.sum(
        d_after * before, axis=0, keepdims=True
    )
    both = dot3(c_out, b_in, ((1,), (1,)))
    flipped = cumulated.T
    first_half = lax.broadcasted_iota(jnp.int32, (BLOCK, LANES), 1) < SP
    scaled_low = scaled.astype(BF)
    d_low = d_out.astype(BF)
    zero = jnp.zeros((BLOCK, LANES), BF)
    d_both = jnp.zeros((BLOCK, BLOCK), F32)
    parts = []
    for pair in range(SH // 2):
        columns = slice(pair * LANES, (pair + 1) * LANES)
        falls = []
        for head in (2 * pair, 2 * pair + 1):
            spread_now = cumulated[:, head : head + 1] - flipped[head : head + 1, :]
            falls.append(jnp.exp(jnp.where(lower, spread_now, NEGATIVE)))
        weight = jnp.concatenate([(falls[0] * both).astype(BF), (falls[1] * both).astype(BF)])
        low = d_low[:, columns]
        low = jnp.concatenate([jnp.where(first_half, low, zero), jnp.where(first_half, zero, low)])
        d_weight = dot(low, scaled_low[:, columns], ((1,), (1,)))
        d_both = d_both + falls[0] * d_weight[:BLOCK] + falls[1] * d_weight[BLOCK:]
        parts.append(dot(weight, low, ((0,), (0,))))
    d_inner = jnp.concatenate(parts, axis=1)
    carried = tail * d_tailed
    d_scaled = d_inner + carried
    d_mixed[...] = (d_scaled * step_wide).astype(BF)
    d_step, d_cumulated, d_last = gather_heads(
        d_scaled * mixed_now,
        d_low.astype(F32) * ssm_now - scaled_low.astype(F32) * d_inner - scaled * carried,
        jnp.broadcast_to(ends, (8, INNER)),
    )
    d_decay = cumulate(d_cumulated, lower.astype(BF), ((0,), (0,))) + d_last[:1]
    d_raw = (d_step - d_decay * rate) * (1.0 / (1.0 + jnp.exp(-raw)))
    real = lax.broadcasted_iota(jnp.int32, (BLOCK, LANES), 1) < SH
    d_raw = jnp.where(real, d_raw, 0.0)
    d_c = d_c + dot1(d_both, b_in)
    d_b = d_b + dot1(d_both, c_out, ((0,), (0,)))
    d_aux[...] = jnp.concatenate([d_b, d_c, d_raw], axis=1).astype(BF)
    d_heads[...] += jnp.concatenate(
        [
            jnp.sum(d_raw, axis=0, keepdims=True),
            jnp.sum(jnp.where(real, d_decay * log_decay, 0.0), axis=0, keepdims=True),
            jnp.zeros((6, LANES), F32),
        ]
    )
    d_state[...] = d_before

    @pl.when(resets[number] != 0)
    def _():
        d_state[...] = jnp.zeros_like(d_state)


def scalars():
    return pl.BlockSpec(memory_space=pltpu.SMEM)


def whole(shape):
    return pl.BlockSpec(shape, lambda number: (0,) * len(shape))


def params_of(limit=VMEM_LIMIT):
    return pltpu.CompilerParams(dimension_semantics=("arbitrary",), vmem_limit_bytes=limit)


def run_forward(resets, mixed, aux, dt_bias, decay_log, state_in):
    rows = mixed.shape[0]
    count = rows // BLOCK
    return pl.pallas_call(
        forward_kernel,
        grid=(count,),
        in_specs=[
            scalars(),
            pl.BlockSpec((BLOCK, INNER), lambda number: (number, 0)),
            pl.BlockSpec((BLOCK, INNER), lambda number: (number, 1)),
            pl.BlockSpec((BLOCK, 3 * LANES), lambda number: (number, 0)),
            whole((1, LANES)),
            whole((1, LANES)),
            whole((STATE, INNER)),
        ],
        out_specs=[
            pl.BlockSpec((BLOCK, INNER), lambda number: (number, 0)),
            pl.BlockSpec((BLOCK, INNER), lambda number: (number, 0)),
            pl.BlockSpec((1, STATE, INNER), lambda number: (number, 0, 0)),
        ],
        out_shape=[
            jax.ShapeDtypeStruct((rows, INNER), F32),
            jax.ShapeDtypeStruct((rows, INNER), BF),
            jax.ShapeDtypeStruct((count, STATE, INNER), BF),
        ],
        scratch_shapes=[pltpu.VMEM((STATE, INNER), F32)],
        compiler_params=params_of(),
        cost_estimate=LONG,
        name="ssm_forward",
    )(resets, mixed, mixed, aux, dt_bias, decay_log, state_in)


def run_state_back(resets, d_gated, mixed, aux, ssm_out, dt_bias, decay_log):
    count = mixed.shape[0] // BLOCK
    turned = lambda number: (count - 1 - number, 0)
    return pl.pallas_call(
        state_back_kernel,
        grid=(count,),
        in_specs=[
            scalars(),
            pl.BlockSpec((BLOCK, INNER), turned),
            pl.BlockSpec((BLOCK, INNER), lambda number: (count - 1 - number, 1)),
            pl.BlockSpec((BLOCK, 3 * LANES), turned),
            pl.BlockSpec((BLOCK, INNER), turned),
            whole((1, LANES)),
            whole((1, LANES)),
        ],
        out_specs=[whole((STATE, INNER)), pl.BlockSpec((BLOCK, INNER), turned)],
        out_shape=[
            jax.ShapeDtypeStruct((STATE, INNER), BF),
            jax.ShapeDtypeStruct((mixed.shape[0], INNER), BF),
        ],
        scratch_shapes=[pltpu.VMEM((STATE, INNER), F32)],
        compiler_params=params_of(WHOLE_LIMIT),
        cost_estimate=COST,
        name="ssm_state_back",
    )(resets, d_gated, mixed, aux, ssm_out, dt_bias, decay_log)


def run_backward(resets, d_gated, mixed, aux, ssm_out, states, dt_bias, decay_log, d_state_in):
    rows = mixed.shape[0]
    count = rows // BLOCK
    turned = lambda number: (count - 1 - number, 0)
    return pl.pallas_call(
        backward_kernel,
        grid=(count,),
        in_specs=[
            scalars(),
            pl.BlockSpec((BLOCK, INNER), turned),
            pl.BlockSpec((BLOCK, INNER), turned),
            pl.BlockSpec((BLOCK, INNER), lambda number: (count - 1 - number, 1)),
            pl.BlockSpec((BLOCK, 3 * LANES), turned),
            pl.BlockSpec((BLOCK, INNER), turned),
            pl.BlockSpec((1, STATE, INNER), lambda number: (count - 1 - number, 0, 0)),
            whole((1, LANES)),
            whole((1, LANES)),
            whole((STATE, INNER)),
        ],
        out_specs=[
            pl.BlockSpec((BLOCK, INNER), turned),
            pl.BlockSpec((BLOCK, 3 * LANES), turned),
            whole((8, LANES)),
        ],
        out_shape=[
            jax.ShapeDtypeStruct((rows, INNER), BF),
            jax.ShapeDtypeStruct((rows, 3 * LANES), BF),
            jax.ShapeDtypeStruct((8, LANES), F32),
        ],
        scratch_shapes=[pltpu.VMEM((STATE, INNER), F32)],
        compiler_params=params_of(),
        cost_estimate=COST,
        name="ssm_backward",
    )(resets, d_gated, mixed, mixed, aux, ssm_out, states, dt_bias, decay_log, d_state_in)


def head_rows(ref, start, group, width):
    return jnp.concatenate(
        [
            ref[start : start + BLOCK, (group * width + head) * HD : (group * width + head + 1) * HD]
            for head in range(width)
        ]
    )


def masked_scores(q_rows, k_rows, bias_row, lower, width):
    raw = dot(q_rows, k_rows, ((1,), (1,))) + bias_row
    edge = raw.shape[1] - BLOCK
    corner = jnp.where(jnp.concatenate([lower] * width), raw[:, edge:], NEGATIVE)
    return jnp.concatenate([raw[:, :edge], corner], axis=1)


def attend_kernel(q_ref, prior_ref, here_ref, bias_ref, out_ref, total_ref):
    width = QH // KVH
    rows = q_ref.shape[0]
    halo = prior_ref.shape[0]
    lower = lower_ones()
    for group in range(KVH):
        key_columns = slice(group * HD, (group + 1) * HD)
        value_columns = slice((KVH + group) * HD, (KVH + group + 1) * HD)
        keys = jnp.concatenate([prior_ref[:, key_columns], here_ref[:, key_columns]])
        values = jnp.concatenate([prior_ref[:, value_columns], here_ref[:, value_columns]])
        for block in range(rows // BLOCK):
            start = block * BLOCK
            reach = halo + start + BLOCK
            q_rows = head_rows(q_ref, start, group, width)
            scores = masked_scores(
                q_rows, keys[:reach], bias_ref[block : block + 1, :reach], lower, width
            )
            top = jnp.max(scores, axis=1, keepdims=True)
            powers = jnp.exp(scores - top)
            total = jnp.sum(powers, axis=1, keepdims=True)
            probs = (powers * (1.0 / total)).astype(BF)
            out = dot(probs, values[:reach])
            log_total = top + jnp.log(total)
            for head in range(width):
                place = group * width + head
                some = slice(head * BLOCK, (head + 1) * BLOCK)
                out_ref[start : start + BLOCK, place * HD : (place + 1) * HD] = out[some].astype(BF)
                total_ref[start : start + BLOCK, place : place + 1] = log_total[some]


def attend_back_kernel(
    q_ref, prior_ref, here_ref, bias_ref, total_ref, d_ref, dq_ref, d_prior_ref, d_here_ref, sums
):
    width = QH // KVH
    rows = q_ref.shape[0]
    halo = prior_ref.shape[0]
    lower = lower_ones()
    sums[...] = jnp.zeros_like(sums)
    for group in range(KVH):
        key_columns = slice(group * HD, (group + 1) * HD)
        value_columns = slice((KVH + group) * HD, (KVH + group + 1) * HD)
        keys = jnp.concatenate([prior_ref[:, key_columns], here_ref[:, key_columns]])
        values = jnp.concatenate([prior_ref[:, value_columns], here_ref[:, value_columns]])
        for block in range(rows // BLOCK):
            start = block * BLOCK
            reach = halo + start + BLOCK
            q_rows = head_rows(q_ref, start, group, width)
            d_rows = head_rows(d_ref, start, group, width)
            scores = masked_scores(
                q_rows, keys[:reach], bias_ref[block : block + 1, :reach], lower, width
            )
            log_total = jnp.concatenate(
                [
                    total_ref[start : start + BLOCK, group * width + head : group * width + head + 1]
                    for head in range(width)
                ]
            )
            probs = jnp.exp(scores - log_total)
            probs_low = probs.astype(BF)
            d_probs = dot(d_rows, values[:reach], ((1,), (1,)))
            weighed = probs * d_probs
            d_scores = (weighed - probs * jnp.sum(weighed, axis=1, keepdims=True)).astype(BF)
            d_queries = dot(d_scores, keys[:reach]) * HD**-0.5
            for head in range(width):
                place = group * width + head
                some = slice(head * BLOCK, (head + 1) * BLOCK)
                dq_ref[start : start + BLOCK, place * HD : (place + 1) * HD] = d_queries[some].astype(BF)
            sums[:reach, key_columns] += dot(d_scores, q_rows, ((0,), (0,)))
            sums[:reach, value_columns] += dot(probs_low, d_rows, ((0,), (0,)))
    d_prior_ref[...] = sums[:halo].astype(BF)
    d_here_ref[...] = sums[halo:]


def run_attend(queries, prior, here, bias):
    rows = queries.shape[0]
    return pl.pallas_call(
        attend_kernel,
        out_shape=[
            jax.ShapeDtypeStruct((rows, QH * HD), BF),
            jax.ShapeDtypeStruct((rows, QH), F32),
        ],
        compiler_params=pltpu.CompilerParams(vmem_limit_bytes=VMEM_LIMIT),
        cost_estimate=LONG,
        name="attend",
    )(queries, prior, here, bias)


def run_attend_back(queries, prior, here, bias, log_total, d_attended):
    rows = queries.shape[0]
    halo = prior.shape[0]
    return pl.pallas_call(
        attend_back_kernel,
        out_shape=[
            jax.ShapeDtypeStruct((rows, QH * HD), BF),
            jax.ShapeDtypeStruct((halo, 2 * KVH * HD), BF),
            jax.ShapeDtypeStruct((rows, 2 * KVH * HD), F32),
        ],
        scratch_shapes=[pltpu.VMEM((halo + rows, 2 * KVH * HD), F32)],
        compiler_params=pltpu.CompilerParams(vmem_limit_bytes=VMEM_LIMIT),
        cost_estimate=COST,
        name="attend_back",
    )(queries, prior, here, bias, log_total, d_attended)


def swap(value):
    return lax.ppermute(value, "shard", SWAP)


def natural(mine, theirs, position, axis):
    return jnp.where(
        position == 0,
        jnp.concatenate([mine, theirs], axis=axis),
        jnp.concatenate([theirs, mine], axis=axis),
    )


def half_of(value, which, axis):
    size = value.shape[axis] // 2
    return lax.dynamic_slice_in_dim(value, which * size, size, axis)


class Stream:
    def __init__(self, terms, whole, *orders):
        self.terms = terms
        self.count = lax.axis_size("rep")
        self.bits = self.count.bit_length() - 1
        self.stack = None
        self.got = None
        self.gone = 0
        if self.count != 1 << self.bits:
            self.stack = lax.psum(self.part(0, terms[0].shape[0]), "rep")
            self.bits = 0
        places = range(self.bits)
        self.orders = [
            [bit for bit in order if bit < self.bits] + [bit for bit in places if bit not in order]
            for order in orders
        ]
        rep, core = lax.axis_index("rep"), lax.axis_index("shard")
        self.cuts = max(0, self.bits - whole)
        self.sides = [
            jnp.where(core == 0, (rep >> first) & 1, (rep >> second) & 1)
            for first, second in zip(*self.orders)
        ][: self.cuts]
        self.steps = [("scatter", step) for step in places[: self.cuts]]
        self.steps += [("exchange", step) for step in places[self.cuts :]]
        self.steps += [("gather", step) for step in reversed(places[: self.cuts])]

    def pairs(self, step):
        return [
            (rep * 2 + core, (rep ^ (1 << self.orders[core][step])) * 2 + core)
            for rep in range(self.count)
            for core in range(2)
        ]

    def part(self, start, size):
        total = lax.dynamic_slice_in_dim(self.terms[0], start, size, 0).astype(F32)
        for term in self.terms[1:]:
            total = total + lax.dynamic_slice_in_dim(term, start, size, 0).astype(F32)
        return total.astype(BF)

    def latest(self):
        if self.got is not None:
            return self.got
        return self.terms[-1] if self.stack is None else self.stack

    def hold(self, token):
        if self.got is not None:
            self.got = after(self.got, token)
        elif self.stack is None:
            self.terms[-1] = after(self.terms[-1], token)

    def prepare(self):
        kind, step = self.steps[0]
        if kind == "gather":
            if self.stack is None:
                self.stack = self.part(0, self.terms[0].shape[0])
            else:
                self.stack = jnp.concatenate([self.stack, self.got])
            self.operand = self.stack
        elif kind == "exchange":
            self.operand = self.part(0, self.terms[0].shape[0])
        else:
            size = self.terms[0].shape[0] // 2
            self.operand = self.part((1 - self.sides[step]) * size, size)

    def go(self):
        kind, step = self.steps.pop(0)
        self.gone += 1
        got = lax.ppermute(self.operand, ("rep", "shard"), self.pairs(step))
        if kind == "gather":
            self.got = got
        elif kind == "exchange":
            self.terms = [self.operand, got]
        else:
            size = self.terms[0].shape[0] // 2
            self.terms = [
                lax.dynamic_slice_in_dim(term, self.sides[step] * size, size, 0)
                for term in self.terms
            ] + [got]

    def own(self):
        block = jnp.zeros((), jnp.int32)
        for side in self.sides:
            block = 2 * block + side
        return block.astype(jnp.int32)

    def finish(self, outputs, started=None, weights=(), part=None, before=()):
        if self.stack is None:
            self.stack = self.part(0, self.terms[0].shape[0])
        stacks = [self.stack] if self.got is None else [self.stack, self.got]
        blocks = 1 << self.cuts
        far = max(1, blocks // 4)
        quarters = blocks // far
        each = quarters // len(stacks)
        size = stacks[0].shape[0] // each // far
        width = stacks[0].shape[1]
        own = self.own()
        numbers = jnp.arange(quarters, dtype=jnp.int32)
        if part is not None:
            if size % 16:
                return None
            stacks = stacks[part : part + 1]
            numbers = numbers[each * part : each * (part + 1)]
        if size % 16:
            flat = jnp.concatenate(stacks).reshape(blocks, size, width)
            flat = jnp.zeros_like(flat).at[jnp.arange(blocks) ^ own].set(flat).reshape(-1, width)
            made = []
            for shape, _, pieces in outputs:
                cuts = [flat[:, begin:end].astype(F32) for _, begin, end in pieces]
                if pieces[0][0] == TURNED:
                    made.append(cuts[0].T)
                    continue
                value = jnp.stack(cuts) if len(shape.shape) == 3 else jnp.concatenate(cuts, axis=1)
                made.append(value)
            products = [
                jnp.sum(
                    value * weight[:, : value.shape[1]].astype(F32),
                    axis=0 if pieces[0][0] == TURNED else 1,
                )
                for value, weight, (_, _, pieces) in zip(made, weights, outputs)
                if weight is not None
            ]
            spare = outputs[-1][0].shape[-1] - made[-1].shape[-1]
            if spare:
                left = made[-1].ndim == 3
                other = jnp.zeros(made[-1].shape[:-1] + (spare,), F32)
                if started is not None:
                    other = started[..., :spare] if left else started[..., -spare:]
                made[-1] = jnp.concatenate([other, made[-1]] if left else [made[-1], other], axis=-1)
            if products:
                made.append(jnp.broadcast_to(sum(products), (8, products[0].shape[0])))
            return made
        rows = far * size
        in_specs = [
            pl.BlockSpec((rows, width), lambda step, places: (jnp.minimum(step, each - 1), 0))
        ]
        if len(stacks) == 2:
            in_specs.append(
                pl.BlockSpec((rows, width), lambda step, places: (jnp.maximum(step - each, 0), 0))
            )
        out_specs = []
        scratch = []
        for shape, block, pieces in outputs:
            if pieces[0][0] == TURNED:
                out_specs.append(
                    pl.BlockSpec((shape.shape[0], rows), lambda step, places: (0, places[step]))
                )
                scratch = [pltpu.VMEM((rows, block), F32)]
            elif len(shape.shape) == 3:
                last = shape.shape[2] // block - 1
                out_specs.append(
                    pl.BlockSpec(
                        (shape.shape[0], rows, block),
                        lambda step, places, last=last: (0, places[step], last),
                    )
                )
            else:
                out_specs.append(pl.BlockSpec((rows, block), lambda step, places: (places[step], 0)))
        inputs = list(stacks)
        shapes = [shape for shape, _, _ in outputs]
        for weight, (_, block, pieces) in zip(weights, outputs):
            if weight is None:
                continue
            inputs.append(weight)
            if pieces[0][0] == TURNED:
                in_specs.append(
                    pl.BlockSpec((weight.shape[0], rows), lambda step, places: (0, places[step]))
                )
            else:
                in_specs.append(pl.BlockSpec((rows, block), lambda step, places: (places[step], 0)))
        if weights:
            out_specs.append(pl.BlockSpec((8, rows), lambda step, places: (0, places[step])))
            shapes.append(jax.ShapeDtypeStruct((8, rows * quarters), F32))
        aliases = {}
        if part != 1 and started is not None:
            before = [started]
            aliases = {1 + len(inputs): len(outputs) - 1}
        elif part == 1:
            aliases = {1 + len(inputs) + number: number for number in range(len(shapes))}
        inputs += before
        in_specs += [pl.BlockSpec(memory_space=pl.ANY)] * len(before)
        places = jnp.concatenate([numbers ^ (own // far), (own % far).reshape(1)])
        return pl.pallas_call(
            functools.partial(
                finish_kernel,
                len(stacks),
                far,
                [cut for _, _, cut in outputs],
                [weight is not None for weight in weights],
            ),
            grid_spec=pltpu.PrefetchScalarGridSpec(
                num_scalar_prefetch=1,
                grid=numbers.shape,
                in_specs=in_specs,
                out_specs=out_specs,
                scratch_shapes=scratch,
            ),
            out_shape=shapes,
            input_output_aliases=aliases,
            compiler_params=params_of(),
            cost_estimate=COST,
            name="unpack",
        )(places, *inputs)


def finish_kernel(count, far, layout, weighed, places, *refs):
    turned = any(pieces[0][0] == TURNED for pieces in layout)
    if turned:
        held, refs = refs[-1], refs[:-1]
    if any(weighed):
        products, refs = refs[-1], refs[:-1]
    outputs = refs[-len(layout) :]
    weights = list(refs[count : count + sum(weighed)])
    steps = pl.num_programs(0)
    within = places[steps]
    size = refs[0].shape[0] // far

    def write(ref):
        width = ref.shape[1]
        for number in range(far):
            row = pl.multiple_of((within ^ number) * size, size)
            piece_rows = slice(number * size, (number + 1) * size)
            for out, pieces in zip(outputs, layout):
                for target, begin, end in pieces:
                    if target == TURNED:
                        continue
                    value = ref[piece_rows, begin:end].astype(F32)
                    if len(out.shape) == 3:
                        out[target, pl.ds(row, size), :] = value
                    else:
                        out[pl.ds(row, size), target : target + end - begin] = value
            if turned:
                held[pl.ds(row, size), :] = ref[piece_rows, width - held.shape[1] :].astype(F32)
        if turned:
            flipped = held[...].T
            for out, pieces in zip(outputs, layout):
                target, begin, end = pieces[0]
                if target == TURNED:
                    first = width - held.shape[1]
                    out[...] = flipped[begin - first : end - first, :]

    if count == 1:
        write(refs[0])
    else:

        @pl.when(pl.program_id(0) < steps // 2)
        def _():
            write(refs[0])

        @pl.when(pl.program_id(0) >= steps // 2)
        def _():
            write(refs[1])

    if any(weighed):
        ones = jnp.ones((8, LANES), BF)
        total = jnp.zeros(products.shape, F32)
        for out, pieces, used in zip(outputs, layout, weighed):
            if not used:
                continue
            product = out[...] * weights.pop(0)[...].astype(F32)
            if pieces[0][0] == TURNED:
                total = total + jnp.sum(product, axis=0, keepdims=True)
                continue
            narrow = product[:, :LANES]
            for column in range(LANES, product.shape[1], LANES):
                narrow = narrow + product[:, column : column + LANES]
            for part in split3(narrow):
                total = total + dot(ones, part, ((1,), (1,)))
        products[...] = total


def after(value, *others):
    return lax.optimization_barrier((value, *others))[0]


def fence(value, *others):
    anywhere = pl.BlockSpec(memory_space=pl.ANY)
    return pl.pallas_call(
        lambda *refs: None,
        in_specs=[anywhere] * (1 + len(others)),
        out_specs=anywhere,
        out_shape=jax.ShapeDtypeStruct(value.shape, value.dtype),
        input_output_aliases={0: 0},
        cost_estimate=COST,
        name="fence",
    )(value, *others)


def columns_of(ref, which, size):
    return ref[:, pl.ds(pl.multiple_of(which * size, size), size)]


def inverse_rms(values):
    return lax.rsqrt(jnp.mean(values * values, axis=-1, keepdims=True) + EPSILON)


def norm_back(values, inverse, gain, grad):
    scaled = grad * gain
    shared = jnp.mean(scaled * values, axis=-1, keepdims=True) * (inverse * inverse)
    return (
        inverse * (scaled - values * shared),
        jnp.sum(grad * (values * inverse), axis=0, keepdims=True),
    )


def project_small_kernel(
    position,
    tokens,
    gains,
    dt_bias,
    decay_log,
    query_mine,
    query_theirs,
    kv_mine,
    kv_theirs,
    aux_mine,
    aux_theirs,
    normed,
    queries,
    key_vals,
    aux,
    tails,
    carries,
):
    here = position[0]
    half = tokens.shape[1] // 2
    hidden = tokens[...].astype(F32)
    normed[...] = (hidden * inverse_rms(hidden) * gains[0:1]).astype(BF)

    def product(mine, theirs, over=((1,), (0,))):
        return dot(columns_of(normed, here, half), mine[...], over) + dot(
            columns_of(normed, 1 - here, half), theirs[...], over
        )

    key_vals[...] = product(kv_mine, kv_theirs).astype(BF)
    queries[...] = product(query_mine, query_theirs).astype(BF) * jnp.asarray(HD**-0.5, BF)
    found = product(aux_mine, aux_theirs, ((1,), (1,)))
    aux[:, : found.shape[1]] = found
    aux[:, found.shape[1] :] = jnp.zeros_like(aux[:, found.shape[1] :])
    rate = jnp.exp(decay_log[...])
    for block in range(tokens.shape[0] // BLOCK):
        rows = slice(block * BLOCK, (block + 1) * BLOCK)
        _, step_size, _, cumulated = decays(aux[rows, :], dt_bias[...], rate)
        last = cumulated[BLOCK - 1 :, :]
        tails[rows, :] = step_size * jnp.exp(last - cumulated)
        carries[block : block + 1, :] = jnp.exp(last)


def run_project_small(position, tokens, gains, dt_bias, decay_log, query, kv, aux):
    rows, width = tokens.shape
    fixed = lambda shape: pl.BlockSpec(shape, lambda step, place: (0, 0))
    inputs = (tokens, gains, dt_bias, decay_log, *query, *kv, *aux)
    shapes = [
        jax.ShapeDtypeStruct((rows, width), BF),
        jax.ShapeDtypeStruct((rows, KV_AT), BF),
        jax.ShapeDtypeStruct((rows, AUX_AT - KV_AT), BF),
        jax.ShapeDtypeStruct((rows, 3 * LANES), F32),
        jax.ShapeDtypeStruct((rows, LANES), F32),
        jax.ShapeDtypeStruct((8, LANES), F32),
    ]
    return pl.pallas_call(
        project_small_kernel,
        grid_spec=pltpu.PrefetchScalarGridSpec(
            num_scalar_prefetch=1,
            grid=(1,),
            in_specs=[fixed(item.shape) for item in inputs],
            out_specs=[fixed(shape.shape) for shape in shapes],
        ),
        out_shape=shapes,
        compiler_params=params_of(WHOLE_LIMIT),
        cost_estimate=LONG,
        name="project_small",
    )(position, *inputs)


def project_kernel(
    position,
    resets,
    normed,
    aux,
    tails,
    carries,
    ssm_mine,
    ssm_theirs,
    mixed,
    state_out,
):
    here = position[0]
    half = normed.shape[1] // 2
    step = pl.program_id(0)
    found = dot(columns_of(normed, here, half), ssm_mine[...]) + dot(
        columns_of(normed, 1 - here, half), ssm_theirs[...]
    )
    mixed[...] = found.astype(BF)

    for number in range(INNER // CHUNK):

        @pl.when(step == number)
        def _():
            heads = (number * CHUNK // SP, (number + 1) * CHUNK // SP)
            scaled = (found * spread(tails[...], *heads)).astype(BF)
            carried = spread(carries[...], *heads)
            state = jnp.zeros((STATE, CHUNK), F32)
            for block in range(normed.shape[0] // BLOCK):
                rows = slice(block * BLOCK, (block + 1) * BLOCK)
                b_in = aux[rows, :STATE].astype(BF)
                state = jnp.where(resets[block] != 0, 0.0, carried[block : block + 1, :] * state)
                state = state + dot(b_in, scaled[rows, :], ((0,), (0,)))
            state_out[...] = state


CHUNK = 512


def run_project(position, resets, normed, aux, tails, carries, ssm):
    rows, width = normed.shape
    half = width // 2
    inner = ssm[0].shape[1]
    fixed = lambda shape: pl.BlockSpec(shape, lambda step, place, resets: (0, 0))
    sliding = pl.BlockSpec((half, CHUNK), lambda step, place, resets: (0, step))
    return pl.pallas_call(
        project_kernel,
        grid_spec=pltpu.PrefetchScalarGridSpec(
            num_scalar_prefetch=2,
            grid=(inner // CHUNK,),
            in_specs=[
                *[fixed(item.shape) for item in (normed, aux, tails, carries)],
                sliding,
                sliding,
            ],
            out_specs=[
                pl.BlockSpec((rows, CHUNK), lambda step, place, resets: (0, step)),
                pl.BlockSpec(
                    (STATE, CHUNK),
                    lambda step, place, resets: (0, jnp.minimum(step, INNER // CHUNK - 1)),
                ),
            ],
        ),
        out_shape=[
            jax.ShapeDtypeStruct((rows, inner), BF),
            jax.ShapeDtypeStruct((STATE, INNER), F32),
        ],
        compiler_params=params_of(WHOLE_LIMIT),
        cost_estimate=LONG,
        name="project",
    )(position, resets, normed, aux, tails, carries, *ssm)


def middle_kernel(
    position,
    tokens,
    attended,
    gated,
    cotangent,
    gains,
    attn_mine,
    attn_theirs,
    ssm_mine,
    ssm_theirs,
    gate_mine,
    gate_theirs,
    up_mine,
    up_theirs,
    down_mine,
    down_theirs,
    output,
    d_middle,
    d_attn_branch,
    d_ssm_branch,
    d_attended,
    d_gated,
    gain_grads,
    grad_down_theirs,
    grad_down_mine,
    grad_wide_theirs,
    grad_wide_mine,
    attn_branch,
    ssm_branch,
    middle,
    normed,
    flipped,
    out_sum,
    d_normed,
):
    here = position[0]
    step = pl.program_id(0)
    count = pl.num_programs(0)
    width = tokens.shape[1]
    half = width // 2
    attn_half = attended.shape[1] // 2
    ssm_half = gated.shape[1] // 2
    flat = ((1,), (1,))

    def place(which, size):
        return pl.ds(pl.multiple_of(which * size, size), size)

    @pl.when(step == 0)
    def _():
        attn = dot(columns_of(attended, here, attn_half), attn_mine[...]) + dot(
            columns_of(attended, 1 - here, attn_half), attn_theirs[...]
        )
        attn_branch[...] = attn
        ssm = dot(columns_of(gated, here, ssm_half), ssm_mine[...]) + dot(
            columns_of(gated, 1 - here, ssm_half), ssm_theirs[...]
        )
        ssm_branch[...] = ssm
        joined = tokens[...].astype(F32) + 0.5 * (
            attn * inverse_rms(attn) * gains[1:2] + ssm * inverse_rms(ssm) * gains[2:3]
        )
        middle[...] = joined
        out_sum[...] = joined
        scaled = joined * inverse_rms(joined) * gains[3:4]
        normed[...] = scaled.astype(BF)
        flipped[...] = scaled.T.astype(BF)
        d_normed[...] = jnp.zeros_like(d_normed)

    first = step < count // 2
    mine = columns_of(normed, here, half)
    theirs = columns_of(normed, 1 - here, half)
    gate_val = dot(mine, gate_mine[...]) + dot(theirs, gate_theirs[...])
    up_val = dot(mine, up_mine[...]) + dot(theirs, up_theirs[...])
    gate_silu, chance = silu_of(gate_val)
    activated = (gate_silu * up_val).astype(BF)
    down = jnp.where(first, down_theirs[...], down_mine[...])
    d_activated = dot(cotangent[...], down, flat)
    out_sum[...] += dot(activated, down)
    d_up = (d_activated * gate_silu).astype(BF)
    d_gate = (d_activated * up_val * (chance + gate_silu * (1.0 - chance))).astype(BF)
    d_normed[:, place(here, half)] += dot(d_gate, gate_mine[...], flat) + dot(d_up, up_mine[...], flat)
    d_normed[:, place(1 - here, half)] += dot(d_gate, gate_theirs[...], flat) + dot(
        d_up, up_theirs[...], flat
    )
    grad_down = dot(activated, cotangent[...], ((0,), (0,))).astype(BF)

    @pl.when(first)
    def _():
        grad_down_theirs[...] = grad_down

    @pl.when(jnp.logical_not(first))
    def _():
        grad_down_mine[...] = grad_down

    for which, ref in ((here, grad_wide_mine), (1 - here, grad_wide_theirs)):
        turned = flipped[place(which, half), :]
        ref[:, :CHUNK] = dot(turned, d_gate).astype(BF)
        ref[:, CHUNK:] = dot(turned, d_up).astype(BF)

    @pl.when(step == count - 1)
    def _():
        output[...] = out_sum[...].astype(BF)
        joined = middle[...]
        d_joined, d_gain_ff = norm_back(joined, inverse_rms(joined), gains[3:4], d_normed[...])
        d_joined = cotangent[...].astype(F32) + d_joined
        d_middle[...] = d_joined
        attn = attn_branch[...]
        d_attn, d_gain_attn = norm_back(attn, inverse_rms(attn), gains[1:2], 0.5 * d_joined)
        d_attn_low = d_attn.astype(BF)
        d_attn_branch[...] = d_attn_low
        ssm = ssm_branch[...]
        d_ssm, d_gain_ssm = norm_back(ssm, inverse_rms(ssm), gains[2:3], 0.5 * d_joined)
        d_ssm_low = d_ssm.astype(BF)
        d_ssm_branch[...] = d_ssm_low
        gain_grads[...] = jnp.concatenate(
            [d_gain_attn, d_gain_ssm, d_gain_ff, jnp.zeros((5, width), F32)]
        )
        for which, attn_weight, ssm_weight in (
            (here, attn_mine, ssm_mine),
            (1 - here, attn_theirs, ssm_theirs),
        ):
            d_attended[:, place(which, attn_half)] = dot(d_attn_low, attn_weight[...], flat).astype(BF)
            d_gated[:, place(which, ssm_half)] = dot(d_ssm_low, ssm_weight[...], flat).astype(BF)


def run_middle(position, tokens, attended, gated, cotangent, gains, attn, ssm, gate, up, down):
    rows, width = tokens.shape
    half = width // 2
    hidden = gate[0].shape[1]
    count = hidden // CHUNK
    fixed = lambda shape: pl.BlockSpec(shape, lambda step, place: (0,) * len(shape))

    def chunk(step, place):
        first = step < count // 2
        return jnp.where(first, 1 - place[0], place[0]) * (count // 2) + step % (count // 2)

    sliding = pl.BlockSpec((half, CHUNK), lambda step, place: (0, chunk(step, place)))
    early = lambda step, place: (jnp.minimum(step, count // 2 - 1), 0)
    late = lambda step, place: (jnp.maximum(step - count // 2, 0), 0)
    wide = pl.BlockSpec((half, 2 * CHUNK), lambda step, place: (0, chunk(step, place)))
    low = lambda shape: jax.ShapeDtypeStruct(shape, BF)
    full = lambda shape: jax.ShapeDtypeStruct(shape, F32)
    return pl.pallas_call(
        middle_kernel,
        grid_spec=pltpu.PrefetchScalarGridSpec(
            num_scalar_prefetch=1,
            grid=(count,),
            in_specs=[
                *[fixed(item.shape) for item in (tokens, attended, gated, cotangent, gains)],
                *[fixed(item.shape) for item in (*attn, *ssm)],
                *[sliding] * 4,
                pl.BlockSpec((CHUNK, width), late),
                pl.BlockSpec((CHUNK, width), early),
            ],
            out_specs=[
                *[fixed((rows, width))] * 4,
                fixed(attended.shape),
                fixed(gated.shape),
                fixed((8, width)),
                pl.BlockSpec((CHUNK, width), early),
                pl.BlockSpec((CHUNK, width), late),
                wide,
                wide,
            ],
            scratch_shapes=[
                *[pltpu.VMEM((rows, width), F32)] * 3,
                pltpu.VMEM((rows, width), BF),
                pltpu.VMEM((width, rows), BF),
                *[pltpu.VMEM((rows, width), F32)] * 2,
            ],
        ),
        out_shape=[
            low((rows, width)),
            full((rows, width)),
            low((rows, width)),
            low((rows, width)),
            low(attended.shape),
            low(gated.shape),
            full((8, width)),
            low((hidden // 2, width)),
            low((hidden // 2, width)),
            low((half, 2 * hidden)),
            low((half, 2 * hidden)),
        ],
        compiler_params=params_of(LARGE_LIMIT),
        cost_estimate=LONG,
        name="middle",
    )(position, tokens, attended, gated, cotangent, gains, *attn, *ssm, *gate, *up, *down)


def outs_grads_kernel(
    position, attended, gated, normed, d_attn, d_ssm, d_gate, theirs, mine
):
    here = position[0]
    step = pl.program_id(0)
    which = jnp.where(step == 0, 1 - here, here)
    rows = theirs.shape[0]
    down = ((0,), (0,))

    def write(ref):
        at = 0
        for left, right in ((attended, d_attn), (gated, d_ssm), (normed, d_gate)):
            half = left.shape[1] // 2
            for begin in range(0, half, rows):
                turned = left[:, pl.ds(pl.multiple_of(which * half + begin, rows), rows)]
                ref[:, at : at + right.shape[1]] = dot(turned, right[...], down).astype(BF)
                at += right.shape[1]

    @pl.when(step == 0)
    def _():
        write(theirs)

    @pl.when(step == 1)
    def _():
        write(mine)


def run_outs_grads(position, attended, gated, normed, d_attn, d_ssm, d_gate):
    inputs = (attended, gated, normed, d_attn, d_ssm, d_gate)
    rows = attended.shape[1] // 2
    width = sum(
        left.shape[1] // 2 // rows * right.shape[1] for left, right in zip(inputs[:3], inputs[3:])
    )
    fixed = lambda shape: pl.BlockSpec(shape, lambda step, place: (0, 0))
    return pl.pallas_call(
        outs_grads_kernel,
        grid_spec=pltpu.PrefetchScalarGridSpec(
            num_scalar_prefetch=1,
            grid=(2,),
            in_specs=[fixed(item.shape) for item in inputs],
            out_specs=[fixed((rows, width))] * 2,
        ),
        out_shape=[jax.ShapeDtypeStruct((rows, width), BF)] * 2,
        compiler_params=params_of(),
        cost_estimate=COST,
        name="outs_grads",
    )(position, *inputs)


def early_back_kernel(
    position,
    d_query,
    d_kv,
    d_gate,
    query_mine,
    query_theirs,
    kv_mine,
    kv_theirs,
    ssm_mine,
    ssm_theirs,
    d_normed,
):
    here = position[0]
    half = d_normed.shape[1] // 2
    flat = ((1,), (1,))
    for which, query, kv, ssm in (
        (here, query_mine, kv_mine, ssm_mine),
        (1 - here, query_theirs, kv_theirs, ssm_theirs),
    ):
        d_normed[:, pl.ds(pl.multiple_of(which * half, half), half)] = (
            dot(d_query[...], query[...], flat)
            + dot(d_kv[...], kv[...], flat)
            + dot(d_gate[...], ssm[...], flat)
        )


def run_early_back(position, d_query, d_kv, d_gate, query, kv, ssm):
    rows = d_query.shape[0]
    half = query[0].shape[0]
    fixed = lambda shape: pl.BlockSpec(shape, lambda step, place: (0, 0))
    return pl.pallas_call(
        early_back_kernel,
        grid_spec=pltpu.PrefetchScalarGridSpec(
            num_scalar_prefetch=1,
            grid=(1,),
            in_specs=[
                *[fixed(item.shape) for item in (d_query, d_kv, d_gate, *query, *kv)],
                *[pl.BlockSpec((half, INNER), lambda step, place: (0, 1))] * 2,
            ],
            out_specs=fixed((rows, 2 * half)),
        ),
        out_shape=jax.ShapeDtypeStruct((rows, 2 * half), F32),
        compiler_params=params_of(),
        cost_estimate=COST,
        name="early_back",
    )(position, d_query, d_kv, d_gate, *query, *kv, *ssm)


def rest_grads_kernel(
    position, normed, d_query, d_kv, d_mixed, d_aux, gain_grads, d_heads, theirs, mine
):
    here = position[0]
    step = pl.program_id(0)
    half = normed.shape[1] // 2
    which = jnp.where(step == 0, 1 - here, here)
    turned = normed[:, pl.ds(pl.multiple_of(which * half, half), half)]

    def write(ref):
        at = 0
        for right in (d_query, d_kv, d_mixed):
            ref[:, at : at + right.shape[1]] = dot(turned, right[...], ((0,), (0,))).astype(BF)
            at += right.shape[1]
        gains = gain_grads[0:3, pl.ds(pl.multiple_of(which * half, half), half)]
        heads = jnp.concatenate([d_heads[0:1, :], d_heads[1:2, :]], axis=1)
        heads = jnp.concatenate([heads, jnp.zeros((1, half - heads.shape[1]), F32)], axis=1)
        before = 2 * STATE + SH
        columns = jnp.concatenate(
            [
                jnp.zeros((before, half), F32),
                gains,
                heads,
                jnp.zeros((d_aux.shape[1] - before - 4, half), F32),
            ]
        ).T
        ref[:, at:] = (dot(turned, d_aux[...], ((0,), (0,))) + columns).astype(BF)

    @pl.when(step == 0)
    def _():
        write(theirs)

    @pl.when(step == 1)
    def _():
        write(mine)


def run_rest_grads(position, *inputs):
    half = inputs[0].shape[1] // 2
    total = sum(item.shape[1] for item in inputs[1:5])
    fixed = lambda shape: pl.BlockSpec(shape, lambda step, place: (0, 0))
    return pl.pallas_call(
        rest_grads_kernel,
        grid_spec=pltpu.PrefetchScalarGridSpec(
            num_scalar_prefetch=1,
            grid=(2,),
            in_specs=[fixed(item.shape) for item in inputs],
            out_specs=[fixed((half, total))] * 2,
        ),
        out_shape=[jax.ShapeDtypeStruct((half, total), BF)] * 2,
        compiler_params=params_of(),
        cost_estimate=COST,
        name="rest_grads",
    )(position, *inputs)


def late_back_kernel(
    position,
    tokens,
    gains,
    d_middle,
    d_normed,
    d_mixed,
    d_aux,
    aux_mine,
    aux_theirs,
    ssm_mine,
    ssm_theirs,
    grad_tokens,
    total,
):
    here = position[0]
    half = tokens.shape[1] // 2
    for which, aux, ssm in ((here, aux_mine, ssm_mine), (1 - here, aux_theirs, ssm_theirs)):
        columns = pl.ds(pl.multiple_of(which * half, half), half)
        total[:, columns] = (
            d_normed[:, columns]
            + dot(d_mixed[...], ssm[...], ((1,), (1,)))
            + dot(d_aux[:, : aux.shape[0]], aux[...])
        )
    hidden = tokens[...].astype(F32)
    d_hidden, _ = norm_back(hidden, inverse_rms(hidden), gains[0:1], total[...])
    grad_tokens[...] = d_middle[...] + d_hidden


def run_late_back(position, tokens, gains, d_middle, d_normed, d_mixed, d_aux, aux, ssm):
    rows, width = tokens.shape
    half = width // 2
    fixed = lambda shape: pl.BlockSpec(shape, lambda step, place: (0, 0))
    inputs = (tokens, gains, d_middle, d_normed, d_mixed, d_aux, *aux)
    return pl.pallas_call(
        late_back_kernel,
        grid_spec=pltpu.PrefetchScalarGridSpec(
            num_scalar_prefetch=1,
            grid=(1,),
            in_specs=[
                *[fixed(item.shape) for item in inputs],
                *[pl.BlockSpec((half, INNER), lambda step, place: (0, 0))] * 2,
            ],
            out_specs=fixed((rows, width)),
            scratch_shapes=[pltpu.VMEM((rows, width), F32)],
        ),
        out_shape=jax.ShapeDtypeStruct((rows, width), F32),
        compiler_params=params_of(),
        cost_estimate=COST,
        name="late_back",
    )(position, *inputs, *ssm)


def local(
    tokens,
    cotangent,
    doc_blocks,
    gain_in,
    w_query,
    w_kv,
    w_attn_out,
    gain_attn,
    w_ssm_in,
    w_ssm_aux,
    dt_bias,
    decay_log,
    w_ssm_out,
    gain_ssm,
    gain_ff,
    w_gate,
    w_up,
    w_down,
):
    rows, width = tokens.shape
    half = width // 2
    position = lax.axis_index("shard")
    here = position.astype(jnp.int32).reshape(1)
    blocks_here = rows // BLOCK
    docs = doc_blocks[0]
    here_docs = lax.dynamic_slice_in_dim(docs, position * blocks_here, blocks_here, 0)
    prior_docs = jnp.where(position > 0, docs[:blocks_here], -1)
    earlier = jnp.concatenate([prior_docs[-1:], here_docs[:-1]])
    resets = (here_docs != earlier).astype(jnp.int32)
    key_docs = jnp.repeat(jnp.concatenate([prior_docs, here_docs]), BLOCK)
    bias = jnp.where(here_docs[:, None] == key_docs[None, :], 0.0, NEGATIVE)
    lane_pad = LANES - SH
    dt_row = jnp.pad(dt_bias, (0, lane_pad))[None]
    decay_row = jnp.pad(decay_log, (0, lane_pad))[None]

    gain_first = natural(gain_in, swap(gain_in), position, 0).astype(F32)[None]
    query = (w_query, swap(w_query))
    kv = (w_kv, swap(w_kv))
    aux_in = (w_ssm_aux.T, swap(w_ssm_aux.T))
    ssm_in = (w_ssm_in, swap(after(w_ssm_in, kv[1])))
    attn_out, ssm_back, gate, up, down = (
        (weight, swap(weight)) for weight in (w_attn_out, w_ssm_out, w_gate, w_up, w_down)
    )
    normed, scaled_queries, key_vals, aux, tails, carries = run_project_small(
        here, tokens, gain_first, dt_row, decay_row, query, kv, aux_in
    )
    key_prior = lax.ppermute(key_vals, "shard", [(0, 1)])
    later_gains = [
        natural(gain, swap(gain), position, 0).astype(F32)[None]
        for gain in (gain_attn, gain_ssm, gain_ff)
    ]
    gains_all = jnp.concatenate([gain_first, *later_gains, jnp.zeros((4, width), F32)])
    mixed, state_end = run_project(here, resets, normed, aux, tails, carries, ssm_in)
    state_prior = lax.ppermute(state_end, "shard", [(0, 1)])
    attended, log_total = run_attend(scaled_queries, key_prior, key_vals, bias)
    ssm_out, gated, states = run_forward(resets, mixed, aux, dt_row, decay_row, state_prior)

    (
        output,
        d_middle,
        d_attn_low,
        d_ssm_low,
        d_attended,
        d_gated,
        gain_grads,
        down_theirs,
        down_mine,
        wide_theirs,
        wide_mine,
    ) = run_middle(
        here, tokens, attended, gated, cotangent, gains_all, attn_out, ssm_back, gate, up, down
    )
    sums = {
        "down": Stream([down_mine, swap(down_theirs)], WHOLE["down"], *LINKS["down"]),
        "wide": Stream([wide_mine, swap(wide_theirs)], WHOLE["wide"], *LINKS["wide"]),
    }
    token = wide_theirs
    made = {}
    outs_rows = w_attn_out.shape[0]
    full = lambda *shape: jax.ShapeDtypeStruct(shape, F32)
    ssm_pieces = w_ssm_out.shape[0] // outs_rows
    gate_at = width * (1 + ssm_pieces)
    aux_at = AUX_AT + INNER
    spare = aux_at + 2 * STATE + SH
    wide_pieces = [
        [
            (column, 2 * column + offset, 2 * column + offset + CHUNK)
            for column in range(0, w_gate.shape[1], CHUNK)
        ]
        for offset in (0, CHUNK)
    ]
    layouts = {
        "down": [(full(*w_down.shape), width, [(0, 0, width)])],
        "wide": [(full(half, w_gate.shape[1]), w_gate.shape[1], pieces) for pieces in wide_pieces],
        "outs": [
            (full(outs_rows, width), width, [(0, 0, width)]),
            (
                full(ssm_pieces, outs_rows, width),
                width,
                [(piece, width * (1 + piece), width * (2 + piece)) for piece in range(ssm_pieces)],
            ),
            (
                full(half // outs_rows, outs_rows, 2 * INNER),
                INNER,
                [
                    (piece, gate_at + INNER * piece, gate_at + INNER * (piece + 1))
                    for piece in range(half // outs_rows)
                ],
            ),
        ],
        "rest": [
            (full(half, KV_AT), KV_AT, [(0, 0, KV_AT)]),
            (full(half, AUX_AT - KV_AT), AUX_AT - KV_AT, [(0, KV_AT, AUX_AT)]),
            (full(spare - aux_at, half), 3 * LANES, [(TURNED, aux_at, spare)]),
            (full(8, half), 3 * LANES, [(TURNED, spare, spare + 8)]),
            (full(half, 2 * INNER), INNER, [(0, AUX_AT, aux_at)]),
        ],
    }
    def closed(value, number):
        if number + 1 == len(PLAN) or PLAN[number + 1] not in layouts:
            return value
        names = []
        for name in PLAN[number + 1 :]:
            if name not in layouts:
                break
            names.append(name)
        waits = [
            stream.latest()
            for name, stream in sums.items()
            if stream.steps
            and (name in names or stream.gone > 1 or (stream.gone == 1 and name == "down"))
        ]
        return fence(value, *waits)

    d_kv = ssm_in_grad = None
    halves = {}
    rest_weights = (w_query, w_kv, w_ssm_aux.T, None, w_ssm_in)

    def key_grads(made_before):
        if made_before is not None:
            return made_before
        return (d_here + after(d_prior_got, token).astype(F32)).astype(BF)

    def go_on(name):
        nonlocal token, ssm_in_grad
        stream = sums[name]
        stream.hold(token)
        weights = rest_weights if name == "rest" else ()
        place = {"outs": 2, "rest": 4}.get(name)
        shape = layouts[name][place][0].shape if place is not None else None
        if stream.steps:
            stream.prepare()
            token = stream.operand
            stream.go()
            if name == "rest" and not stream.steps and stream.got is not None:
                held = None if ssm_in_grad is None else ssm_in_grad.reshape(shape)
                halves[name] = stream.finish(layouts[name], held, weights, 0)
                if halves[name] is not None:
                    halves[name] = list(halves[name])
                    ssm_in_grad = halves[name][place]
        elif name not in made:
            held = None if place is None or ssm_in_grad is None else ssm_in_grad.reshape(shape)
            if halves.get(name) is not None:
                halves[name][place] = held
                made[name] = stream.finish(layouts[name], None, weights, 1, halves[name])
            else:
                made[name] = stream.finish(layouts[name], held, weights)
            token = made[name][0]
            if place is not None:
                ssm_in_grad = made[name][place].reshape(half, 2 * INNER)

    for number, name in enumerate(PLAN):
        if name in layouts:
            go_on(name)
        elif name == "state":
            d_state_start, d_mixed_gate = run_state_back(
                resets, after(d_gated, token), mixed, aux, ssm_out, dt_row, decay_row
            )
            token = closed(d_state_start, number)
            d_state_end = lax.ppermute(token, "shard", [(1, 0)])
        elif name == "grads":
            outs_theirs, outs_mine = run_outs_grads(
                here, after(attended, token), gated, normed, d_attn_low, d_ssm_low, d_mixed_gate
            )
            token = closed(outs_theirs, number)
            sums["outs"] = Stream([outs_mine, swap(token)], WHOLE["outs"], *LINKS["outs"])
        elif name == "attend":
            d_query, d_prior, d_here = run_attend_back(
                scaled_queries, key_prior, key_vals, bias, log_total, after(d_attended, token)
            )
            token = closed(d_prior, number)
            d_prior_got = lax.ppermute(token, "shard", [(1, 0)])
        elif name == "scan":
            d_mixed, d_aux, d_heads = run_backward(
                resets,
                after(d_gated, token),
                mixed,
                aux,
                ssm_out,
                states,
                dt_row,
                decay_row,
                d_state_end,
            )
            token = d_heads = closed(d_heads, number)
        elif name == "sums":
            d_kv = key_grads(d_kv)
            rest_theirs, rest_mine = run_rest_grads(
                here, normed, d_query, d_kv, d_mixed, d_aux, gain_grads, d_heads
            )
            token = closed(rest_theirs, number)
            sums["rest"] = Stream([rest_mine, swap(token)], WHOLE["rest"], *LINKS["rest"])
        elif name == "early":
            d_kv = key_grads(d_kv)
            d_normed = run_early_back(
                here, after(d_query, token), d_kv, d_mixed_gate, query, kv, ssm_in
            )
            token = d_normed
        elif name == "late":
            grad_tokens = run_late_back(
                here,
                tokens,
                gain_first,
                d_middle,
                d_normed,
                d_mixed,
                after(d_aux, token),
                aux_in,
                ssm_in,
            )
            token = grad_tokens

    for name in layouts:
        while name not in made:
            go_on(name)
    (grad_down,) = made["down"]
    grad_gate, grad_up = made["wide"]
    grad_attn_out, grad_ssm_out, _ = made["outs"]
    grad_query, grad_kv, grad_aux, extras, _, products = made["rest"]
    grad_ssm_in = ssm_in_grad
    gate_products = jnp.sum(
        w_ssm_in[:, INNER:].astype(F32) * grad_ssm_in[:, INNER:], axis=1
    )
    grad_gain_in = (products[0] + gate_products) / gain_in.astype(F32)
    return (
        output,
        grad_tokens,
        grad_gain_in,
        grad_query,
        grad_kv,
        grad_attn_out,
        extras[0],
        grad_ssm_in,
        grad_aux.T,
        extras[3, :SH],
        extras[3, LANES : LANES + SH],
        grad_ssm_out.reshape(w_ssm_out.shape),
        extras[1],
        extras[2],
        grad_gate,
        grad_up,
        grad_down,
    )


def solution(mesh):
    halves = P("shard", None)
    half = P("shard")
    tokens = P(("rep", "shard"), None)
    return jax.shard_map(
        local,
        mesh=mesh,
        in_specs=(
            tokens,
            tokens,
            P("rep", None),
            half,
            halves,
            halves,
            halves,
            half,
            halves,
            halves,
            P(),
            P(),
            halves,
            half,
            half,
            halves,
            halves,
            halves,
        ),
        out_specs=(
            tokens,
            tokens,
            half,
            halves,
            halves,
            halves,
            half,
            halves,
            halves,
            P(),
            P(),
            halves,
            half,
            half,
            halves,
            halves,
            halves,
        ),
        check_vma=False,
    )
```

```python
import functools

import jax
import jax.numpy as jnp
from jax import lax
from jax.experimental import pallas as pl
from jax.experimental.pallas import tpu as pltpu
from jax.sharding import PartitionSpec as P

HD = 64
QH = 8
KVH = 2
SH = 24
SP = 64
STATE = 128
BLOCK = 128
INNER = 1536
LANES = 128
KV_AT = QH * HD
X, Y, Z, ZZ = 0, 1, 2, 3
TURNED = -1
WHOLE = {"down": 2, "wide": 1, "outs": 1, "rest": 2}
LINKS = {
    "down": ((Z, Y, ZZ, X), (Z, X, Y, ZZ)),
    "wide": ((X, Y, ZZ, Z), (Y, X, Z, ZZ)),
    "outs": ((Z, Y, X, ZZ), (Y, X, Z, ZZ)),
    "rest": ((X, Z, Y, ZZ), (Y, X, Z, ZZ)),
}
PLAN = (
    "state",
    "wide",
    "down",
    "scan",
    "grads",
    "wide",
    "down",
    "attend",
    "outs",
    "wide",
    "sums",
    "early",
    "down",
    "outs",
    "wide",
    "rest",
    "down",
    "outs",
    "wide",
    "rest",
    "down",
    "outs",
    "wide",
    "rest",
    "down",
    "outs",
    "wide",
    "rest",
    "down",
    "outs",
    "late",
    "wide",
    "rest",
    "outs",
    "rest",
    "outs",
    "rest",
)
AUX_AT = KV_AT + 2 * KVH * HD
EPSILON = 1e-05
NEGATIVE = -1e30
BF = jnp.bfloat16
F32 = jnp.float32
SWAP = [(0, 1), (1, 0)]
VMEM_LIMIT = 30 * 1024 * 1024
LARGE_LIMIT = 50 * 1024 * 1024
WHOLE_LIMIT = 60 * 1024 * 1024
LONG = pl.CostEstimate(flops=15_000_000_000, bytes_accessed=1_000_000, transcendentals=0)
COST = pl.CostEstimate(flops=1_000_000, bytes_accessed=1_000_000, transcendentals=0)


def dot(left, right, over=((1,), (0,))):
    return lax.dot_general(left, right, (over, ((), ())), preferred_element_type=F32)


def split2(value):
    high = value.astype(BF)
    return high, (value - high.astype(F32)).astype(BF)


def split3(value):
    high = value.astype(BF)
    rest = value - high.astype(F32)
    middle = rest.astype(BF)
    return high, middle, (rest - middle.astype(F32)).astype(BF)


def dot3(left, right, over=((1,), (0,))):
    left_high, left_low = split2(left)
    right_high, right_low = split2(right)
    return dot(left_high, right_high, over) + (
        dot(left_high, right_low, over) + dot(left_low, right_high, over)
    )


def dot1(left, right, over=((1,), (0,))):
    return dot(left.astype(BF), right.astype(BF), over)


def spread(value, begin=0, end=SH):
    first_half = lax.broadcasted_iota(jnp.int32, (value.shape[0], LANES), 1) < SP
    return jnp.concatenate(
        [
            jnp.where(first_half, value[:, head : head + 1], value[:, head + 1 : head + 2])
            for head in range(begin, end, 2)
        ],
        axis=1,
    )


def gather_heads(*values):
    parts = [part for value in values for part in split2(value)]
    sums = dot(jnp.concatenate(parts), head_ones(), ((1,), (1,)))
    found, row = [], 0
    for value in values:
        rows = value.shape[0]
        found.append(sums[row : row + rows] + sums[row + rows : row + 2 * rows])
        row += 2 * rows
    return found


def head_ones():
    head = lax.broadcasted_iota(jnp.int32, (LANES, INNER), 0)
    column = lax.broadcasted_iota(jnp.int32, (LANES, INNER), 1)
    return ((column >= head * SP) & (column < (head + 1) * SP)).astype(BF)


def lower_ones():
    rows = lax.broadcasted_iota(jnp.int32, (BLOCK, BLOCK), 0)
    columns = lax.broadcasted_iota(jnp.int32, (BLOCK, BLOCK), 1)
    return rows >= columns


def cumulate(value, lower, over):
    high, middle, low = split3(value)
    return dot(lower, high, over) + (dot(lower, middle, over) + dot(lower, low, over))


def decays(aux, dt_bias, rate):
    raw = aux[:, 2 * STATE :] + dt_bias
    step = jnp.maximum(raw, 0.0) + jnp.log1p(jnp.exp(-jnp.abs(raw)))
    log_decay = -step * rate
    cumulated = cumulate(log_decay, lower_ones().astype(BF), ((1,), (0,)))
    return raw, step, log_decay, cumulated


def forward_kernel(
    resets, mixed, gate, aux, dt_bias, decay_log, state_in, ssm_out, gated, states, state
):
    number = pl.program_id(0)

    @pl.when(number == 0)
    def _():
        state[...] = state_in[...]

    @pl.when(resets[number] != 0)
    def _():
        state[...] = jnp.zeros_like(state)

    aux_now = aux[...]
    b_in = aux_now[:, :STATE]
    c_out = aux_now[:, STATE : 2 * STATE]
    _, step, _, cumulated = decays(aux_now, dt_bias[...], jnp.exp(decay_log[...]))
    scaled = mixed[...].astype(F32) * spread(step)
    wide = spread(cumulated)
    tail = jnp.exp(wide[BLOCK - 1 :, :] - wide)
    grown = jnp.exp(wide)
    before = state[...]
    states[...] = before[None].astype(BF)
    state[...] = grown[BLOCK - 1 :, :] * before + dot1(b_in, scaled * tail, ((0,), (0,)))
    outer = grown * dot1(c_out, before)
    both = dot3(c_out, b_in, ((1,), (1,)))
    lower = lower_ones()
    flipped = cumulated.T
    first_half = lax.broadcasted_iota(jnp.int32, (BLOCK, LANES), 1) < SP
    scaled_low = scaled.astype(BF)
    zero = jnp.zeros((BLOCK, LANES), BF)
    for pair in range(SH // 2):
        weights = []
        for head in (2 * pair, 2 * pair + 1):
            spread_now = cumulated[:, head : head + 1] - flipped[head : head + 1, :]
            weights.append((jnp.exp(jnp.where(lower, spread_now, NEGATIVE)) * both).astype(BF))
        columns = slice(pair * LANES, (pair + 1) * LANES)
        low = scaled_low[:, columns]
        low = jnp.concatenate([jnp.where(first_half, low, zero), jnp.where(first_half, zero, low)])
        inner = dot(jnp.concatenate(weights, axis=1), low)
        total = inner + outer[:, columns]
        ssm_out[:, columns] = total
        gate_now = gate[:, columns].astype(F32)
        gated[:, columns] = (total * (gate_now / (1.0 + jnp.exp(-gate_now)))).astype(BF)


def silu_of(gate):
    chance = 1.0 / (1.0 + jnp.exp(-gate))
    return gate * chance, chance


def state_back_kernel(
    resets, d_gated, gate, aux, ssm_out, dt_bias, decay_log, d_state_out, d_gate, d_state
):
    number = pl.num_programs(0) - 1 - pl.program_id(0)

    @pl.when(pl.program_id(0) == 0)
    def _():
        d_state[...] = jnp.zeros_like(d_state)

    aux_now = aux[...]
    _, _, _, cumulated = decays(aux_now, dt_bias[...], jnp.exp(decay_log[...]))
    grown = spread(jnp.exp(cumulated))
    gate_silu, chance = silu_of(gate[...].astype(F32))
    d_gated_now = d_gated[...].astype(F32)
    d_gate[...] = (d_gated_now * ssm_out[...] * (chance + gate_silu * (1.0 - chance))).astype(BF)
    d_grown = d_gated_now * gate_silu * grown
    c_out = aux_now[:, STATE : 2 * STATE]
    d_state[...] = grown[BLOCK - 1 :, :] * d_state[...] + dot1(c_out, d_grown, ((0,), (0,)))

    @pl.when(resets[number] != 0)
    def _():
        d_state[...] = jnp.zeros_like(d_state)

    d_state_out[...] = d_state[...].astype(BF)


def backward_kernel(
    resets,
    d_gated,
    mixed,
    gate,
    aux,
    ssm_out,
    states,
    dt_bias,
    decay_log,
    d_state_in,
    d_mixed,
    d_aux,
    d_heads,
    d_state,
):
    number = pl.num_programs(0) - 1 - pl.program_id(0)

    @pl.when(pl.program_id(0) == 0)
    def _():
        d_state[...] = d_state_in[...].astype(F32)
        d_heads[...] = jnp.zeros_like(d_heads)

    lower = lower_ones()
    aux_now = aux[...]
    b_in = aux_now[:, :STATE]
    c_out = aux_now[:, STATE : 2 * STATE]
    rate = jnp.exp(decay_log[...])
    raw, step, log_decay, cumulated = decays(aux_now, dt_bias[...], rate)
    step_wide = spread(step)
    mixed_now = mixed[...].astype(F32)
    scaled = mixed_now * step_wide
    wide = spread(cumulated)
    tail = jnp.exp(wide[BLOCK - 1 :, :] - wide)
    grown = jnp.exp(wide)
    gate_now = gate[...].astype(F32)
    gate_silu, _ = silu_of(gate_now)
    d_gated_now = d_gated[...].astype(F32)
    ssm_now = ssm_out[...]
    d_out = d_gated_now * gate_silu
    before = states[0].astype(F32)
    d_after = d_state[...]
    d_grown = d_out * grown
    d_c = dot1(d_grown, before, ((1,), (1,)))
    d_before = grown[BLOCK - 1 :, :] * d_after + dot1(c_out, d_grown, ((0,), (0,)))
    tailed = scaled * tail
    d_b = dot1(tailed, d_after, ((1,), (1,)))
    d_tailed = dot1(b_in, d_after)
    ends = jnp.sum(tailed * d_tailed, axis=0, keepdims=True) + grown[BLOCK - 1 :, :] * jnp.sum(
        d_after * before, axis=0, keepdims=True
    )
    both = dot3(c_out, b_in, ((1,), (1,)))
    flipped = cumulated.T
    first_half = lax.broadcasted_iota(jnp.int32, (BLOCK, LANES), 1) < SP
    scaled_low = scaled.astype(BF)
    d_low = d_out.astype(BF)
    zero = jnp.zeros((BLOCK, LANES), BF)
    d_both = jnp.zeros((BLOCK, BLOCK), F32)
    parts = []
    for pair in range(SH // 2):
        columns = slice(pair * LANES, (pair + 1) * LANES)
        falls = []
        for head in (2 * pair, 2 * pair + 1):
            spread_now = cumulated[:, head : head + 1] - flipped[head : head + 1, :]
            falls.append(jnp.exp(jnp.where(lower, spread_now, NEGATIVE)))
        weight = jnp.concatenate([(falls[0] * both).astype(BF), (falls[1] * both).astype(BF)])
        low = d_low[:, columns]
        low = jnp.concatenate([jnp.where(first_half, low, zero), jnp.where(first_half, zero, low)])
        d_weight = dot(low, scaled_low[:, columns], ((1,), (1,)))
        d_both = d_both + falls[0] * d_weight[:BLOCK] + falls[1] * d_weight[BLOCK:]
        parts.append(dot(weight, low, ((0,), (0,))))
    d_inner = jnp.concatenate(parts, axis=1)
    carried = tail * d_tailed
    d_scaled = d_inner + carried
    d_mixed[...] = (d_scaled * step_wide).astype(BF)
    d_step, d_cumulated, d_last = gather_heads(
        d_scaled * mixed_now,
        d_low.astype(F32) * ssm_now - scaled_low.astype(F32) * d_inner - scaled * carried,
        jnp.broadcast_to(ends, (8, INNER)),
    )
    d_decay = cumulate(d_cumulated, lower.astype(BF), ((0,), (0,))) + d_last[:1]
    d_raw = (d_step - d_decay * rate) * (1.0 / (1.0 + jnp.exp(-raw)))
    real = lax.broadcasted_iota(jnp.int32, (BLOCK, LANES), 1) < SH
    d_raw = jnp.where(real, d_raw, 0.0)
    d_c = d_c + dot1(d_both, b_in)
    d_b = d_b + dot1(d_both, c_out, ((0,), (0,)))
    d_aux[...] = jnp.concatenate([d_b, d_c, d_raw], axis=1).astype(BF)
    d_heads[...] += jnp.concatenate(
        [
            jnp.sum(d_raw, axis=0, keepdims=True),
            jnp.sum(jnp.where(real, d_decay * log_decay, 0.0), axis=0, keepdims=True),
            jnp.zeros((6, LANES), F32),
        ]
    )
    d_state[...] = d_before

    @pl.when(resets[number] != 0)
    def _():
        d_state[...] = jnp.zeros_like(d_state)


def scalars():
    return pl.BlockSpec(memory_space=pltpu.SMEM)


def whole(shape):
    return pl.BlockSpec(shape, lambda number: (0,) * len(shape))


def params_of(limit=VMEM_LIMIT):
    return pltpu.CompilerParams(dimension_semantics=("arbitrary",), vmem_limit_bytes=limit)


def run_forward(resets, mixed, aux, dt_bias, decay_log, state_in):
    rows = mixed.shape[0]
    count = rows // BLOCK
    return pl.pallas_call(
        forward_kernel,
        grid=(count,),
        in_specs=[
            scalars(),
            pl.BlockSpec((BLOCK, INNER), lambda number: (number, 0)),
            pl.BlockSpec((BLOCK, INNER), lambda number: (number, 1)),
            pl.BlockSpec((BLOCK, 3 * LANES), lambda number: (number, 0)),
            whole((1, LANES)),
            whole((1, LANES)),
            whole((STATE, INNER)),
        ],
        out_specs=[
            pl.BlockSpec((BLOCK, INNER), lambda number: (number, 0)),
            pl.BlockSpec((BLOCK, INNER), lambda number: (number, 0)),
            pl.BlockSpec((1, STATE, INNER), lambda number: (number, 0, 0)),
        ],
        out_shape=[
            jax.ShapeDtypeStruct((rows, INNER), F32),
            jax.ShapeDtypeStruct((rows, INNER), BF),
            jax.ShapeDtypeStruct((count, STATE, INNER), BF),
        ],
        scratch_shapes=[pltpu.VMEM((STATE, INNER), F32)],
        compiler_params=params_of(),
        cost_estimate=LONG,
        name="ssm_forward",
    )(resets, mixed, mixed, aux, dt_bias, decay_log, state_in)


def run_state_back(resets, d_gated, mixed, aux, ssm_out, dt_bias, decay_log):
    count = mixed.shape[0] // BLOCK
    turned = lambda number: (count - 1 - number, 0)
    return pl.pallas_call(
        state_back_kernel,
        grid=(count,),
        in_specs=[
            scalars(),
            pl.BlockSpec((BLOCK, INNER), turned),
            pl.BlockSpec((BLOCK, INNER), lambda number: (count - 1 - number, 1)),
            pl.BlockSpec((BLOCK, 3 * LANES), turned),
            pl.BlockSpec((BLOCK, INNER), turned),
            whole((1, LANES)),
            whole((1, LANES)),
        ],
        out_specs=[whole((STATE, INNER)), pl.BlockSpec((BLOCK, INNER), turned)],
        out_shape=[
            jax.ShapeDtypeStruct((STATE, INNER), BF),
            jax.ShapeDtypeStruct((mixed.shape[0], INNER), BF),
        ],
        scratch_shapes=[pltpu.VMEM((STATE, INNER), F32)],
        compiler_params=params_of(WHOLE_LIMIT),
        cost_estimate=COST,
        name="ssm_state_back",
    )(resets, d_gated, mixed, aux, ssm_out, dt_bias, decay_log)


def run_backward(resets, d_gated, mixed, aux, ssm_out, states, dt_bias, decay_log, d_state_in):
    rows = mixed.shape[0]
    count = rows // BLOCK
    turned = lambda number: (count - 1 - number, 0)
    return pl.pallas_call(
        backward_kernel,
        grid=(count,),
        in_specs=[
            scalars(),
            pl.BlockSpec((BLOCK, INNER), turned),
            pl.BlockSpec((BLOCK, INNER), turned),
            pl.BlockSpec((BLOCK, INNER), lambda number: (count - 1 - number, 1)),
            pl.BlockSpec((BLOCK, 3 * LANES), turned),
            pl.BlockSpec((BLOCK, INNER), turned),
            pl.BlockSpec((1, STATE, INNER), lambda number: (count - 1 - number, 0, 0)),
            whole((1, LANES)),
            whole((1, LANES)),
            whole((STATE, INNER)),
        ],
        out_specs=[
            pl.BlockSpec((BLOCK, INNER), turned),
            pl.BlockSpec((BLOCK, 3 * LANES), turned),
            whole((8, LANES)),
        ],
        out_shape=[
            jax.ShapeDtypeStruct((rows, INNER), BF),
            jax.ShapeDtypeStruct((rows, 3 * LANES), BF),
            jax.ShapeDtypeStruct((8, LANES), F32),
        ],
        scratch_shapes=[pltpu.VMEM((STATE, INNER), F32)],
        compiler_params=params_of(),
        cost_estimate=COST,
        name="ssm_backward",
    )(resets, d_gated, mixed, mixed, aux, ssm_out, states, dt_bias, decay_log, d_state_in)


def head_rows(ref, start, group, width):
    return jnp.concatenate(
        [
            ref[start : start + BLOCK, (group * width + head) * HD : (group * width + head + 1) * HD]
            for head in range(width)
        ]
    )


def masked_scores(q_rows, k_rows, bias_row, lower, width):
    raw = dot(q_rows, k_rows, ((1,), (1,))) + bias_row
    edge = raw.shape[1] - BLOCK
    corner = jnp.where(jnp.concatenate([lower] * width), raw[:, edge:], NEGATIVE)
    return jnp.concatenate([raw[:, :edge], corner], axis=1)


def attend_kernel(q_ref, prior_ref, here_ref, bias_ref, out_ref, total_ref):
    width = QH // KVH
    rows = q_ref.shape[0]
    halo = prior_ref.shape[0]
    lower = lower_ones()
    for group in range(KVH):
        key_columns = slice(group * HD, (group + 1) * HD)
        value_columns = slice((KVH + group) * HD, (KVH + group + 1) * HD)
        keys = jnp.concatenate([prior_ref[:, key_columns], here_ref[:, key_columns]])
        values = jnp.concatenate([prior_ref[:, value_columns], here_ref[:, value_columns]])
        for block in range(rows // BLOCK):
            start = block * BLOCK
            reach = halo + start + BLOCK
            q_rows = head_rows(q_ref, start, group, width)
            scores = masked_scores(
                q_rows, keys[:reach], bias_ref[block : block + 1, :reach], lower, width
            )
            top = jnp.max(scores, axis=1, keepdims=True)
            powers = jnp.exp(scores - top)
            total = jnp.sum(powers, axis=1, keepdims=True)
            probs = (powers * (1.0 / total)).astype(BF)
            out = dot(probs, values[:reach])
            log_total = top + jnp.log(total)
            for head in range(width):
                place = group * width + head
                some = slice(head * BLOCK, (head + 1) * BLOCK)
                out_ref[start : start + BLOCK, place * HD : (place + 1) * HD] = out[some].astype(BF)
                total_ref[start : start + BLOCK, place : place + 1] = log_total[some]


def attend_back_kernel(
    q_ref, prior_ref, here_ref, bias_ref, total_ref, d_ref, dq_ref, d_prior_ref, d_here_ref, sums
):
    width = QH // KVH
    rows = q_ref.shape[0]
    halo = prior_ref.shape[0]
    lower = lower_ones()
    sums[...] = jnp.zeros_like(sums)
    for group in range(KVH):
        key_columns = slice(group * HD, (group + 1) * HD)
        value_columns = slice((KVH + group) * HD, (KVH + group + 1) * HD)
        keys = jnp.concatenate([prior_ref[:, key_columns], here_ref[:, key_columns]])
        values = jnp.concatenate([prior_ref[:, value_columns], here_ref[:, value_columns]])
        for block in range(rows // BLOCK):
            start = block * BLOCK
            reach = halo + start + BLOCK
            q_rows = head_rows(q_ref, start, group, width)
            d_rows = head_rows(d_ref, start, group, width)
            scores = masked_scores(
                q_rows, keys[:reach], bias_ref[block : block + 1, :reach], lower, width
            )
            log_total = jnp.concatenate(
                [
                    total_ref[start : start + BLOCK, group * width + head : group * width + head + 1]
                    for head in range(width)
                ]
            )
            probs = jnp.exp(scores - log_total)
            probs_low = probs.astype(BF)
            d_probs = dot(d_rows, values[:reach], ((1,), (1,)))
            weighed = probs * d_probs
            d_scores = (weighed - probs * jnp.sum(weighed, axis=1, keepdims=True)).astype(BF)
            d_queries = dot(d_scores, keys[:reach]) * HD**-0.5
            for head in range(width):
                place = group * width + head
                some = slice(head * BLOCK, (head + 1) * BLOCK)
                dq_ref[start : start + BLOCK, place * HD : (place + 1) * HD] = d_queries[some].astype(BF)
            sums[:reach, key_columns] += dot(d_scores, q_rows, ((0,), (0,)))
            sums[:reach, value_columns] += dot(probs_low, d_rows, ((0,), (0,)))
    d_prior_ref[...] = sums[:halo].astype(BF)
    d_here_ref[...] = sums[halo:]


def run_attend(queries, prior, here, bias):
    rows = queries.shape[0]
    return pl.pallas_call(
        attend_kernel,
        out_shape=[
            jax.ShapeDtypeStruct((rows, QH * HD), BF),
            jax.ShapeDtypeStruct((rows, QH), F32),
        ],
        compiler_params=pltpu.CompilerParams(vmem_limit_bytes=VMEM_LIMIT),
        cost_estimate=LONG,
        name="attend",
    )(queries, prior, here, bias)


def run_attend_back(queries, prior, here, bias, log_total, d_attended):
    rows = queries.shape[0]
    halo = prior.shape[0]
    return pl.pallas_call(
        attend_back_kernel,
        out_shape=[
            jax.ShapeDtypeStruct((rows, QH * HD), BF),
            jax.ShapeDtypeStruct((halo, 2 * KVH * HD), BF),
            jax.ShapeDtypeStruct((rows, 2 * KVH * HD), F32),
        ],
        scratch_shapes=[pltpu.VMEM((halo + rows, 2 * KVH * HD), F32)],
        compiler_params=pltpu.CompilerParams(vmem_limit_bytes=VMEM_LIMIT),
        cost_estimate=COST,
        name="attend_back",
    )(queries, prior, here, bias, log_total, d_attended)


def swap(value):
    return lax.ppermute(value, "shard", SWAP)


def natural(mine, theirs, position, axis):
    return jnp.where(
        position == 0,
        jnp.concatenate([mine, theirs], axis=axis),
        jnp.concatenate([theirs, mine], axis=axis),
    )


def half_of(value, which, axis):
    size = value.shape[axis] // 2
    return lax.dynamic_slice_in_dim(value, which * size, size, axis)


class Stream:
    def __init__(self, terms, whole, *orders):
        self.terms = terms
        self.count = lax.axis_size("rep")
        self.bits = self.count.bit_length() - 1
        self.stack = None
        self.got = None
        self.gone = 0
        if self.count != 1 << self.bits:
            self.stack = lax.psum(self.part(0, terms[0].shape[0]), "rep")
            self.bits = 0
        places = range(self.bits)
        self.orders = [
            [bit for bit in order if bit < self.bits] + [bit for bit in places if bit not in order]
            for order in orders
        ]
        rep, core = lax.axis_index("rep"), lax.axis_index("shard")
        self.cuts = max(0, self.bits - whole)
        self.sides = [
            jnp.where(core == 0, (rep >> first) & 1, (rep >> second) & 1)
            for first, second in zip(*self.orders)
        ][: self.cuts]
        self.steps = [("scatter", step) for step in places[: self.cuts]]
        self.steps += [("exchange", step) for step in places[self.cuts :]]
        self.steps += [("gather", step) for step in reversed(places[: self.cuts])]

    def pairs(self, step):
        return [
            (rep * 2 + core, (rep ^ (1 << self.orders[core][step])) * 2 + core)
            for rep in range(self.count)
            for core in range(2)
        ]

    def part(self, start, size):
        total = lax.dynamic_slice_in_dim(self.terms[0], start, size, 0).astype(F32)
        for term in self.terms[1:]:
            total = total + lax.dynamic_slice_in_dim(term, start, size, 0).astype(F32)
        return total.astype(BF)

    def latest(self):
        if self.got is not None:
            return self.got
        return self.terms[-1] if self.stack is None else self.stack

    def hold(self, token):
        if self.got is not None:
            self.got = after(self.got, token)
        elif self.stack is None:
            self.terms[-1] = after(self.terms[-1], token)

    def prepare(self):
        kind, step = self.steps[0]
        if kind == "gather":
            if self.stack is None:
                self.stack = self.part(0, self.terms[0].shape[0])
            else:
                self.stack = jnp.concatenate([self.stack, self.got])
            self.operand = self.stack
        elif kind == "exchange":
            self.operand = self.part(0, self.terms[0].shape[0])
        else:
            size = self.terms[0].shape[0] // 2
            self.operand = self.part((1 - self.sides[step]) * size, size)

    def go(self):
        kind, step = self.steps.pop(0)
        self.gone += 1
        got = lax.ppermute(self.operand, ("rep", "shard"), self.pairs(step))
        if kind == "gather":
            self.got = got
        elif kind == "exchange":
            self.terms = [self.operand, got]
        else:
            size = self.terms[0].shape[0] // 2
            self.terms = [
                lax.dynamic_slice_in_dim(term, self.sides[step] * size, size, 0)
                for term in self.terms
            ] + [got]

    def own(self):
        block = jnp.zeros((), jnp.int32)
        for side in self.sides:
            block = 2 * block + side
        return block.astype(jnp.int32)

    def finish(self, outputs, started=None, weights=(), part=None, before=()):
        if self.stack is None:
            self.stack = self.part(0, self.terms[0].shape[0])
        stacks = [self.stack] if self.got is None else [self.stack, self.got]
        blocks = 1 << self.cuts
        far = max(1, blocks // 4)
        quarters = blocks // far
        each = quarters // len(stacks)
        size = stacks[0].shape[0] // each // far
        width = stacks[0].shape[1]
        own = self.own()
        numbers = jnp.arange(quarters, dtype=jnp.int32)
        if part is not None:
            if size % 16:
                return None
            stacks = stacks[part : part + 1]
            numbers = numbers[each * part : each * (part + 1)]
        if size % 16:
            flat = jnp.concatenate(stacks).reshape(blocks, size, width)
            flat = jnp.zeros_like(flat).at[jnp.arange(blocks) ^ own].set(flat).reshape(-1, width)
            made = []
            for shape, _, pieces in outputs:
                cuts = [flat[:, begin:end].astype(F32) for _, begin, end in pieces]
                if pieces[0][0] == TURNED:
                    made.append(cuts[0].T)
                    continue
                value = jnp.stack(cuts) if len(shape.shape) == 3 else jnp.concatenate(cuts, axis=1)
                made.append(value)
            products = [
                jnp.sum(
                    value * weight[:, : value.shape[1]].astype(F32),
                    axis=0 if pieces[0][0] == TURNED else 1,
                )
                for value, weight, (_, _, pieces) in zip(made, weights, outputs)
                if weight is not None
            ]
            spare = outputs[-1][0].shape[-1] - made[-1].shape[-1]
            if spare:
                left = made[-1].ndim == 3
                other = jnp.zeros(made[-1].shape[:-1] + (spare,), F32)
                if started is not None:
                    other = started[..., :spare] if left else started[..., -spare:]
                made[-1] = jnp.concatenate([other, made[-1]] if left else [made[-1], other], axis=-1)
            if products:
                made.append(jnp.broadcast_to(sum(products), (8, products[0].shape[0])))
            return made
        rows = far * size
        in_specs = [
            pl.BlockSpec((rows, width), lambda step, places: (jnp.minimum(step, each - 1), 0))
        ]
        if len(stacks) == 2:
            in_specs.append(
                pl.BlockSpec((rows, width), lambda step, places: (jnp.maximum(step - each, 0), 0))
            )
        out_specs = []
        scratch = []
        for shape, block, pieces in outputs:
            if pieces[0][0] == TURNED:
                out_specs.append(
                    pl.BlockSpec((shape.shape[0], rows), lambda step, places: (0, places[step]))
                )
                scratch = [pltpu.VMEM((rows, block), F32)]
            elif len(shape.shape) == 3:
                last = shape.shape[2] // block - 1
                out_specs.append(
                    pl.BlockSpec(
                        (shape.shape[0], rows, block),
                        lambda step, places, last=last: (0, places[step], last),
                    )
                )
            else:
                out_specs.append(pl.BlockSpec((rows, block), lambda step, places: (places[step], 0)))
        inputs = list(stacks)
        shapes = [shape for shape, _, _ in outputs]
        for weight, (_, block, pieces) in zip(weights, outputs):
            if weight is None:
                continue
            inputs.append(weight)
            if pieces[0][0] == TURNED:
                in_specs.append(
                    pl.BlockSpec((weight.shape[0], rows), lambda step, places: (0, places[step]))
                )
            else:
                in_specs.append(pl.BlockSpec((rows, block), lambda step, places: (places[step], 0)))
        if weights:
            out_specs.append(pl.BlockSpec((8, rows), lambda step, places: (0, places[step])))
            shapes.append(jax.ShapeDtypeStruct((8, rows * quarters), F32))
        aliases = {}
        if part != 1 and started is not None:
            before = [started]
            aliases = {1 + len(inputs): len(outputs) - 1}
        elif part == 1:
            aliases = {1 + len(inputs) + number: number for number in range(len(shapes))}
        inputs += before
        in_specs += [pl.BlockSpec(memory_space=pl.ANY)] * len(before)
        places = jnp.concatenate([numbers ^ (own // far), (own % far).reshape(1)])
        return pl.pallas_call(
            functools.partial(
                finish_kernel,
                len(stacks),
                far,
                [cut for _, _, cut in outputs],
                [weight is not None for weight in weights],
            ),
            grid_spec=pltpu.PrefetchScalarGridSpec(
                num_scalar_prefetch=1,
                grid=numbers.shape,
                in_specs=in_specs,
                out_specs=out_specs,
                scratch_shapes=scratch,
            ),
            out_shape=shapes,
            input_output_aliases=aliases,
            compiler_params=params_of(),
            cost_estimate=COST,
            name="unpack",
        )(places, *inputs)


def finish_kernel(count, far, layout, weighed, places, *refs):
    turned = any(pieces[0][0] == TURNED for pieces in layout)
    if turned:
        held, refs = refs[-1], refs[:-1]
    if any(weighed):
        products, refs = refs[-1], refs[:-1]
    outputs = refs[-len(layout) :]
    weights = list(refs[count : count + sum(weighed)])
    steps = pl.num_programs(0)
    within = places[steps]
    size = refs[0].shape[0] // far

    def write(ref):
        width = ref.shape[1]
        for number in range(far):
            row = pl.multiple_of((within ^ number) * size, size)
            piece_rows = slice(number * size, (number + 1) * size)
            for out, pieces in zip(outputs, layout):
                for target, begin, end in pieces:
                    if target == TURNED:
                        continue
                    value = ref[piece_rows, begin:end].astype(F32)
                    if len(out.shape) == 3:
                        out[target, pl.ds(row, size), :] = value
                    else:
                        out[pl.ds(row, size), target : target + end - begin] = value
            if turned:
                held[pl.ds(row, size), :] = ref[piece_rows, width - held.shape[1] :].astype(F32)
        if turned:
            flipped = held[...].T
            for out, pieces in zip(outputs, layout):
                target, begin, end = pieces[0]
                if target == TURNED:
                    first = width - held.shape[1]
                    out[...] = flipped[begin - first : end - first, :]

    if count == 1:
        write(refs[0])
    else:

        @pl.when(pl.program_id(0) < steps // 2)
        def _():
            write(refs[0])

        @pl.when(pl.program_id(0) >= steps // 2)
        def _():
            write(refs[1])

    if any(weighed):
        ones = jnp.ones((8, LANES), BF)
        total = jnp.zeros(products.shape, F32)
        for out, pieces, used in zip(outputs, layout, weighed):
            if not used:
                continue
            product = out[...] * weights.pop(0)[...].astype(F32)
            if pieces[0][0] == TURNED:
                total = total + jnp.sum(product, axis=0, keepdims=True)
                continue
            narrow = product[:, :LANES]
            for column in range(LANES, product.shape[1], LANES):
                narrow = narrow + product[:, column : column + LANES]
            for part in split3(narrow):
                total = total + dot(ones, part, ((1,), (1,)))
        products[...] = total


def after(value, *others):
    return lax.optimization_barrier((value, *others))[0]


def fence(value, *others):
    anywhere = pl.BlockSpec(memory_space=pl.ANY)
    return pl.pallas_call(
        lambda *refs: None,
        in_specs=[anywhere] * (1 + len(others)),
        out_specs=anywhere,
        out_shape=jax.ShapeDtypeStruct(value.shape, value.dtype),
        input_output_aliases={0: 0},
        cost_estimate=COST,
        name="fence",
    )(value, *others)


def columns_of(ref, which, size):
    return ref[:, pl.ds(pl.multiple_of(which * size, size), size)]


def inverse_rms(values):
    return lax.rsqrt(jnp.mean(values * values, axis=-1, keepdims=True) + EPSILON)


def norm_back(values, inverse, gain, grad):
    scaled = grad * gain
    shared = jnp.mean(scaled * values, axis=-1, keepdims=True) * (inverse * inverse)
    return (
        inverse * (scaled - values * shared),
        jnp.sum(grad * (values * inverse), axis=0, keepdims=True),
    )


def project_small_kernel(
    position,
    tokens,
    gains,
    dt_bias,
    decay_log,
    query_mine,
    query_theirs,
    kv_mine,
    kv_theirs,
    aux_mine,
    aux_theirs,
    normed,
    queries,
    key_vals,
    aux,
    tails,
    carries,
):
    here = position[0]
    half = tokens.shape[1] // 2
    hidden = tokens[...].astype(F32)
    normed[...] = (hidden * inverse_rms(hidden) * gains[0:1]).astype(BF)

    def product(mine, theirs, over=((1,), (0,))):
        return dot(columns_of(normed, here, half), mine[...], over) + dot(
            columns_of(normed, 1 - here, half), theirs[...], over
        )

    key_vals[...] = product(kv_mine, kv_theirs).astype(BF)
    queries[...] = product(query_mine, query_theirs).astype(BF) * jnp.asarray(HD**-0.5, BF)
    found = product(aux_mine, aux_theirs, ((1,), (1,)))
    aux[:, : found.shape[1]] = found
    aux[:, found.shape[1] :] = jnp.zeros_like(aux[:, found.shape[1] :])
    rate = jnp.exp(decay_log[...])
    for block in range(tokens.shape[0] // BLOCK):
        rows = slice(block * BLOCK, (block + 1) * BLOCK)
        _, step_size, _, cumulated = decays(aux[rows, :], dt_bias[...], rate)
        last = cumulated[BLOCK - 1 :, :]
        tails[rows, :] = step_size * jnp.exp(last - cumulated)
        carries[block : block + 1, :] = jnp.exp(last)


def run_project_small(position, tokens, gains, dt_bias, decay_log, query, kv, aux):
    rows, width = tokens.shape
    fixed = lambda shape: pl.BlockSpec(shape, lambda step, place: (0, 0))
    inputs = (tokens, gains, dt_bias, decay_log, *query, *kv, *aux)
    shapes = [
        jax.ShapeDtypeStruct((rows, width), BF),
        jax.ShapeDtypeStruct((rows, KV_AT), BF),
        jax.ShapeDtypeStruct((rows, AUX_AT - KV_AT), BF),
        jax.ShapeDtypeStruct((rows, 3 * LANES), F32),
        jax.ShapeDtypeStruct((rows, LANES), F32),
        jax.ShapeDtypeStruct((8, LANES), F32),
    ]
    return pl.pallas_call(
        project_small_kernel,
        grid_spec=pltpu.PrefetchScalarGridSpec(
            num_scalar_prefetch=1,
            grid=(1,),
            in_specs=[fixed(item.shape) for item in inputs],
            out_specs=[fixed(shape.shape) for shape in shapes],
        ),
        out_shape=shapes,
        compiler_params=params_of(WHOLE_LIMIT),
        cost_estimate=LONG,
        name="project_small",
    )(position, *inputs)


def project_kernel(
    position,
    resets,
    normed,
    aux,
    tails,
    carries,
    ssm_mine,
    ssm_theirs,
    mixed,
    state_out,
):
    here = position[0]
    half = normed.shape[1] // 2
    step = pl.program_id(0)
    found = dot(columns_of(normed, here, half), ssm_mine[...]) + dot(
        columns_of(normed, 1 - here, half), ssm_theirs[...]
    )
    mixed[...] = found.astype(BF)

    for number in range(INNER // CHUNK):

        @pl.when(step == number)
        def _():
            heads = (number * CHUNK // SP, (number + 1) * CHUNK // SP)
            scaled = (found * spread(tails[...], *heads)).astype(BF)
            carried = spread(carries[...], *heads)
            state = jnp.zeros((STATE, CHUNK), F32)
            for block in range(normed.shape[0] // BLOCK):
                rows = slice(block * BLOCK, (block + 1) * BLOCK)
                b_in = aux[rows, :STATE].astype(BF)
                state = jnp.where(resets[block] != 0, 0.0, carried[block : block + 1, :] * state)
                state = state + dot(b_in, scaled[rows, :], ((0,), (0,)))
            state_out[...] = state


CHUNK = 512


def run_project(position, resets, normed, aux, tails, carries, ssm):
    rows, width = normed.shape
    half = width // 2
    inner = ssm[0].shape[1]
    fixed = lambda shape: pl.BlockSpec(shape, lambda step, place, resets: (0, 0))
    sliding = pl.BlockSpec((half, CHUNK), lambda step, place, resets: (0, step))
    return pl.pallas_call(
        project_kernel,
        grid_spec=pltpu.PrefetchScalarGridSpec(
            num_scalar_prefetch=2,
            grid=(inner // CHUNK,),
            in_specs=[
                *[fixed(item.shape) for item in (normed, aux, tails, carries)],
                sliding,
                sliding,
            ],
            out_specs=[
                pl.BlockSpec((rows, CHUNK), lambda step, place, resets: (0, step)),
                pl.BlockSpec(
                    (STATE, CHUNK),
                    lambda step, place, resets: (0, jnp.minimum(step, INNER // CHUNK - 1)),
                ),
            ],
        ),
        out_shape=[
            jax.ShapeDtypeStruct((rows, inner), BF),
            jax.ShapeDtypeStruct((STATE, INNER), F32),
        ],
        compiler_params=params_of(WHOLE_LIMIT),
        cost_estimate=LONG,
        name="project",
    )(position, resets, normed, aux, tails, carries, *ssm)


def middle_kernel(
    position,
    tokens,
    attended,
    gated,
    cotangent,
    gains,
    attn_mine,
    attn_theirs,
    ssm_mine,
    ssm_theirs,
    gate_mine,
    gate_theirs,
    up_mine,
    up_theirs,
    down_mine,
    down_theirs,
    output,
    d_middle,
    d_attn_branch,
    d_ssm_branch,
    d_attended,
    d_gated,
    gain_grads,
    grad_down_theirs,
    grad_down_mine,
    grad_wide_theirs,
    grad_wide_mine,
    attn_branch,
    ssm_branch,
    middle,
    normed,
    flipped,
    out_sum,
    d_normed,
):
    here = position[0]
    step = pl.program_id(0)
    count = pl.num_programs(0)
    width = tokens.shape[1]
    half = width // 2
    attn_half = attended.shape[1] // 2
    ssm_half = gated.shape[1] // 2
    flat = ((1,), (1,))

    def place(which, size):
        return pl.ds(pl.multiple_of(which * size, size), size)

    @pl.when(step == 0)
    def _():
        attn = dot(columns_of(attended, here, attn_half), attn_mine[...]) + dot(
            columns_of(attended, 1 - here, attn_half), attn_theirs[...]
        )
        attn_branch[...] = attn
        ssm = dot(columns_of(gated, here, ssm_half), ssm_mine[...]) + dot(
            columns_of(gated, 1 - here, ssm_half), ssm_theirs[...]
        )
        ssm_branch[...] = ssm
        joined = tokens[...].astype(F32) + 0.5 * (
            attn * inverse_rms(attn) * gains[1:2] + ssm * inverse_rms(ssm) * gains[2:3]
        )
        middle[...] = joined
        out_sum[...] = joined
        scaled = joined * inverse_rms(joined) * gains[3:4]
        normed[...] = scaled.astype(BF)
        flipped[...] = scaled.T.astype(BF)
        d_normed[...] = jnp.zeros_like(d_normed)

    first = step < count // 2
    mine = columns_of(normed, here, half)
    theirs = columns_of(normed, 1 - here, half)
    gate_val = dot(mine, gate_mine[...]) + dot(theirs, gate_theirs[...])
    up_val = dot(mine, up_mine[...]) + dot(theirs, up_theirs[...])
    gate_silu, chance = silu_of(gate_val)
    activated = (gate_silu * up_val).astype(BF)
    down = jnp.where(first, down_theirs[...], down_mine[...])
    d_activated = dot(cotangent[...], down, flat)
    out_sum[...] += dot(activated, down)
    d_up = (d_activated * gate_silu).astype(BF)
    d_gate = (d_activated * up_val * (chance + gate_silu * (1.0 - chance))).astype(BF)
    d_normed[:, place(here, half)] += dot(d_gate, gate_mine[...], flat) + dot(d_up, up_mine[...], flat)
    d_normed[:, place(1 - here, half)] += dot(d_gate, gate_theirs[...], flat) + dot(
        d_up, up_theirs[...], flat
    )
    grad_down = dot(activated, cotangent[...], ((0,), (0,))).astype(BF)

    @pl.when(first)
    def _():
        grad_down_theirs[...] = grad_down

    @pl.when(jnp.logical_not(first))
    def _():
        grad_down_mine[...] = grad_down

    for which, ref in ((here, grad_wide_mine), (1 - here, grad_wide_theirs)):
        turned = flipped[place(which, half), :]
        ref[:, :CHUNK] = dot(turned, d_gate).astype(BF)
        ref[:, CHUNK:] = dot(turned, d_up).astype(BF)

    @pl.when(step == count - 1)
    def _():
        output[...] = out_sum[...].astype(BF)
        joined = middle[...]
        d_joined, d_gain_ff = norm_back(joined, inverse_rms(joined), gains[3:4], d_normed[...])
        d_joined = cotangent[...].astype(F32) + d_joined
        d_middle[...] = d_joined
        attn = attn_branch[...]
        d_attn, d_gain_attn = norm_back(attn, inverse_rms(attn), gains[1:2], 0.5 * d_joined)
        d_attn_low = d_attn.astype(BF)
        d_attn_branch[...] = d_attn_low
        ssm = ssm_branch[...]
        d_ssm, d_gain_ssm = norm_back(ssm, inverse_rms(ssm), gains[2:3], 0.5 * d_joined)
        d_ssm_low = d_ssm.astype(BF)
        d_ssm_branch[...] = d_ssm_low
        gain_grads[...] = jnp.concatenate(
            [d_gain_attn, d_gain_ssm, d_gain_ff, jnp.zeros((5, width), F32)]
        )
        for which, attn_weight, ssm_weight in (
            (here, attn_mine, ssm_mine),
            (1 - here, attn_theirs, ssm_theirs),
        ):
            d_attended[:, place(which, attn_half)] = dot(d_attn_low, attn_weight[...], flat).astype(BF)
            d_gated[:, place(which, ssm_half)] = dot(d_ssm_low, ssm_weight[...], flat).astype(BF)


def run_middle(position, tokens, attended, gated, cotangent, gains, attn, ssm, gate, up, down):
    rows, width = tokens.shape
    half = width // 2
    hidden = gate[0].shape[1]
    count = hidden // CHUNK
    fixed = lambda shape: pl.BlockSpec(shape, lambda step, place: (0,) * len(shape))

    def chunk(step, place):
        first = step < count // 2
        return jnp.where(first, 1 - place[0], place[0]) * (count // 2) + step % (count // 2)

    sliding = pl.BlockSpec((half, CHUNK), lambda step, place: (0, chunk(step, place)))
    early = lambda step, place: (jnp.minimum(step, count // 2 - 1), 0)
    late = lambda step, place: (jnp.maximum(step - count // 2, 0), 0)
    wide = pl.BlockSpec((half, 2 * CHUNK), lambda step, place: (0, chunk(step, place)))
    low = lambda shape: jax.ShapeDtypeStruct(shape, BF)
    full = lambda shape: jax.ShapeDtypeStruct(shape, F32)
    return pl.pallas_call(
        middle_kernel,
        grid_spec=pltpu.PrefetchScalarGridSpec(
            num_scalar_prefetch=1,
            grid=(count,),
            in_specs=[
                *[fixed(item.shape) for item in (tokens, attended, gated, cotangent, gains)],
                *[fixed(item.shape) for item in (*attn, *ssm)],
                *[sliding] * 4,
                pl.BlockSpec((CHUNK, width), late),
                pl.BlockSpec((CHUNK, width), early),
            ],
            out_specs=[
                *[fixed((rows, width))] * 4,
                fixed(attended.shape),
                fixed(gated.shape),
                fixed((8, width)),
                pl.BlockSpec((CHUNK, width), early),
                pl.BlockSpec((CHUNK, width), late),
                wide,
                wide,
            ],
            scratch_shapes=[
                *[pltpu.VMEM((rows, width), F32)] * 3,
                pltpu.VMEM((rows, width), BF),
                pltpu.VMEM((width, rows), BF),
                *[pltpu.VMEM((rows, width), F32)] * 2,
            ],
        ),
        out_shape=[
            low((rows, width)),
            full((rows, width)),
            low((rows, width)),
            low((rows, width)),
            low(attended.shape),
            low(gated.shape),
            full((8, width)),
            low((hidden // 2, width)),
            low((hidden // 2, width)),
            low((half, 2 * hidden)),
            low((half, 2 * hidden)),
        ],
        compiler_params=params_of(LARGE_LIMIT),
        cost_estimate=LONG,
        name="middle",
    )(position, tokens, attended, gated, cotangent, gains, *attn, *ssm, *gate, *up, *down)


def outs_grads_kernel(
    position, attended, gated, normed, d_attn, d_ssm, d_gate, theirs, mine
):
    here = position[0]
    step = pl.program_id(0)
    which = jnp.where(step == 0, 1 - here, here)
    rows = theirs.shape[0]
    down = ((0,), (0,))

    def write(ref):
        at = 0
        for left, right in ((attended, d_attn), (gated, d_ssm), (normed, d_gate)):
            half = left.shape[1] // 2
            for begin in range(0, half, rows):
                turned = left[:, pl.ds(pl.multiple_of(which * half + begin, rows), rows)]
                ref[:, at : at + right.shape[1]] = dot(turned, right[...], down).astype(BF)
                at += right.shape[1]

    @pl.when(step == 0)
    def _():
        write(theirs)

    @pl.when(step == 1)
    def _():
        write(mine)


def run_outs_grads(position, attended, gated, normed, d_attn, d_ssm, d_gate):
    inputs = (attended, gated, normed, d_attn, d_ssm, d_gate)
    rows = attended.shape[1] // 2
    width = sum(
        left.shape[1] // 2 // rows * right.shape[1] for left, right in zip(inputs[:3], inputs[3:])
    )
    fixed = lambda shape: pl.BlockSpec(shape, lambda step, place: (0, 0))
    return pl.pallas_call(
        outs_grads_kernel,
        grid_spec=pltpu.PrefetchScalarGridSpec(
            num_scalar_prefetch=1,
            grid=(2,),
            in_specs=[fixed(item.shape) for item in inputs],
            out_specs=[fixed((rows, width))] * 2,
        ),
        out_shape=[jax.ShapeDtypeStruct((rows, width), BF)] * 2,
        compiler_params=params_of(),
        cost_estimate=COST,
        name="outs_grads",
    )(position, *inputs)


def early_back_kernel(
    position,
    d_query,
    d_kv,
    d_gate,
    query_mine,
    query_theirs,
    kv_mine,
    kv_theirs,
    ssm_mine,
    ssm_theirs,
    d_normed,
):
    here = position[0]
    half = d_normed.shape[1] // 2
    flat = ((1,), (1,))
    for which, query, kv, ssm in (
        (here, query_mine, kv_mine, ssm_mine),
        (1 - here, query_theirs, kv_theirs, ssm_theirs),
    ):
        d_normed[:, pl.ds(pl.multiple_of(which * half, half), half)] = (
            dot(d_query[...], query[...], flat)
            + dot(d_kv[...], kv[...], flat)
            + dot(d_gate[...], ssm[...], flat)
        )


def run_early_back(position, d_query, d_kv, d_gate, query, kv, ssm):
    rows = d_query.shape[0]
    half = query[0].shape[0]
    fixed = lambda shape: pl.BlockSpec(shape, lambda step, place: (0, 0))
    return pl.pallas_call(
        early_back_kernel,
        grid_spec=pltpu.PrefetchScalarGridSpec(
            num_scalar_prefetch=1,
            grid=(1,),
            in_specs=[
                *[fixed(item.shape) for item in (d_query, d_kv, d_gate, *query, *kv)],
                *[pl.BlockSpec((half, INNER), lambda step, place: (0, 1))] * 2,
            ],
            out_specs=fixed((rows, 2 * half)),
        ),
        out_shape=jax.ShapeDtypeStruct((rows, 2 * half), F32),
        compiler_params=params_of(),
        cost_estimate=COST,
        name="early_back",
    )(position, d_query, d_kv, d_gate, *query, *kv, *ssm)


def rest_grads_kernel(
    position, normed, d_query, d_kv, d_mixed, d_aux, gain_grads, d_heads, theirs, mine
):
    here = position[0]
    step = pl.program_id(0)
    half = normed.shape[1] // 2
    which = jnp.where(step == 0, 1 - here, here)
    turned = normed[:, pl.ds(pl.multiple_of(which * half, half), half)]

    def write(ref):
        at = 0
        for right in (d_query, d_kv, d_mixed):
            ref[:, at : at + right.shape[1]] = dot(turned, right[...], ((0,), (0,))).astype(BF)
            at += right.shape[1]
        gains = gain_grads[0:3, pl.ds(pl.multiple_of(which * half, half), half)]
        heads = jnp.concatenate([d_heads[0:1, :], d_heads[1:2, :]], axis=1)
        heads = jnp.concatenate([heads, jnp.zeros((1, half - heads.shape[1]), F32)], axis=1)
        before = 2 * STATE + SH
        columns = jnp.concatenate(
            [
                jnp.zeros((before, half), F32),
                gains,
                heads,
                jnp.zeros((d_aux.shape[1] - before - 4, half), F32),
            ]
        ).T
        ref[:, at:] = (dot(turned, d_aux[...], ((0,), (0,))) + columns).astype(BF)

    @pl.when(step == 0)
    def _():
        write(theirs)

    @pl.when(step == 1)
    def _():
        write(mine)


def run_rest_grads(position, *inputs):
    half = inputs[0].shape[1] // 2
    total = sum(item.shape[1] for item in inputs[1:5])
    fixed = lambda shape: pl.BlockSpec(shape, lambda step, place: (0, 0))
    return pl.pallas_call(
        rest_grads_kernel,
        grid_spec=pltpu.PrefetchScalarGridSpec(
            num_scalar_prefetch=1,
            grid=(2,),
            in_specs=[fixed(item.shape) for item in inputs],
            out_specs=[fixed((half, total))] * 2,
        ),
        out_shape=[jax.ShapeDtypeStruct((half, total), BF)] * 2,
        compiler_params=params_of(),
        cost_estimate=COST,
        name="rest_grads",
    )(position, *inputs)


def late_back_kernel(
    position,
    tokens,
    gains,
    d_middle,
    d_normed,
    d_mixed,
    d_aux,
    aux_mine,
    aux_theirs,
    ssm_mine,
    ssm_theirs,
    grad_tokens,
    total,
):
    here = position[0]
    half = tokens.shape[1] // 2
    for which, aux, ssm in ((here, aux_mine, ssm_mine), (1 - here, aux_theirs, ssm_theirs)):
        columns = pl.ds(pl.multiple_of(which * half, half), half)
        total[:, columns] = (
            d_normed[:, columns]
            + dot(d_mixed[...], ssm[...], ((1,), (1,)))
            + dot(d_aux[:, : aux.shape[0]], aux[...])
        )
    hidden = tokens[...].astype(F32)
    d_hidden, _ = norm_back(hidden, inverse_rms(hidden), gains[0:1], total[...])
    grad_tokens[...] = d_middle[...] + d_hidden


def run_late_back(position, tokens, gains, d_middle, d_normed, d_mixed, d_aux, aux, ssm):
    rows, width = tokens.shape
    half = width // 2
    fixed = lambda shape: pl.BlockSpec(shape, lambda step, place: (0, 0))
    inputs = (tokens, gains, d_middle, d_normed, d_mixed, d_aux, *aux)
    return pl.pallas_call(
        late_back_kernel,
        grid_spec=pltpu.PrefetchScalarGridSpec(
            num_scalar_prefetch=1,
            grid=(1,),
            in_specs=[
                *[fixed(item.shape) for item in inputs],
                *[pl.BlockSpec((half, INNER), lambda step, place: (0, 0))] * 2,
            ],
            out_specs=fixed((rows, width)),
            scratch_shapes=[pltpu.VMEM((rows, width), F32)],
        ),
        out_shape=jax.ShapeDtypeStruct((rows, width), F32),
        compiler_params=params_of(),
        cost_estimate=COST,
        name="late_back",
    )(position, *inputs, *ssm)


def local(
    tokens,
    cotangent,
    doc_blocks,
    gain_in,
    w_query,
    w_kv,
    w_attn_out,
    gain_attn,
    w_ssm_in,
    w_ssm_aux,
    dt_bias,
    decay_log,
    w_ssm_out,
    gain_ssm,
    gain_ff,
    w_gate,
    w_up,
    w_down,
):
    rows, width = tokens.shape
    half = width // 2
    position = lax.axis_index("shard")
    here = position.astype(jnp.int32).reshape(1)
    blocks_here = rows // BLOCK
    docs = doc_blocks[0]
    here_docs = lax.dynamic_slice_in_dim(docs, position * blocks_here, blocks_here, 0)
    prior_docs = jnp.where(position > 0, docs[:blocks_here], -1)
    earlier = jnp.concatenate([prior_docs[-1:], here_docs[:-1]])
    resets = (here_docs != earlier).astype(jnp.int32)
    key_docs = jnp.repeat(jnp.concatenate([prior_docs, here_docs]), BLOCK)
    bias = jnp.where(here_docs[:, None] == key_docs[None, :], 0.0, NEGATIVE)
    lane_pad = LANES - SH
    dt_row = jnp.pad(dt_bias, (0, lane_pad))[None]
    decay_row = jnp.pad(decay_log, (0, lane_pad))[None]

    gain_first = natural(gain_in, swap(gain_in), position, 0).astype(F32)[None]
    query = (w_query, swap(w_query))
    kv = (w_kv, swap(w_kv))
    aux_in = (w_ssm_aux.T, swap(w_ssm_aux.T))
    ssm_in = (w_ssm_in, swap(after(w_ssm_in, kv[1])))
    attn_out, ssm_back, gate, up, down = (
        (weight, swap(weight)) for weight in (w_attn_out, w_ssm_out, w_gate, w_up, w_down)
    )
    normed, scaled_queries, key_vals, aux, tails, carries = run_project_small(
        here, tokens, gain_first, dt_row, decay_row, query, kv, aux_in
    )
    key_prior = lax.ppermute(key_vals, "shard", [(0, 1)])
    later_gains = [
        natural(gain, swap(gain), position, 0).astype(F32)[None]
        for gain in (gain_attn, gain_ssm, gain_ff)
    ]
    gains_all = jnp.concatenate([gain_first, *later_gains, jnp.zeros((4, width), F32)])
    mixed, state_end = run_project(here, resets, normed, aux, tails, carries, ssm_in)
    state_prior = lax.ppermute(state_end, "shard", [(0, 1)])
    attended, log_total = run_attend(scaled_queries, key_prior, key_vals, bias)
    ssm_out, gated, states = run_forward(resets, mixed, aux, dt_row, decay_row, state_prior)

    (
        output,
        d_middle,
        d_attn_low,
        d_ssm_low,
        d_attended,
        d_gated,
        gain_grads,
        down_theirs,
        down_mine,
        wide_theirs,
        wide_mine,
    ) = run_middle(
        here, tokens, attended, gated, cotangent, gains_all, attn_out, ssm_back, gate, up, down
    )
    sums = {
        "down": Stream([down_mine, swap(down_theirs)], WHOLE["down"], *LINKS["down"]),
        "wide": Stream([wide_mine, swap(wide_theirs)], WHOLE["wide"], *LINKS["wide"]),
    }
    token = wide_theirs
    made = {}
    outs_rows = w_attn_out.shape[0]
    full = lambda *shape: jax.ShapeDtypeStruct(shape, F32)
    ssm_pieces = w_ssm_out.shape[0] // outs_rows
    gate_at = width * (1 + ssm_pieces)
    aux_at = AUX_AT + INNER
    spare = aux_at + 2 * STATE + SH
    wide_pieces = [
        [
            (column, 2 * column + offset, 2 * column + offset + CHUNK)
            for column in range(0, w_gate.shape[1], CHUNK)
        ]
        for offset in (0, CHUNK)
    ]
    layouts = {
        "down": [(full(*w_down.shape), width, [(0, 0, width)])],
        "wide": [(full(half, w_gate.shape[1]), w_gate.shape[1], pieces) for pieces in wide_pieces],
        "outs": [
            (full(outs_rows, width), width, [(0, 0, width)]),
            (
                full(ssm_pieces, outs_rows, width),
                width,
                [(piece, width * (1 + piece), width * (2 + piece)) for piece in range(ssm_pieces)],
            ),
            (
                full(half // outs_rows, outs_rows, 2 * INNER),
                INNER,
                [
                    (piece, gate_at + INNER * piece, gate_at + INNER * (piece + 1))
                    for piece in range(half // outs_rows)
                ],
            ),
        ],
        "rest": [
            (full(half, KV_AT), KV_AT, [(0, 0, KV_AT)]),
            (full(half, AUX_AT - KV_AT), AUX_AT - KV_AT, [(0, KV_AT, AUX_AT)]),
            (full(spare - aux_at, half), 3 * LANES, [(TURNED, aux_at, spare)]),
            (full(8, half), 3 * LANES, [(TURNED, spare, spare + 8)]),
            (full(half, 2 * INNER), INNER, [(0, AUX_AT, aux_at)]),
        ],
    }
    def closed(value, number):
        if number + 1 == len(PLAN) or PLAN[number + 1] not in layouts:
            return value
        names = []
        for name in PLAN[number + 1 :]:
            if name not in layouts:
                break
            names.append(name)
        waits = [
            stream.latest()
            for name, stream in sums.items()
            if stream.steps
            and (name in names or stream.gone > 1 or (stream.gone == 1 and name == "down"))
        ]
        return fence(value, *waits)

    d_kv = ssm_in_grad = None
    halves = {}
    rest_weights = (w_query, w_kv, w_ssm_aux.T, None, w_ssm_in)

    def key_grads(made_before):
        if made_before is not None:
            return made_before
        return (d_here + after(d_prior_got, token).astype(F32)).astype(BF)

    def go_on(name):
        nonlocal token, ssm_in_grad
        stream = sums[name]
        stream.hold(token)
        weights = rest_weights if name == "rest" else ()
        place = {"outs": 2, "rest": 4}.get(name)
        shape = layouts[name][place][0].shape if place is not None else None
        if stream.steps:
            stream.prepare()
            token = stream.operand
            stream.go()
            if name == "rest" and not stream.steps and stream.got is not None:
                held = None if ssm_in_grad is None else ssm_in_grad.reshape(shape)
                halves[name] = stream.finish(layouts[name], held, weights, 0)
                if halves[name] is not None:
                    halves[name] = list(halves[name])
                    ssm_in_grad = halves[name][place]
        elif name not in made:
            held = None if place is None or ssm_in_grad is None else ssm_in_grad.reshape(shape)
            if halves.get(name) is not None:
                halves[name][place] = held
                made[name] = stream.finish(layouts[name], None, weights, 1, halves[name])
            else:
                made[name] = stream.finish(layouts[name], held, weights)
            token = made[name][0]
            if place is not None:
                ssm_in_grad = made[name][place].reshape(half, 2 * INNER)

    for number, name in enumerate(PLAN):
        if name in layouts:
            go_on(name)
        elif name == "state":
            d_state_start, d_mixed_gate = run_state_back(
                resets, after(d_gated, token), mixed, aux, ssm_out, dt_row, decay_row
            )
            token = closed(d_state_start, number)
            d_state_end = lax.ppermute(token, "shard", [(1, 0)])
        elif name == "grads":
            outs_theirs, outs_mine = run_outs_grads(
                here, after(attended, token), gated, normed, d_attn_low, d_ssm_low, d_mixed_gate
            )
            token = closed(outs_theirs, number)
            sums["outs"] = Stream([outs_mine, swap(token)], WHOLE["outs"], *LINKS["outs"])
        elif name == "attend":
            d_query, d_prior, d_here = run_attend_back(
                scaled_queries, key_prior, key_vals, bias, log_total, after(d_attended, token)
            )
            token = closed(d_prior, number)
            d_prior_got = lax.ppermute(token, "shard", [(1, 0)])
        elif name == "scan":
            d_mixed, d_aux, d_heads = run_backward(
                resets,
                after(d_gated, token),
                mixed,
                aux,
                ssm_out,
                states,
                dt_row,
                decay_row,
                d_state_end,
            )
            token = d_heads = closed(d_heads, number)
        elif name == "sums":
            d_kv = key_grads(d_kv)
            rest_theirs, rest_mine = run_rest_grads(
                here, normed, d_query, d_kv, d_mixed, d_aux, gain_grads, d_heads
            )
            token = closed(rest_theirs, number)
            sums["rest"] = Stream([rest_mine, swap(token)], WHOLE["rest"], *LINKS["rest"])
        elif name == "early":
            d_kv = key_grads(d_kv)
            d_normed = run_early_back(
                here, after(d_query, token), d_kv, d_mixed_gate, query, kv, ssm_in
            )
            token = d_normed
        elif name == "late":
            grad_tokens = run_late_back(
                here,
                tokens,
                gain_first,
                d_middle,
                d_normed,
                d_mixed,
                after(d_aux, token),
                aux_in,
                ssm_in,
            )
            token = grad_tokens

    for name in layouts:
        while name not in made:
            go_on(name)
    (grad_down,) = made["down"]
    grad_gate, grad_up = made["wide"]
    grad_attn_out, grad_ssm_out, _ = made["outs"]
    grad_query, grad_kv, grad_aux, extras, _, products = made["rest"]
    grad_ssm_in = ssm_in_grad
    gate_products = jnp.sum(
        w_ssm_in[:, INNER:].astype(F32) * grad_ssm_in[:, INNER:], axis=1
    )
    grad_gain_in = (products[0] + gate_products) / gain_in.astype(F32)
    return (
        output,
        grad_tokens,
        grad_gain_in,
        grad_query,
        grad_kv,
        grad_attn_out,
        extras[0],
        grad_ssm_in,
        grad_aux.T,
        extras[3, :SH],
        extras[3, LANES : LANES + SH],
        grad_ssm_out.reshape(w_ssm_out.shape),
        extras[1],
        extras[2],
        grad_gate,
        grad_up,
        grad_down,
    )


def solution(mesh):
    halves = P("shard", None)
    half = P("shard")
    tokens = P(("rep", "shard"), None)
    return jax.shard_map(
        local,
        mesh=mesh,
        in_specs=(
            tokens,
            tokens,
            P("rep", None),
            half,
            halves,
            halves,
            halves,
            half,
            halves,
            halves,
            P(),
            P(),
            halves,
            half,
            half,
            halves,
            halves,
            halves,
        ),
        out_specs=(
            tokens,
            tokens,
            half,
            halves,
            halves,
            halves,
            half,
            halves,
            halves,
            P(),
            P(),
            halves,
            half,
            half,
            halves,
            halves,
            halves,
        ),
        check_vma=False,
    )
```

```python
import functools

import jax
import jax.numpy as jnp
from jax import lax
from jax.experimental import pallas as pl
from jax.experimental.pallas import tpu as pltpu
from jax.sharding import PartitionSpec as P

HD = 64
QH = 8
KVH = 2
SH = 24
SP = 64
STATE = 128
BLOCK = 128
INNER = 1536
LANES = 128
KV_AT = QH * HD
X, Y, Z, ZZ = 0, 1, 2, 3
TURNED = -1
WHOLE = {"down": 2, "wide": 1, "outs": 1, "rest": 2}
LINKS = {
    "down": ((Z, Y, ZZ, X), (Z, X, Y, ZZ)),
    "wide": ((X, Y, ZZ, Z), (Y, X, Z, ZZ)),
    "outs": ((Z, Y, X, ZZ), (Y, X, Z, ZZ)),
    "rest": ((X, Z, Y, ZZ), (Y, X, Z, ZZ)),
}
PLAN = (
    "state",
    "wide",
    "down",
    "attend",
    "grads",
    "wide",
    "down",
    "scan",
    "outs",
    "wide",
    "sums",
    "early",
    "down",
    "outs",
    "wide",
    "rest",
    "down",
    "outs",
    "wide",
    "rest",
    "down",
    "outs",
    "wide",
    "rest",
    "down",
    "outs",
    "wide",
    "rest",
    "down",
    "outs",
    "late",
    "wide",
    "rest",
    "outs",
    "rest",
    "outs",
    "rest",
)
AUX_AT = KV_AT + 2 * KVH * HD
EPSILON = 1e-05
NEGATIVE = -1e30
BF = jnp.bfloat16
F32 = jnp.float32
SWAP = [(0, 1), (1, 0)]
VMEM_LIMIT = 30 * 1024 * 1024
LARGE_LIMIT = 50 * 1024 * 1024
WHOLE_LIMIT = 60 * 1024 * 1024
LONG = pl.CostEstimate(flops=15_000_000_000, bytes_accessed=1_000_000, transcendentals=0)
COST = pl.CostEstimate(flops=1_000_000, bytes_accessed=1_000_000, transcendentals=0)


def dot(left, right, over=((1,), (0,))):
    return lax.dot_general(left, right, (over, ((), ())), preferred_element_type=F32)


def split2(value):
    high = value.astype(BF)
    return high, (value - high.astype(F32)).astype(BF)


def split3(value):
    high = value.astype(BF)
    rest = value - high.astype(F32)
    middle = rest.astype(BF)
    return high, middle, (rest - middle.astype(F32)).astype(BF)


def dot3(left, right, over=((1,), (0,))):
    left_high, left_low = split2(left)
    right_high, right_low = split2(right)
    return dot(left_high, right_high, over) + (
        dot(left_high, right_low, over) + dot(left_low, right_high, over)
    )


def dot1(left, right, over=((1,), (0,))):
    return dot(left.astype(BF), right.astype(BF), over)


def spread(value, begin=0, end=SH):
    first_half = lax.broadcasted_iota(jnp.int32, (value.shape[0], LANES), 1) < SP
    return jnp.concatenate(
        [
            jnp.where(first_half, value[:, head : head + 1], value[:, head + 1 : head + 2])
            for head in range(begin, end, 2)
        ],
        axis=1,
    )


def gather_heads(*values):
    parts = [part for value in values for part in split2(value)]
    sums = dot(jnp.concatenate(parts), head_ones(), ((1,), (1,)))
    found, row = [], 0
    for value in values:
        rows = value.shape[0]
        found.append(sums[row : row + rows] + sums[row + rows : row + 2 * rows])
        row += 2 * rows
    return found


def head_ones():
    head = lax.broadcasted_iota(jnp.int32, (LANES, INNER), 0)
    column = lax.broadcasted_iota(jnp.int32, (LANES, INNER), 1)
    return ((column >= head * SP) & (column < (head + 1) * SP)).astype(BF)


def lower_ones():
    rows = lax.broadcasted_iota(jnp.int32, (BLOCK, BLOCK), 0)
    columns = lax.broadcasted_iota(jnp.int32, (BLOCK, BLOCK), 1)
    return rows >= columns


def cumulate(value, lower, over):
    high, middle, low = split3(value)
    return dot(lower, high, over) + (dot(lower, middle, over) + dot(lower, low, over))


def decays(aux, dt_bias, rate):
    raw = aux[:, 2 * STATE :] + dt_bias
    step = jnp.maximum(raw, 0.0) + jnp.log1p(jnp.exp(-jnp.abs(raw)))
    log_decay = -step * rate
    cumulated = cumulate(log_decay, lower_ones().astype(BF), ((1,), (0,)))
    return raw, step, log_decay, cumulated


def forward_kernel(
    resets, mixed, gate, aux, dt_bias, decay_log, state_in, ssm_out, gated, states, state
):
    number = pl.program_id(0)

    @pl.when(number == 0)
    def _():
        state[...] = state_in[...]

    @pl.when(resets[number] != 0)
    def _():
        state[...] = jnp.zeros_like(state)

    aux_now = aux[...]
    b_in = aux_now[:, :STATE]
    c_out = aux_now[:, STATE : 2 * STATE]
    _, step, _, cumulated = decays(aux_now, dt_bias[...], jnp.exp(decay_log[...]))
    scaled = mixed[...].astype(F32) * spread(step)
    wide = spread(cumulated)
    tail = jnp.exp(wide[BLOCK - 1 :, :] - wide)
    grown = jnp.exp(wide)
    before = state[...]
    states[...] = before[None].astype(BF)
    state[...] = grown[BLOCK - 1 :, :] * before + dot1(b_in, scaled * tail, ((0,), (0,)))
    outer = grown * dot1(c_out, before)
    both = dot3(c_out, b_in, ((1,), (1,)))
    lower = lower_ones()
    flipped = cumulated.T
    first_half = lax.broadcasted_iota(jnp.int32, (BLOCK, LANES), 1) < SP
    scaled_low = scaled.astype(BF)
    zero = jnp.zeros((BLOCK, LANES), BF)
    for pair in range(SH // 2):
        weights = []
        for head in (2 * pair, 2 * pair + 1):
            spread_now = cumulated[:, head : head + 1] - flipped[head : head + 1, :]
            weights.append((jnp.exp(jnp.where(lower, spread_now, NEGATIVE)) * both).astype(BF))
        columns = slice(pair * LANES, (pair + 1) * LANES)
        low = scaled_low[:, columns]
        low = jnp.concatenate([jnp.where(first_half, low, zero), jnp.where(first_half, zero, low)])
        inner = dot(jnp.concatenate(weights, axis=1), low)
        total = inner + outer[:, columns]
        ssm_out[:, columns] = total
        gate_now = gate[:, columns].astype(F32)
        gated[:, columns] = (total * (gate_now / (1.0 + jnp.exp(-gate_now)))).astype(BF)


def silu_of(gate):
    chance = 1.0 / (1.0 + jnp.exp(-gate))
    return gate * chance, chance


def state_back_kernel(
    resets, d_gated, gate, aux, ssm_out, dt_bias, decay_log, d_state_out, d_gate, d_state
):
    number = pl.num_programs(0) - 1 - pl.program_id(0)

    @pl.when(pl.program_id(0) == 0)
    def _():
        d_state[...] = jnp.zeros_like(d_state)

    aux_now = aux[...]
    _, _, _, cumulated = decays(aux_now, dt_bias[...], jnp.exp(decay_log[...]))
    grown = spread(jnp.exp(cumulated))
    gate_silu, chance = silu_of(gate[...].astype(F32))
    d_gated_now = d_gated[...].astype(F32)
    d_gate[...] = (d_gated_now * ssm_out[...] * (chance + gate_silu * (1.0 - chance))).astype(BF)
    d_grown = d_gated_now * gate_silu * grown
    c_out = aux_now[:, STATE : 2 * STATE]
    d_state[...] = grown[BLOCK - 1 :, :] * d_state[...] + dot1(c_out, d_grown, ((0,), (0,)))

    @pl.when(resets[number] != 0)
    def _():
        d_state[...] = jnp.zeros_like(d_state)

    d_state_out[...] = d_state[...].astype(BF)


def backward_kernel(
    resets,
    d_gated,
    mixed,
    gate,
    aux,
    ssm_out,
    states,
    dt_bias,
    decay_log,
    d_state_in,
    d_mixed,
    d_aux,
    d_heads,
    d_state,
):
    number = pl.num_programs(0) - 1 - pl.program_id(0)

    @pl.when(pl.program_id(0) == 0)
    def _():
        d_state[...] = d_state_in[...].astype(F32)
        d_heads[...] = jnp.zeros_like(d_heads)

    lower = lower_ones()
    aux_now = aux[...]
    b_in = aux_now[:, :STATE]
    c_out = aux_now[:, STATE : 2 * STATE]
    rate = jnp.exp(decay_log[...])
    raw, step, log_decay, cumulated = decays(aux_now, dt_bias[...], rate)
    step_wide = spread(step)
    mixed_now = mixed[...].astype(F32)
    scaled = mixed_now * step_wide
    wide = spread(cumulated)
    tail = jnp.exp(wide[BLOCK - 1 :, :] - wide)
    grown = jnp.exp(wide)
    gate_now = gate[...].astype(F32)
    gate_silu, _ = silu_of(gate_now)
    d_gated_now = d_gated[...].astype(F32)
    ssm_now = ssm_out[...]
    d_out = d_gated_now * gate_silu
    before = states[0].astype(F32)
    d_after = d_state[...]
    d_grown = d_out * grown
    d_c = dot1(d_grown, before, ((1,), (1,)))
    d_before = grown[BLOCK - 1 :, :] * d_after + dot1(c_out, d_grown, ((0,), (0,)))
    tailed = scaled * tail
    d_b = dot1(tailed, d_after, ((1,), (1,)))
    d_tailed = dot1(b_in, d_after)
    ends = jnp.sum(tailed * d_tailed, axis=0, keepdims=True) + grown[BLOCK - 1 :, :] * jnp.sum(
        d_after * before, axis=0, keepdims=True
    )
    both = dot3(c_out, b_in, ((1,), (1,)))
    flipped = cumulated.T
    first_half = lax.broadcasted_iota(jnp.int32, (BLOCK, LANES), 1) < SP
    scaled_low = scaled.astype(BF)
    d_low = d_out.astype(BF)
    zero = jnp.zeros((BLOCK, LANES), BF)
    d_both = jnp.zeros((BLOCK, BLOCK), F32)
    parts = []
    for pair in range(SH // 2):
        columns = slice(pair * LANES, (pair + 1) * LANES)
        falls = []
        for head in (2 * pair, 2 * pair + 1):
            spread_now = cumulated[:, head : head + 1] - flipped[head : head + 1, :]
            falls.append(jnp.exp(jnp.where(lower, spread_now, NEGATIVE)))
        weight = jnp.concatenate([(falls[0] * both).astype(BF), (falls[1] * both).astype(BF)])
        low = d_low[:, columns]
        low = jnp.concatenate([jnp.where(first_half, low, zero), jnp.where(first_half, zero, low)])
        d_weight = dot(low, scaled_low[:, columns], ((1,), (1,)))
        d_both = d_both + falls[0] * d_weight[:BLOCK] + falls[1] * d_weight[BLOCK:]
        parts.append(dot(weight, low, ((0,), (0,))))
    d_inner = jnp.concatenate(parts, axis=1)
    carried = tail * d_tailed
    d_scaled = d_inner + carried
    d_mixed[...] = (d_scaled * step_wide).astype(BF)
    d_step, d_cumulated, d_last = gather_heads(
        d_scaled * mixed_now,
        d_low.astype(F32) * ssm_now - scaled_low.astype(F32) * d_inner - scaled * carried,
        jnp.broadcast_to(ends, (8, INNER)),
    )
    d_decay = cumulate(d_cumulated, lower.astype(BF), ((0,), (0,))) + d_last[:1]
    d_raw = (d_step - d_decay * rate) * (1.0 / (1.0 + jnp.exp(-raw)))
    real = lax.broadcasted_iota(jnp.int32, (BLOCK, LANES), 1) < SH
    d_raw = jnp.where(real, d_raw, 0.0)
    d_c = d_c + dot1(d_both, b_in)
    d_b = d_b + dot1(d_both, c_out, ((0,), (0,)))
    d_aux[...] = jnp.concatenate([d_b, d_c, d_raw], axis=1).astype(BF)
    d_heads[...] += jnp.concatenate(
        [
            jnp.sum(d_raw, axis=0, keepdims=True),
            jnp.sum(jnp.where(real, d_decay * log_decay, 0.0), axis=0, keepdims=True),
            jnp.zeros((6, LANES), F32),
        ]
    )
    d_state[...] = d_before

    @pl.when(resets[number] != 0)
    def _():
        d_state[...] = jnp.zeros_like(d_state)


def scalars():
    return pl.BlockSpec(memory_space=pltpu.SMEM)


def whole(shape):
    return pl.BlockSpec(shape, lambda number: (0,) * len(shape))


def params_of(limit=VMEM_LIMIT):
    return pltpu.CompilerParams(dimension_semantics=("arbitrary",), vmem_limit_bytes=limit)


def run_forward(resets, mixed, aux, dt_bias, decay_log, state_in):
    rows = mixed.shape[0]
    count = rows // BLOCK
    return pl.pallas_call(
        forward_kernel,
        grid=(count,),
        in_specs=[
            scalars(),
            pl.BlockSpec((BLOCK, INNER), lambda number: (number, 0)),
            pl.BlockSpec((BLOCK, INNER), lambda number: (number, 1)),
            pl.BlockSpec((BLOCK, 3 * LANES), lambda number: (number, 0)),
            whole((1, LANES)),
            whole((1, LANES)),
            whole((STATE, INNER)),
        ],
        out_specs=[
            pl.BlockSpec((BLOCK, INNER), lambda number: (number, 0)),
            pl.BlockSpec((BLOCK, INNER), lambda number: (number, 0)),
            pl.BlockSpec((1, STATE, INNER), lambda number: (number, 0, 0)),
        ],
        out_shape=[
            jax.ShapeDtypeStruct((rows, INNER), F32),
            jax.ShapeDtypeStruct((rows, INNER), BF),
            jax.ShapeDtypeStruct((count, STATE, INNER), BF),
        ],
        scratch_shapes=[pltpu.VMEM((STATE, INNER), F32)],
        compiler_params=params_of(),
        cost_estimate=LONG,
        name="ssm_forward",
    )(resets, mixed, mixed, aux, dt_bias, decay_log, state_in)


def run_state_back(resets, d_gated, mixed, aux, ssm_out, dt_bias, decay_log):
    count = mixed.shape[0] // BLOCK
    turned = lambda number: (count - 1 - number, 0)
    return pl.pallas_call(
        state_back_kernel,
        grid=(count,),
        in_specs=[
            scalars(),
            pl.BlockSpec((BLOCK, INNER), turned),
            pl.BlockSpec((BLOCK, INNER), lambda number: (count - 1 - number, 1)),
            pl.BlockSpec((BLOCK, 3 * LANES), turned),
            pl.BlockSpec((BLOCK, INNER), turned),
            whole((1, LANES)),
            whole((1, LANES)),
        ],
        out_specs=[whole((STATE, INNER)), pl.BlockSpec((BLOCK, INNER), turned)],
        out_shape=[
            jax.ShapeDtypeStruct((STATE, INNER), BF),
            jax.ShapeDtypeStruct((mixed.shape[0], INNER), BF),
        ],
        scratch_shapes=[pltpu.VMEM((STATE, INNER), F32)],
        compiler_params=params_of(WHOLE_LIMIT),
        cost_estimate=COST,
        name="ssm_state_back",
    )(resets, d_gated, mixed, aux, ssm_out, dt_bias, decay_log)


def run_backward(resets, d_gated, mixed, aux, ssm_out, states, dt_bias, decay_log, d_state_in):
    rows = mixed.shape[0]
    count = rows // BLOCK
    turned = lambda number: (count - 1 - number, 0)
    return pl.pallas_call(
        backward_kernel,
        grid=(count,),
        in_specs=[
            scalars(),
            pl.BlockSpec((BLOCK, INNER), turned),
            pl.BlockSpec((BLOCK, INNER), turned),
            pl.BlockSpec((BLOCK, INNER), lambda number: (count - 1 - number, 1)),
            pl.BlockSpec((BLOCK, 3 * LANES), turned),
            pl.BlockSpec((BLOCK, INNER), turned),
            pl.BlockSpec((1, STATE, INNER), lambda number: (count - 1 - number, 0, 0)),
            whole((1, LANES)),
            whole((1, LANES)),
            whole((STATE, INNER)),
        ],
        out_specs=[
            pl.BlockSpec((BLOCK, INNER), turned),
            pl.BlockSpec((BLOCK, 3 * LANES), turned),
            whole((8, LANES)),
        ],
        out_shape=[
            jax.ShapeDtypeStruct((rows, INNER), BF),
            jax.ShapeDtypeStruct((rows, 3 * LANES), BF),
            jax.ShapeDtypeStruct((8, LANES), F32),
        ],
        scratch_shapes=[pltpu.VMEM((STATE, INNER), F32)],
        compiler_params=params_of(),
        cost_estimate=COST,
        name="ssm_backward",
    )(resets, d_gated, mixed, mixed, aux, ssm_out, states, dt_bias, decay_log, d_state_in)


def head_rows(ref, start, group, width):
    return jnp.concatenate(
        [
            ref[start : start + BLOCK, (group * width + head) * HD : (group * width + head + 1) * HD]
            for head in range(width)
        ]
    )


def masked_scores(q_rows, k_rows, bias_row, lower, width):
    raw = dot(q_rows, k_rows, ((1,), (1,))) + bias_row
    edge = raw.shape[1] - BLOCK
    corner = jnp.where(jnp.concatenate([lower] * width), raw[:, edge:], NEGATIVE)
    return jnp.concatenate([raw[:, :edge], corner], axis=1)


def attend_kernel(q_ref, prior_ref, here_ref, bias_ref, out_ref, total_ref):
    width = QH // KVH
    rows = q_ref.shape[0]
    halo = prior_ref.shape[0]
    lower = lower_ones()
    for group in range(KVH):
        key_columns = slice(group * HD, (group + 1) * HD)
        value_columns = slice((KVH + group) * HD, (KVH + group + 1) * HD)
        keys = jnp.concatenate([prior_ref[:, key_columns], here_ref[:, key_columns]])
        values = jnp.concatenate([prior_ref[:, value_columns], here_ref[:, value_columns]])
        for block in range(rows // BLOCK):
            start = block * BLOCK
            reach = halo + start + BLOCK
            q_rows = head_rows(q_ref, start, group, width)
            scores = masked_scores(
                q_rows, keys[:reach], bias_ref[block : block + 1, :reach], lower, width
            )
            top = jnp.max(scores, axis=1, keepdims=True)
            powers = jnp.exp(scores - top)
            total = jnp.sum(powers, axis=1, keepdims=True)
            probs = (powers * (1.0 / total)).astype(BF)
            out = dot(probs, values[:reach])
            log_total = top + jnp.log(total)
            for head in range(width):
                place = group * width + head
                some = slice(head * BLOCK, (head + 1) * BLOCK)
                out_ref[start : start + BLOCK, place * HD : (place + 1) * HD] = out[some].astype(BF)
                total_ref[start : start + BLOCK, place : place + 1] = log_total[some]


def attend_back_kernel(
    q_ref, prior_ref, here_ref, bias_ref, total_ref, d_ref, dq_ref, d_prior_ref, d_here_ref, sums
):
    width = QH // KVH
    rows = q_ref.shape[0]
    halo = prior_ref.shape[0]
    lower = lower_ones()
    sums[...] = jnp.zeros_like(sums)
    for group in range(KVH):
        key_columns = slice(group * HD, (group + 1) * HD)
        value_columns = slice((KVH + group) * HD, (KVH + group + 1) * HD)
        keys = jnp.concatenate([prior_ref[:, key_columns], here_ref[:, key_columns]])
        values = jnp.concatenate([prior_ref[:, value_columns], here_ref[:, value_columns]])
        for block in range(rows // BLOCK):
            start = block * BLOCK
            reach = halo + start + BLOCK
            q_rows = head_rows(q_ref, start, group, width)
            d_rows = head_rows(d_ref, start, group, width)
            scores = masked_scores(
                q_rows, keys[:reach], bias_ref[block : block + 1, :reach], lower, width
            )
            log_total = jnp.concatenate(
                [
                    total_ref[start : start + BLOCK, group * width + head : group * width + head + 1]
                    for head in range(width)
                ]
            )
            probs = jnp.exp(scores - log_total)
            probs_low = probs.astype(BF)
            d_probs = dot(d_rows, values[:reach], ((1,), (1,)))
            weighed = probs * d_probs
            d_scores = (weighed - probs * jnp.sum(weighed, axis=1, keepdims=True)).astype(BF)
            d_queries = dot(d_scores, keys[:reach]) * HD**-0.5
            for head in range(width):
                place = group * width + head
                some = slice(head * BLOCK, (head + 1) * BLOCK)
                dq_ref[start : start + BLOCK, place * HD : (place + 1) * HD] = d_queries[some].astype(BF)
            sums[:reach, key_columns] += dot(d_scores, q_rows, ((0,), (0,)))
            sums[:reach, value_columns] += dot(probs_low, d_rows, ((0,), (0,)))
    d_prior_ref[...] = sums[:halo].astype(BF)
    d_here_ref[...] = sums[halo:]


def run_attend(queries, prior, here, bias):
    rows = queries.shape[0]
    return pl.pallas_call(
        attend_kernel,
        out_shape=[
            jax.ShapeDtypeStruct((rows, QH * HD), BF),
            jax.ShapeDtypeStruct((rows, QH), F32),
        ],
        compiler_params=pltpu.CompilerParams(vmem_limit_bytes=VMEM_LIMIT),
        cost_estimate=LONG,
        name="attend",
    )(queries, prior, here, bias)


def run_attend_back(queries, prior, here, bias, log_total, d_attended):
    rows = queries.shape[0]
    halo = prior.shape[0]
    return pl.pallas_call(
        attend_back_kernel,
        out_shape=[
            jax.ShapeDtypeStruct((rows, QH * HD), BF),
            jax.ShapeDtypeStruct((halo, 2 * KVH * HD), BF),
            jax.ShapeDtypeStruct((rows, 2 * KVH * HD), F32),
        ],
        scratch_shapes=[pltpu.VMEM((halo + rows, 2 * KVH * HD), F32)],
        compiler_params=pltpu.CompilerParams(vmem_limit_bytes=VMEM_LIMIT),
        cost_estimate=COST,
        name="attend_back",
    )(queries, prior, here, bias, log_total, d_attended)


def swap(value):
    return lax.ppermute(value, "shard", SWAP)


def natural(mine, theirs, position, axis):
    return jnp.where(
        position == 0,
        jnp.concatenate([mine, theirs], axis=axis),
        jnp.concatenate([theirs, mine], axis=axis),
    )


def half_of(value, which, axis):
    size = value.shape[axis] // 2
    return lax.dynamic_slice_in_dim(value, which * size, size, axis)


class Stream:
    def __init__(self, terms, whole, *orders):
        self.terms = terms
        self.count = lax.axis_size("rep")
        self.bits = self.count.bit_length() - 1
        self.stack = None
        self.got = None
        self.gone = 0
        if self.count != 1 << self.bits:
            self.stack = lax.psum(self.part(0, terms[0].shape[0]), "rep")
            self.bits = 0
        places = range(self.bits)
        self.orders = [
            [bit for bit in order if bit < self.bits] + [bit for bit in places if bit not in order]
            for order in orders
        ]
        rep, core = lax.axis_index("rep"), lax.axis_index("shard")
        self.cuts = max(0, self.bits - whole)
        self.sides = [
            jnp.where(core == 0, (rep >> first) & 1, (rep >> second) & 1)
            for first, second in zip(*self.orders)
        ][: self.cuts]
        self.steps = [("scatter", step) for step in places[: self.cuts]]
        self.steps += [("exchange", step) for step in places[self.cuts :]]
        self.steps += [("gather", step) for step in reversed(places[: self.cuts])]

    def pairs(self, step):
        return [
            (rep * 2 + core, (rep ^ (1 << self.orders[core][step])) * 2 + core)
            for rep in range(self.count)
            for core in range(2)
        ]

    def part(self, start, size):
        total = lax.dynamic_slice_in_dim(self.terms[0], start, size, 0).astype(F32)
        for term in self.terms[1:]:
            total = total + lax.dynamic_slice_in_dim(term, start, size, 0).astype(F32)
        return total.astype(BF)

    def latest(self):
        if self.got is not None:
            return self.got
        return self.terms[-1] if self.stack is None else self.stack

    def hold(self, token):
        if self.got is not None:
            self.got = after(self.got, token)
        elif self.stack is None:
            self.terms[-1] = after(self.terms[-1], token)

    def prepare(self):
        kind, step = self.steps[0]
        if kind == "gather":
            if self.stack is None:
                self.stack = self.part(0, self.terms[0].shape[0])
            else:
                self.stack = jnp.concatenate([self.stack, self.got])
            self.operand = self.stack
        elif kind == "exchange":
            self.operand = self.part(0, self.terms[0].shape[0])
        else:
            size = self.terms[0].shape[0] // 2
            self.operand = self.part((1 - self.sides[step]) * size, size)

    def go(self):
        kind, step = self.steps.pop(0)
        self.gone += 1
        got = lax.ppermute(self.operand, ("rep", "shard"), self.pairs(step))
        if kind == "gather":
            self.got = got
        elif kind == "exchange":
            self.terms = [self.operand, got]
        else:
            size = self.terms[0].shape[0] // 2
            self.terms = [
                lax.dynamic_slice_in_dim(term, self.sides[step] * size, size, 0)
                for term in self.terms
            ] + [got]

    def own(self):
        block = jnp.zeros((), jnp.int32)
        for side in self.sides:
            block = 2 * block + side
        return block.astype(jnp.int32)

    def finish(self, outputs, started=None, weights=(), part=None, before=()):
        if self.stack is None:
            self.stack = self.part(0, self.terms[0].shape[0])
        stacks = [self.stack] if self.got is None else [self.stack, self.got]
        blocks = 1 << self.cuts
        far = max(1, blocks // 4)
        quarters = blocks // far
        each = quarters // len(stacks)
        size = stacks[0].shape[0] // each // far
        width = stacks[0].shape[1]
        own = self.own()
        numbers = jnp.arange(quarters, dtype=jnp.int32)
        if part is not None:
            if size % 16:
                return None
            stacks = stacks[part : part + 1]
            numbers = numbers[each * part : each * (part + 1)]
        if size % 16:
            flat = jnp.concatenate(stacks).reshape(blocks, size, width)
            flat = jnp.zeros_like(flat).at[jnp.arange(blocks) ^ own].set(flat).reshape(-1, width)
            made = []
            for shape, _, pieces in outputs:
                cuts = [flat[:, begin:end].astype(F32) for _, begin, end in pieces]
                if pieces[0][0] == TURNED:
                    made.append(cuts[0].T)
                    continue
                value = jnp.stack(cuts) if len(shape.shape) == 3 else jnp.concatenate(cuts, axis=1)
                made.append(value)
            products = [
                jnp.sum(
                    value * weight[:, : value.shape[1]].astype(F32),
                    axis=0 if pieces[0][0] == TURNED else 1,
                )
                for value, weight, (_, _, pieces) in zip(made, weights, outputs)
                if weight is not None
            ]
            spare = outputs[-1][0].shape[-1] - made[-1].shape[-1]
            if spare:
                left = made[-1].ndim == 3
                other = jnp.zeros(made[-1].shape[:-1] + (spare,), F32)
                if started is not None:
                    other = started[..., :spare] if left else started[..., -spare:]
                made[-1] = jnp.concatenate([other, made[-1]] if left else [made[-1], other], axis=-1)
            if products:
                made.append(jnp.broadcast_to(sum(products), (8, products[0].shape[0])))
            return made
        rows = far * size
        in_specs = [
            pl.BlockSpec((rows, width), lambda step, places: (jnp.minimum(step, each - 1), 0))
        ]
        if len(stacks) == 2:
            in_specs.append(
                pl.BlockSpec((rows, width), lambda step, places: (jnp.maximum(step - each, 0), 0))
            )
        out_specs = []
        scratch = []
        for shape, block, pieces in outputs:
            if pieces[0][0] == TURNED:
                out_specs.append(
                    pl.BlockSpec((shape.shape[0], rows), lambda step, places: (0, places[step]))
                )
                scratch = [pltpu.VMEM((rows, block), F32)]
            elif len(shape.shape) == 3:
                last = shape.shape[2] // block - 1
                out_specs.append(
                    pl.BlockSpec(
                        (shape.shape[0], rows, block),
                        lambda step, places, last=last: (0, places[step], last),
                    )
                )
            else:
                out_specs.append(pl.BlockSpec((rows, block), lambda step, places: (places[step], 0)))
        inputs = list(stacks)
        shapes = [shape for shape, _, _ in outputs]
        for weight, (_, block, pieces) in zip(weights, outputs):
            if weight is None:
                continue
            inputs.append(weight)
            if pieces[0][0] == TURNED:
                in_specs.append(
                    pl.BlockSpec((weight.shape[0], rows), lambda step, places: (0, places[step]))
                )
            else:
                in_specs.append(pl.BlockSpec((rows, block), lambda step, places: (places[step], 0)))
        if weights:
            out_specs.append(pl.BlockSpec((8, rows), lambda step, places: (0, places[step])))
            shapes.append(jax.ShapeDtypeStruct((8, rows * quarters), F32))
        aliases = {}
        if part != 1 and started is not None:
            before = [started]
            aliases = {1 + len(inputs): len(outputs) - 1}
        elif part == 1:
            aliases = {1 + len(inputs) + number: number for number in range(len(shapes))}
        inputs += before
        in_specs += [pl.BlockSpec(memory_space=pl.ANY)] * len(before)
        places = jnp.concatenate([numbers ^ (own // far), (own % far).reshape(1)])
        return pl.pallas_call(
            functools.partial(
                finish_kernel,
                len(stacks),
                far,
                [cut for _, _, cut in outputs],
                [weight is not None for weight in weights],
            ),
            grid_spec=pltpu.PrefetchScalarGridSpec(
                num_scalar_prefetch=1,
                grid=numbers.shape,
                in_specs=in_specs,
                out_specs=out_specs,
                scratch_shapes=scratch,
            ),
            out_shape=shapes,
            input_output_aliases=aliases,
            compiler_params=params_of(),
            cost_estimate=COST,
            name="unpack",
        )(places, *inputs)


def finish_kernel(count, far, layout, weighed, places, *refs):
    turned = any(pieces[0][0] == TURNED for pieces in layout)
    if turned:
        held, refs = refs[-1], refs[:-1]
    if any(weighed):
        products, refs = refs[-1], refs[:-1]
    outputs = refs[-len(layout) :]
    weights = list(refs[count : count + sum(weighed)])
    steps = pl.num_programs(0)
    within = places[steps]
    size = refs[0].shape[0] // far

    def write(ref):
        width = ref.shape[1]
        for number in range(far):
            row = pl.multiple_of((within ^ number) * size, size)
            piece_rows = slice(number * size, (number + 1) * size)
            for out, pieces in zip(outputs, layout):
                for target, begin, end in pieces:
                    if target == TURNED:
                        continue
                    value = ref[piece_rows, begin:end].astype(F32)
                    if len(out.shape) == 3:
                        out[target, pl.ds(row, size), :] = value
                    else:
                        out[pl.ds(row, size), target : target + end - begin] = value
            if turned:
                held[pl.ds(row, size), :] = ref[piece_rows, width - held.shape[1] :].astype(F32)
        if turned:
            flipped = held[...].T
            for out, pieces in zip(outputs, layout):
                target, begin, end = pieces[0]
                if target == TURNED:
                    first = width - held.shape[1]
                    out[...] = flipped[begin - first : end - first, :]

    if count == 1:
        write(refs[0])
    else:

        @pl.when(pl.program_id(0) < steps // 2)
        def _():
            write(refs[0])

        @pl.when(pl.program_id(0) >= steps // 2)
        def _():
            write(refs[1])

    if any(weighed):
        ones = jnp.ones((8, LANES), BF)
        total = jnp.zeros(products.shape, F32)
        for out, pieces, used in zip(outputs, layout, weighed):
            if not used:
                continue
            product = out[...] * weights.pop(0)[...].astype(F32)
            if pieces[0][0] == TURNED:
                total = total + jnp.sum(product, axis=0, keepdims=True)
                continue
            narrow = product[:, :LANES]
            for column in range(LANES, product.shape[1], LANES):
                narrow = narrow + product[:, column : column + LANES]
            for part in split3(narrow):
                total = total + dot(ones, part, ((1,), (1,)))
        products[...] = total


def after(value, *others):
    return lax.optimization_barrier((value, *others))[0]


def fence(value, *others):
    anywhere = pl.BlockSpec(memory_space=pl.ANY)
    return pl.pallas_call(
        lambda *refs: None,
        in_specs=[anywhere] * (1 + len(others)),
        out_specs=anywhere,
        out_shape=jax.ShapeDtypeStruct(value.shape, value.dtype),
        input_output_aliases={0: 0},
        cost_estimate=COST,
        name="fence",
    )(value, *others)


def columns_of(ref, which, size):
    return ref[:, pl.ds(pl.multiple_of(which * size, size), size)]


def inverse_rms(values):
    return lax.rsqrt(jnp.mean(values * values, axis=-1, keepdims=True) + EPSILON)


def norm_back(values, inverse, gain, grad):
    scaled = grad * gain
    shared = jnp.mean(scaled * values, axis=-1, keepdims=True) * (inverse * inverse)
    return (
        inverse * (scaled - values * shared),
        jnp.sum(grad * (values * inverse), axis=0, keepdims=True),
    )


def project_small_kernel(
    position,
    tokens,
    gains,
    dt_bias,
    decay_log,
    query_mine,
    query_theirs,
    kv_mine,
    kv_theirs,
    aux_mine,
    aux_theirs,
    normed,
    queries,
    key_vals,
    aux,
    tails,
    carries,
):
    here = position[0]
    half = tokens.shape[1] // 2
    hidden = tokens[...].astype(F32)
    normed[...] = (hidden * inverse_rms(hidden) * gains[0:1]).astype(BF)

    def product(mine, theirs, over=((1,), (0,))):
        return dot(columns_of(normed, here, half), mine[...], over) + dot(
            columns_of(normed, 1 - here, half), theirs[...], over
        )

    key_vals[...] = product(kv_mine, kv_theirs).astype(BF)
    queries[...] = product(query_mine, query_theirs).astype(BF) * jnp.asarray(HD**-0.5, BF)
    found = product(aux_mine, aux_theirs, ((1,), (1,)))
    aux[:, : found.shape[1]] = found
    aux[:, found.shape[1] :] = jnp.zeros_like(aux[:, found.shape[1] :])
    rate = jnp.exp(decay_log[...])
    for block in range(tokens.shape[0] // BLOCK):
        rows = slice(block * BLOCK, (block + 1) * BLOCK)
        _, step_size, _, cumulated = decays(aux[rows, :], dt_bias[...], rate)
        last = cumulated[BLOCK - 1 :, :]
        tails[rows, :] = step_size * jnp.exp(last - cumulated)
        carries[block : block + 1, :] = jnp.exp(last)


def run_project_small(position, tokens, gains, dt_bias, decay_log, query, kv, aux):
    rows, width = tokens.shape
    fixed = lambda shape: pl.BlockSpec(shape, lambda step, place: (0, 0))
    inputs = (tokens, gains, dt_bias, decay_log, *query, *kv, *aux)
    shapes = [
        jax.ShapeDtypeStruct((rows, width), BF),
        jax.ShapeDtypeStruct((rows, KV_AT), BF),
        jax.ShapeDtypeStruct((rows, AUX_AT - KV_AT), BF),
        jax.ShapeDtypeStruct((rows, 3 * LANES), F32),
        jax.ShapeDtypeStruct((rows, LANES), F32),
        jax.ShapeDtypeStruct((8, LANES), F32),
    ]
    return pl.pallas_call(
        project_small_kernel,
        grid_spec=pltpu.PrefetchScalarGridSpec(
            num_scalar_prefetch=1,
            grid=(1,),
            in_specs=[fixed(item.shape) for item in inputs],
            out_specs=[fixed(shape.shape) for shape in shapes],
        ),
        out_shape=shapes,
        compiler_params=params_of(WHOLE_LIMIT),
        cost_estimate=LONG,
        name="project_small",
    )(position, *inputs)


def project_kernel(
    position,
    resets,
    normed,
    aux,
    tails,
    carries,
    ssm_mine,
    ssm_theirs,
    mixed,
    state_out,
):
    here = position[0]
    half = normed.shape[1] // 2
    step = pl.program_id(0)
    found = dot(columns_of(normed, here, half), ssm_mine[...]) + dot(
        columns_of(normed, 1 - here, half), ssm_theirs[...]
    )
    mixed[...] = found.astype(BF)

    for number in range(INNER // CHUNK):

        @pl.when(step == number)
        def _():
            heads = (number * CHUNK // SP, (number + 1) * CHUNK // SP)
            scaled = (found * spread(tails[...], *heads)).astype(BF)
            carried = spread(carries[...], *heads)
            state = jnp.zeros((STATE, CHUNK), F32)
            for block in range(normed.shape[0] // BLOCK):
                rows = slice(block * BLOCK, (block + 1) * BLOCK)
                b_in = aux[rows, :STATE].astype(BF)
                state = jnp.where(resets[block] != 0, 0.0, carried[block : block + 1, :] * state)
                state = state + dot(b_in, scaled[rows, :], ((0,), (0,)))
            state_out[...] = state


CHUNK = 512


def run_project(position, resets, normed, aux, tails, carries, ssm):
    rows, width = normed.shape
    half = width // 2
    inner = ssm[0].shape[1]
    fixed = lambda shape: pl.BlockSpec(shape, lambda step, place, resets: (0, 0))
    sliding = pl.BlockSpec((half, CHUNK), lambda step, place, resets: (0, step))
    return pl.pallas_call(
        project_kernel,
        grid_spec=pltpu.PrefetchScalarGridSpec(
            num_scalar_prefetch=2,
            grid=(inner // CHUNK,),
            in_specs=[
                *[fixed(item.shape) for item in (normed, aux, tails, carries)],
                sliding,
                sliding,
            ],
            out_specs=[
                pl.BlockSpec((rows, CHUNK), lambda step, place, resets: (0, step)),
                pl.BlockSpec(
                    (STATE, CHUNK),
                    lambda step, place, resets: (0, jnp.minimum(step, INNER // CHUNK - 1)),
                ),
            ],
        ),
        out_shape=[
            jax.ShapeDtypeStruct((rows, inner), BF),
            jax.ShapeDtypeStruct((STATE, INNER), F32),
        ],
        compiler_params=params_of(WHOLE_LIMIT),
        cost_estimate=LONG,
        name="project",
    )(position, resets, normed, aux, tails, carries, *ssm)


def middle_kernel(
    position,
    tokens,
    attended,
    gated,
    cotangent,
    gains,
    attn_mine,
    attn_theirs,
    ssm_mine,
    ssm_theirs,
    gate_mine,
    gate_theirs,
    up_mine,
    up_theirs,
    down_mine,
    down_theirs,
    output,
    d_middle,
    d_attn_branch,
    d_ssm_branch,
    d_attended,
    d_gated,
    gain_grads,
    grad_down_theirs,
    grad_down_mine,
    grad_wide_theirs,
    grad_wide_mine,
    attn_branch,
    ssm_branch,
    middle,
    normed,
    flipped,
    out_sum,
    d_normed,
):
    here = position[0]
    step = pl.program_id(0)
    count = pl.num_programs(0)
    width = tokens.shape[1]
    half = width // 2
    attn_half = attended.shape[1] // 2
    ssm_half = gated.shape[1] // 2
    flat = ((1,), (1,))

    def place(which, size):
        return pl.ds(pl.multiple_of(which * size, size), size)

    @pl.when(step == 0)
    def _():
        attn = dot(columns_of(attended, here, attn_half), attn_mine[...]) + dot(
            columns_of(attended, 1 - here, attn_half), attn_theirs[...]
        )
        attn_branch[...] = attn
        ssm = dot(columns_of(gated, here, ssm_half), ssm_mine[...]) + dot(
            columns_of(gated, 1 - here, ssm_half), ssm_theirs[...]
        )
        ssm_branch[...] = ssm
        joined = tokens[...].astype(F32) + 0.5 * (
            attn * inverse_rms(attn) * gains[1:2] + ssm * inverse_rms(ssm) * gains[2:3]
        )
        middle[...] = joined
        out_sum[...] = joined
        scaled = joined * inverse_rms(joined) * gains[3:4]
        normed[...] = scaled.astype(BF)
        flipped[...] = scaled.T.astype(BF)
        d_normed[...] = jnp.zeros_like(d_normed)

    first = step < count // 2
    mine = columns_of(normed, here, half)
    theirs = columns_of(normed, 1 - here, half)
    gate_val = dot(mine, gate_mine[...]) + dot(theirs, gate_theirs[...])
    up_val = dot(mine, up_mine[...]) + dot(theirs, up_theirs[...])
    gate_silu, chance = silu_of(gate_val)
    activated = (gate_silu * up_val).astype(BF)
    down = jnp.where(first, down_theirs[...], down_mine[...])
    d_activated = dot(cotangent[...], down, flat)
    out_sum[...] += dot(activated, down)
    d_up = (d_activated * gate_silu).astype(BF)
    d_gate = (d_activated * up_val * (chance + gate_silu * (1.0 - chance))).astype(BF)
    d_normed[:, place(here, half)] += dot(d_gate, gate_mine[...], flat) + dot(d_up, up_mine[...], flat)
    d_normed[:, place(1 - here, half)] += dot(d_gate, gate_theirs[...], flat) + dot(
        d_up, up_theirs[...], flat
    )
    grad_down = dot(activated, cotangent[...], ((0,), (0,))).astype(BF)

    @pl.when(first)
    def _():
        grad_down_theirs[...] = grad_down

    @pl.when(jnp.logical_not(first))
    def _():
        grad_down_mine[...] = grad_down

    for which, ref in ((here, grad_wide_mine), (1 - here, grad_wide_theirs)):
        turned = flipped[place(which, half), :]
        ref[:, :CHUNK] = dot(turned, d_gate).astype(BF)
        ref[:, CHUNK:] = dot(turned, d_up).astype(BF)

    @pl.when(step == count - 1)
    def _():
        output[...] = out_sum[...].astype(BF)
        joined = middle[...]
        d_joined, d_gain_ff = norm_back(joined, inverse_rms(joined), gains[3:4], d_normed[...])
        d_joined = cotangent[...].astype(F32) + d_joined
        d_middle[...] = d_joined
        attn = attn_branch[...]
        d_attn, d_gain_attn = norm_back(attn, inverse_rms(attn), gains[1:2], 0.5 * d_joined)
        d_attn_low = d_attn.astype(BF)
        d_attn_branch[...] = d_attn_low
        ssm = ssm_branch[...]
        d_ssm, d_gain_ssm = norm_back(ssm, inverse_rms(ssm), gains[2:3], 0.5 * d_joined)
        d_ssm_low = d_ssm.astype(BF)
        d_ssm_branch[...] = d_ssm_low
        gain_grads[...] = jnp.concatenate(
            [d_gain_attn, d_gain_ssm, d_gain_ff, jnp.zeros((5, width), F32)]
        )
        for which, attn_weight, ssm_weight in (
            (here, attn_mine, ssm_mine),
            (1 - here, attn_theirs, ssm_theirs),
        ):
            d_attended[:, place(which, attn_half)] = dot(d_attn_low, attn_weight[...], flat).astype(BF)
            d_gated[:, place(which, ssm_half)] = dot(d_ssm_low, ssm_weight[...], flat).astype(BF)


def run_middle(position, tokens, attended, gated, cotangent, gains, attn, ssm, gate, up, down):
    rows, width = tokens.shape
    half = width // 2
    hidden = gate[0].shape[1]
    count = hidden // CHUNK
    fixed = lambda shape: pl.BlockSpec(shape, lambda step, place: (0,) * len(shape))

    def chunk(step, place):
        first = step < count // 2
        return jnp.where(first, 1 - place[0], place[0]) * (count // 2) + step % (count // 2)

    sliding = pl.BlockSpec((half, CHUNK), lambda step, place: (0, chunk(step, place)))
    early = lambda step, place: (jnp.minimum(step, count // 2 - 1), 0)
    late = lambda step, place: (jnp.maximum(step - count // 2, 0), 0)
    wide = pl.BlockSpec((half, 2 * CHUNK), lambda step, place: (0, chunk(step, place)))
    low = lambda shape: jax.ShapeDtypeStruct(shape, BF)
    full = lambda shape: jax.ShapeDtypeStruct(shape, F32)
    return pl.pallas_call(
        middle_kernel,
        grid_spec=pltpu.PrefetchScalarGridSpec(
            num_scalar_prefetch=1,
            grid=(count,),
            in_specs=[
                *[fixed(item.shape) for item in (tokens, attended, gated, cotangent, gains)],
                *[fixed(item.shape) for item in (*attn, *ssm)],
                *[sliding] * 4,
                pl.BlockSpec((CHUNK, width), late),
                pl.BlockSpec((CHUNK, width), early),
            ],
            out_specs=[
                *[fixed((rows, width))] * 4,
                fixed(attended.shape),
                fixed(gated.shape),
                fixed((8, width)),
                pl.BlockSpec((CHUNK, width), early),
                pl.BlockSpec((CHUNK, width), late),
                wide,
                wide,
            ],
            scratch_shapes=[
                *[pltpu.VMEM((rows, width), F32)] * 3,
                pltpu.VMEM((rows, width), BF),
                pltpu.VMEM((width, rows), BF),
                *[pltpu.VMEM((rows, width), F32)] * 2,
            ],
        ),
        out_shape=[
            low((rows, width)),
            full((rows, width)),
            low((rows, width)),
            low((rows, width)),
            low(attended.shape),
            low(gated.shape),
            full((8, width)),
            low((hidden // 2, width)),
            low((hidden // 2, width)),
            low((half, 2 * hidden)),
            low((half, 2 * hidden)),
        ],
        compiler_params=params_of(LARGE_LIMIT),
        cost_estimate=LONG,
        name="middle",
    )(position, tokens, attended, gated, cotangent, gains, *attn, *ssm, *gate, *up, *down)


def outs_grads_kernel(
    position, attended, gated, normed, d_attn, d_ssm, d_gate, theirs, mine
):
    here = position[0]
    step = pl.program_id(0)
    which = jnp.where(step == 0, 1 - here, here)
    rows = theirs.shape[0]
    down = ((0,), (0,))

    def write(ref):
        at = 0
        for left, right in ((attended, d_attn), (gated, d_ssm), (normed, d_gate)):
            half = left.shape[1] // 2
            for begin in range(0, half, rows):
                turned = left[:, pl.ds(pl.multiple_of(which * half + begin, rows), rows)]
                ref[:, at : at + right.shape[1]] = dot(turned, right[...], down).astype(BF)
                at += right.shape[1]

    @pl.when(step == 0)
    def _():
        write(theirs)

    @pl.when(step == 1)
    def _():
        write(mine)


def run_outs_grads(position, attended, gated, normed, d_attn, d_ssm, d_gate):
    inputs = (attended, gated, normed, d_attn, d_ssm, d_gate)
    rows = attended.shape[1] // 2
    width = sum(
        left.shape[1] // 2 // rows * right.shape[1] for left, right in zip(inputs[:3], inputs[3:])
    )
    fixed = lambda shape: pl.BlockSpec(shape, lambda step, place: (0, 0))
    return pl.pallas_call(
        outs_grads_kernel,
        grid_spec=pltpu.PrefetchScalarGridSpec(
            num_scalar_prefetch=1,
            grid=(2,),
            in_specs=[fixed(item.shape) for item in inputs],
            out_specs=[fixed((rows, width))] * 2,
        ),
        out_shape=[jax.ShapeDtypeStruct((rows, width), BF)] * 2,
        compiler_params=params_of(),
        cost_estimate=COST,
        name="outs_grads",
    )(position, *inputs)


def early_back_kernel(
    position,
    d_query,
    d_kv,
    d_gate,
    query_mine,
    query_theirs,
    kv_mine,
    kv_theirs,
    ssm_mine,
    ssm_theirs,
    d_normed,
):
    here = position[0]
    half = d_normed.shape[1] // 2
    flat = ((1,), (1,))
    for which, query, kv, ssm in (
        (here, query_mine, kv_mine, ssm_mine),
        (1 - here, query_theirs, kv_theirs, ssm_theirs),
    ):
        d_normed[:, pl.ds(pl.multiple_of(which * half, half), half)] = (
            dot(d_query[...], query[...], flat)
            + dot(d_kv[...], kv[...], flat)
            + dot(d_gate[...], ssm[...], flat)
        )


def run_early_back(position, d_query, d_kv, d_gate, query, kv, ssm):
    rows = d_query.shape[0]
    half = query[0].shape[0]
    fixed = lambda shape: pl.BlockSpec(shape, lambda step, place: (0, 0))
    return pl.pallas_call(
        early_back_kernel,
        grid_spec=pltpu.PrefetchScalarGridSpec(
            num_scalar_prefetch=1,
            grid=(1,),
            in_specs=[
                *[fixed(item.shape) for item in (d_query, d_kv, d_gate, *query, *kv)],
                *[pl.BlockSpec((half, INNER), lambda step, place: (0, 1))] * 2,
            ],
            out_specs=fixed((rows, 2 * half)),
        ),
        out_shape=jax.ShapeDtypeStruct((rows, 2 * half), F32),
        compiler_params=params_of(),
        cost_estimate=COST,
        name="early_back",
    )(position, d_query, d_kv, d_gate, *query, *kv, *ssm)


def rest_grads_kernel(
    position, normed, d_query, d_kv, d_mixed, d_aux, gain_grads, d_heads, theirs, mine
):
    here = position[0]
    step = pl.program_id(0)
    half = normed.shape[1] // 2
    which = jnp.where(step == 0, 1 - here, here)
    turned = normed[:, pl.ds(pl.multiple_of(which * half, half), half)]

    def write(ref):
        at = 0
        for right in (d_query, d_kv, d_mixed):
            ref[:, at : at + right.shape[1]] = dot(turned, right[...], ((0,), (0,))).astype(BF)
            at += right.shape[1]
        gains = gain_grads[0:3, pl.ds(pl.multiple_of(which * half, half), half)]
        heads = jnp.concatenate([d_heads[0:1, :], d_heads[1:2, :]], axis=1)
        heads = jnp.concatenate([heads, jnp.zeros((1, half - heads.shape[1]), F32)], axis=1)
        before = 2 * STATE + SH
        columns = jnp.concatenate(
            [
                jnp.zeros((before, half), F32),
                gains,
                heads,
                jnp.zeros((d_aux.shape[1] - before - 4, half), F32),
            ]
        ).T
        ref[:, at:] = (dot(turned, d_aux[...], ((0,), (0,))) + columns).astype(BF)

    @pl.when(step == 0)
    def _():
        write(theirs)

    @pl.when(step == 1)
    def _():
        write(mine)


def run_rest_grads(position, *inputs):
    half = inputs[0].shape[1] // 2
    total = sum(item.shape[1] for item in inputs[1:5])
    fixed = lambda shape: pl.BlockSpec(shape, lambda step, place: (0, 0))
    return pl.pallas_call(
        rest_grads_kernel,
        grid_spec=pltpu.PrefetchScalarGridSpec(
            num_scalar_prefetch=1,
            grid=(2,),
            in_specs=[fixed(item.shape) for item in inputs],
            out_specs=[fixed((half, total))] * 2,
        ),
        out_shape=[jax.ShapeDtypeStruct((half, total), BF)] * 2,
        compiler_params=params_of(),
        cost_estimate=COST,
        name="rest_grads",
    )(position, *inputs)


def late_back_kernel(
    position,
    tokens,
    gains,
    d_middle,
    d_normed,
    d_mixed,
    d_aux,
    aux_mine,
    aux_theirs,
    ssm_mine,
    ssm_theirs,
    grad_tokens,
    total,
):
    here = position[0]
    half = tokens.shape[1] // 2
    for which, aux, ssm in ((here, aux_mine, ssm_mine), (1 - here, aux_theirs, ssm_theirs)):
        columns = pl.ds(pl.multiple_of(which * half, half), half)
        total[:, columns] = (
            d_normed[:, columns]
            + dot(d_mixed[...], ssm[...], ((1,), (1,)))
            + dot(d_aux[:, : aux.shape[0]], aux[...])
        )
    hidden = tokens[...].astype(F32)
    d_hidden, _ = norm_back(hidden, inverse_rms(hidden), gains[0:1], total[...])
    grad_tokens[...] = d_middle[...] + d_hidden


def run_late_back(position, tokens, gains, d_middle, d_normed, d_mixed, d_aux, aux, ssm):
    rows, width = tokens.shape
    half = width // 2
    fixed = lambda shape: pl.BlockSpec(shape, lambda step, place: (0, 0))
    inputs = (tokens, gains, d_middle, d_normed, d_mixed, d_aux, *aux)
    return pl.pallas_call(
        late_back_kernel,
        grid_spec=pltpu.PrefetchScalarGridSpec(
            num_scalar_prefetch=1,
            grid=(1,),
            in_specs=[
                *[fixed(item.shape) for item in inputs],
                *[pl.BlockSpec((half, INNER), lambda step, place: (0, 0))] * 2,
            ],
            out_specs=fixed((rows, width)),
            scratch_shapes=[pltpu.VMEM((rows, width), F32)],
        ),
        out_shape=jax.ShapeDtypeStruct((rows, width), F32),
        compiler_params=params_of(),
        cost_estimate=COST,
        name="late_back",
    )(position, *inputs, *ssm)


def local(
    tokens,
    cotangent,
    doc_blocks,
    gain_in,
    w_query,
    w_kv,
    w_attn_out,
    gain_attn,
    w_ssm_in,
    w_ssm_aux,
    dt_bias,
    decay_log,
    w_ssm_out,
    gain_ssm,
    gain_ff,
    w_gate,
    w_up,
    w_down,
):
    rows, width = tokens.shape
    half = width // 2
    position = lax.axis_index("shard")
    here = position.astype(jnp.int32).reshape(1)
    blocks_here = rows // BLOCK
    docs = doc_blocks[0]
    here_docs = lax.dynamic_slice_in_dim(docs, position * blocks_here, blocks_here, 0)
    prior_docs = jnp.where(position > 0, docs[:blocks_here], -1)
    earlier = jnp.concatenate([prior_docs[-1:], here_docs[:-1]])
    resets = (here_docs != earlier).astype(jnp.int32)
    key_docs = jnp.repeat(jnp.concatenate([prior_docs, here_docs]), BLOCK)
    bias = jnp.where(here_docs[:, None] == key_docs[None, :], 0.0, NEGATIVE)
    lane_pad = LANES - SH
    dt_row = jnp.pad(dt_bias, (0, lane_pad))[None]
    decay_row = jnp.pad(decay_log, (0, lane_pad))[None]

    gain_first = natural(gain_in, swap(gain_in), position, 0).astype(F32)[None]
    query = (w_query, swap(w_query))
    kv = (w_kv, swap(w_kv))
    aux_in = (w_ssm_aux.T, swap(w_ssm_aux.T))
    ssm_in = (w_ssm_in, swap(after(w_ssm_in, kv[1])))
    attn_out, ssm_back, gate, up, down = (
        (weight, swap(weight)) for weight in (w_attn_out, w_ssm_out, w_gate, w_up, w_down)
    )
    normed, scaled_queries, key_vals, aux, tails, carries = run_project_small(
        here, tokens, gain_first, dt_row, decay_row, query, kv, aux_in
    )
    key_prior = lax.ppermute(key_vals, "shard", [(0, 1)])
    later_gains = [
        natural(gain, swap(gain), position, 0).astype(F32)[None]
        for gain in (gain_attn, gain_ssm, gain_ff)
    ]
    gains_all = jnp.concatenate([gain_first, *later_gains, jnp.zeros((4, width), F32)])
    mixed, state_end = run_project(here, resets, normed, aux, tails, carries, ssm_in)
    state_prior = lax.ppermute(state_end, "shard", [(0, 1)])
    attended, log_total = run_attend(scaled_queries, key_prior, key_vals, bias)
    ssm_out, gated, states = run_forward(resets, mixed, aux, dt_row, decay_row, state_prior)

    (
        output,
        d_middle,
        d_attn_low,
        d_ssm_low,
        d_attended,
        d_gated,
        gain_grads,
        down_theirs,
        down_mine,
        wide_theirs,
        wide_mine,
    ) = run_middle(
        here, tokens, attended, gated, cotangent, gains_all, attn_out, ssm_back, gate, up, down
    )
    sums = {
        "down": Stream([down_mine, swap(down_theirs)], WHOLE["down"], *LINKS["down"]),
        "wide": Stream([wide_mine, swap(wide_theirs)], WHOLE["wide"], *LINKS["wide"]),
    }
    token = wide_theirs
    made = {}
    outs_rows = w_attn_out.shape[0]
    full = lambda *shape: jax.ShapeDtypeStruct(shape, F32)
    ssm_pieces = w_ssm_out.shape[0] // outs_rows
    gate_at = width * (1 + ssm_pieces)
    aux_at = AUX_AT + INNER
    spare = aux_at + 2 * STATE + SH
    wide_pieces = [
        [
            (column, 2 * column + offset, 2 * column + offset + CHUNK)
            for column in range(0, w_gate.shape[1], CHUNK)
        ]
        for offset in (0, CHUNK)
    ]
    layouts = {
        "down": [(full(*w_down.shape), width, [(0, 0, width)])],
        "wide": [(full(half, w_gate.shape[1]), w_gate.shape[1], pieces) for pieces in wide_pieces],
        "outs": [
            (full(outs_rows, width), width, [(0, 0, width)]),
            (
                full(ssm_pieces, outs_rows, width),
                width,
                [(piece, width * (1 + piece), width * (2 + piece)) for piece in range(ssm_pieces)],
            ),
            (
                full(half // outs_rows, outs_rows, 2 * INNER),
                INNER,
                [
                    (piece, gate_at + INNER * piece, gate_at + INNER * (piece + 1))
                    for piece in range(half // outs_rows)
                ],
            ),
        ],
        "rest": [
            (full(half, KV_AT), KV_AT, [(0, 0, KV_AT)]),
            (full(half, AUX_AT - KV_AT), AUX_AT - KV_AT, [(0, KV_AT, AUX_AT)]),
            (full(spare - aux_at, half), 3 * LANES, [(TURNED, aux_at, spare)]),
            (full(8, half), 3 * LANES, [(TURNED, spare, spare + 8)]),
            (full(half, 2 * INNER), INNER, [(0, AUX_AT, aux_at)]),
        ],
    }
    def closed(value, number):
        if number + 1 == len(PLAN) or PLAN[number + 1] not in layouts:
            return value
        names = []
        for name in PLAN[number + 1 :]:
            if name not in layouts:
                break
            names.append(name)
        waits = [
            stream.latest()
            for name, stream in sums.items()
            if stream.steps
            and (name in names or stream.gone > 1 or (stream.gone == 1 and name == "down"))
        ]
        return fence(value, *waits)

    d_kv = ssm_in_grad = None
    halves = {}
    rest_weights = (w_query, w_kv, w_ssm_aux.T, None, w_ssm_in)

    def key_grads(made_before):
        if made_before is not None:
            return made_before
        return (d_here + after(d_prior_got, token).astype(F32)).astype(BF)

    def go_on(name):
        nonlocal token, ssm_in_grad
        stream = sums[name]
        stream.hold(token)
        weights = rest_weights if name == "rest" else ()
        place = {"outs": 2, "rest": 4}.get(name)
        shape = layouts[name][place][0].shape if place is not None else None
        if stream.steps:
            stream.prepare()
            token = stream.operand
            stream.go()
            if name == "rest" and not stream.steps and stream.got is not None:
                held = None if ssm_in_grad is None else ssm_in_grad.reshape(shape)
                halves[name] = stream.finish(layouts[name], held, weights, 0)
                if halves[name] is not None:
                    halves[name] = list(halves[name])
                    ssm_in_grad = halves[name][place]
        elif name not in made:
            held = None if place is None or ssm_in_grad is None else ssm_in_grad.reshape(shape)
            if halves.get(name) is not None:
                halves[name][place] = held
                made[name] = stream.finish(layouts[name], None, weights, 1, halves[name])
            else:
                made[name] = stream.finish(layouts[name], held, weights)
            token = made[name][0]
            if place is not None:
                ssm_in_grad = made[name][place].reshape(half, 2 * INNER)

    for number, name in enumerate(PLAN):
        if name in layouts:
            go_on(name)
        elif name == "state":
            d_state_start, d_mixed_gate = run_state_back(
                resets, after(d_gated, token), mixed, aux, ssm_out, dt_row, decay_row
            )
            token = closed(d_state_start, number)
            d_state_end = lax.ppermute(token, "shard", [(1, 0)])
        elif name == "grads":
            outs_theirs, outs_mine = run_outs_grads(
                here, after(attended, token), gated, normed, d_attn_low, d_ssm_low, d_mixed_gate
            )
            token = closed(outs_theirs, number)
            sums["outs"] = Stream([outs_mine, swap(token)], WHOLE["outs"], *LINKS["outs"])
        elif name == "attend":
            d_query, d_prior, d_here = run_attend_back(
                scaled_queries, key_prior, key_vals, bias, log_total, after(d_attended, token)
            )
            token = closed(d_prior, number)
            d_prior_got = lax.ppermute(token, "shard", [(1, 0)])
        elif name == "scan":
            d_mixed, d_aux, d_heads = run_backward(
                resets,
                after(d_gated, token),
                mixed,
                aux,
                ssm_out,
                states,
                dt_row,
                decay_row,
                d_state_end,
            )
            token = d_heads = closed(d_heads, number)
        elif name == "sums":
            d_kv = key_grads(d_kv)
            rest_theirs, rest_mine = run_rest_grads(
                here, normed, d_query, d_kv, d_mixed, d_aux, gain_grads, d_heads
            )
            token = closed(rest_theirs, number)
            sums["rest"] = Stream([rest_mine, swap(token)], WHOLE["rest"], *LINKS["rest"])
        elif name == "early":
            d_kv = key_grads(d_kv)
            d_normed = run_early_back(
                here, after(d_query, token), d_kv, d_mixed_gate, query, kv, ssm_in
            )
            token = d_normed
        elif name == "late":
            grad_tokens = run_late_back(
                here,
                tokens,
                gain_first,
                d_middle,
                d_normed,
                d_mixed,
                after(d_aux, token),
                aux_in,
                ssm_in,
            )
            token = grad_tokens

    for name in layouts:
        while name not in made:
            go_on(name)
    (grad_down,) = made["down"]
    grad_gate, grad_up = made["wide"]
    grad_attn_out, grad_ssm_out, _ = made["outs"]
    grad_query, grad_kv, grad_aux, extras, _, products = made["rest"]
    grad_ssm_in = ssm_in_grad
    gate_products = jnp.sum(
        w_ssm_in[:, INNER:].astype(F32) * grad_ssm_in[:, INNER:], axis=1
    )
    grad_gain_in = (products[0] + gate_products) / gain_in.astype(F32)
    return (
        output,
        grad_tokens,
        grad_gain_in,
        grad_query,
        grad_kv,
        grad_attn_out,
        extras[0],
        grad_ssm_in,
        grad_aux.T,
        extras[3, :SH],
        extras[3, LANES : LANES + SH],
        grad_ssm_out.reshape(w_ssm_out.shape),
        extras[1],
        extras[2],
        grad_gate,
        grad_up,
        grad_down,
    )


def solution(mesh):
    halves = P("shard", None)
    half = P("shard")
    tokens = P(("rep", "shard"), None)
    return jax.shard_map(
        local,
        mesh=mesh,
        in_specs=(
            tokens,
            tokens,
            P("rep", None),
            half,
            halves,
            halves,
            halves,
            half,
            halves,
            halves,
            P(),
            P(),
            halves,
            half,
            half,
            halves,
            halves,
            halves,
        ),
        out_specs=(
            tokens,
            tokens,
            half,
            halves,
            halves,
            halves,
            half,
            halves,
            halves,
            P(),
            P(),
            halves,
            half,
            half,
            halves,
            halves,
            halves,
        ),
        check_vma=False,
    )
```
